256 devices in a mesh: slab: 8 (over x_hi, y), cell: 32 (over z, x_lo, core).
Axes of the slice: x: 4 (x_hi: 2, x_lo: 2; x = x_hi * 2 + x_lo), y: 4, z: 8, core: 2. Of those that a mesh axis runs over, the one named last changes fastest.
Arguments:
- positions: float32 [3, 2097152], P(None, ('slab', 'cell')), may hold values from 0 to 32, as said below
- burgers: float32 [3, 2097152], P(None, ('slab', 'cell')), may hold values from -0.018 to 0.018
- mobility: float32 [2097152], P(('slab', 'cell')), may hold values from 0.5 to 2
- near_list: int32 [16384, 6], P(('slab', 'cell')), may hold values from 0 to 255
- near_count: int32 [16384], P(('slab', 'cell')), may hold values from 1 to 6, as said below
- send_list: int32 [4, 12288], P(None, ('slab', 'cell')), may hold values from 0 to 63
Outputs:
- displacement: float32 [3, 2097152], P(None, ('slab', 'cell'))
- velocity: float32 [3, 2097152], P(None, ('slab', 'cell'))
The draws below stay inside these ranges and needn't reach their ends.
Inputs may be any that keep to these rules, and one draw needn't show every extreme that they name: `positions`: cell (s, c) owns the segments of its block of 8192; every coordinate lies in that cell's box. `near_count`: some cells carry pile-ups with up to 6 live slots a block; the others have 1 or 2.
All inputs are finite; a program needn't handle non-finite values.
Results may differ from the reference program's by a relative error of at most 0.00035.
Values sent between devices are 32-bit elements; how exact they have to be, the bound alone decides.
No kernel may reach another device: no remote copies, remote signals or barrier semaphores. Data moves between devices by JAX's collectives and lax.ppermute only.
A program may use at most 128 MiB of HBM per device.

```python
import math
import jax
import jax.numpy as jnp
from jax import lax

BLK_DEV = 64
NEAR = 6
SUBSTEPS = 4
SEG_DEV = 8192
GHOST = 48
EXT = 256
SEGS = 2097152
BLOCKS = 16384
N_SLAB = 8
N_CELL = 32
DEVICES = 256


def draw_positions(key, part):
    key = jax.random.fold_in(key, 5)
    unit = jax.random.uniform(key, (3, SEGS), jnp.float32)
    owner = jnp.arange(SEGS, dtype=jnp.int32) // SEG_DEV
    shift_x = (owner // N_CELL).astype(jnp.float32)
    shift_y = (owner % N_CELL).astype(jnp.float32)
    return jnp.stack([unit[0] + shift_x, unit[1] + shift_y, unit[2]])


def draw_near_count(key, part):
    key = jax.random.fold_in(key, 11)
    first_key, second_key = jax.random.split(key)
    cells = BLOCKS // BLK_DEV
    pileup = jax.random.randint(first_key, (cells,), 0, 4) == 0
    pileup = pileup.at[0].set(True)
    owner = jnp.arange(BLOCKS, dtype=jnp.int32) // BLK_DEV
    ceiling = jnp.where(pileup[owner], NEAR, 2)
    random = jax.random.randint(second_key, (BLOCKS,), 0, NEAR)
    amount = 1 + random % ceiling
    return jnp.where(jnp.arange(BLOCKS, dtype=jnp.int32) % BLK_DEV == 0, ceiling, amount).astype(jnp.int32)


def plant(entries, key, low, top_value):
    longest = entries.shape.index(max(entries.shape))
    spots = []
    for shift in (0, 1):
        where = [jax.random.randint(jax.random.fold_in(key, axis), (), 0, length) for axis, length in enumerate(entries.shape)]
        where[longest] = (where[longest] + shift) % entries.shape[longest]
        spots.append(tuple(where))
    return entries.at[spots[0]].set(low).at[spots[1]].set(top_value)


def level_of(key, extent, shards, low, high):
    def one(position, blocks):
        steps = jax.random.uniform(jax.random.fold_in(jax.random.fold_in(key, 6), position), (blocks,), jnp.float32, low / len(shards), high / len(shards))
        return jnp.repeat(jnp.exp(steps), extent[position] // blocks).reshape((-1,) + (1,) * (len(extent) - position - 1))

    factor_of = one(*shards[0])
    for cut in shards[1:]:
        factor_of = factor_of * one(*cut)
    return factor_of


def gaussian(key, dims, spread, reach, cuts=(), held_as=jnp.bfloat16):
    factor_of = level_of(key, dims, cuts, -0.22, 0.18) if cuts else 1.0
    array = jax.random.normal(key, dims, jnp.float32) * spread * factor_of
    return jnp.minimum(jnp.maximum(array, -reach), reach).astype(held_as)


def setup_inputs(seed: int = 0) -> dict:
    keys = jax.random.split(jax.random.key(seed), 7)
    positions = draw_positions(jax.random.fold_in(keys[6], 71), 0)
    burgers = gaussian(keys[1], (3, SEGS), 0.003, 0.018, ((1, 256),), jnp.float32)
    mobility = jnp.clip(jnp.exp(math.log(2.0) - 1.3862944 * jax.random.uniform(keys[2], (SEGS,), jnp.float32) ** level_of(keys[2], (SEGS,), ((0, 256),), -0.2, 0.2)), 0.5, 2.0)
    near_list = plant(jax.random.randint(keys[3], (BLOCKS, NEAR), 0, EXT), jax.random.fold_in(keys[3], 1), 0, EXT - 1).astype(jnp.int32)
    near_count = draw_near_count(jax.random.fold_in(keys[6], 71), 0)
    send_list = plant(jax.random.randint(keys[5], (4, GHOST * DEVICES), 0, BLK_DEV), jax.random.fold_in(keys[5], 1), 0, BLK_DEV - 1).astype(jnp.int32)
    return dict(positions=positions, burgers=burgers, mobility=mobility, near_list=near_list, near_count=near_count, send_list=send_list)


core_sq = 0.04
far_sq = 1.0
time_step = 0.2
highest = lax.Precision.HIGHEST


def far_terms(places, burgers, lowest, amount, n_cells):
    targets = lowest + jnp.arange(amount, dtype=jnp.int32)
    centres = jnp.stack([(targets // n_cells).astype(jnp.float32) + 0.5, (targets % n_cells).astype(jnp.float32) + 0.5, jnp.full((amount,), 0.5, jnp.float32)])
    offsets = centres[:, :, None] - places[:, None, :]
    dist_sq = jnp.sum(offsets * offsets, axis=0) + far_sq
    inverse = dist_sq ** -1.5
    direct = jnp.einsum("cj,aj->ca", inverse, burgers, precision=highest)
    weighted = offsets * (inverse / dist_sq)[None]
    gradient = -3.0 * jnp.einsum("kcj,aj->cak", weighted, burgers, precision=highest)
    return jnp.concatenate([direct, gradient.reshape(amount, 9)], axis=1)


def pair_slot(target_places, ext_places, ext_burgers, column, live):
    source = jnp.take(ext_places, column, axis=1)
    source_burg = jnp.take(ext_burgers, column, axis=1)
    offsets = target_places[:, :, :, None] - source[:, :, None, :]
    dist_sq = jnp.sum(offsets * offsets, axis=0)
    kernel = (dist_sq + core_sq) ** -1.5 - (dist_sq + far_sq) ** -1.5
    kernel = jnp.where(live[:, None, None], kernel, 0.0)
    return jnp.einsum("bij,abj->abi", kernel, source_burg, precision=highest)


def reference(positions, burgers, mobility, near_list, near_count, send_list):
    def one_cell(lowest):
        return far_terms(positions, burgers, lowest, 1, N_CELL)[0]

    expansion = lax.map(one_cell, jnp.arange(DEVICES, dtype=jnp.int32))
    device_ids = jnp.arange(DEVICES, dtype=jnp.int32)
    centres = jnp.stack([(device_ids // N_CELL).astype(jnp.float32) + 0.5, (device_ids % N_CELL).astype(jnp.float32) + 0.5, jnp.full((DEVICES,), 0.5, jnp.float32)])
    lists = send_list.reshape(4, N_SLAB, N_CELL, GHOST)

    def far_force(places):
        grid = places.reshape(3, DEVICES, SEG_DEV)
        offsets = grid - centres[:, :, None]
        moved = jnp.einsum("dak,kdn->adn", expansion[:, 3:].reshape(DEVICES, 3, 3), offsets, precision=highest)
        return (expansion[:, :3].T[:, :, None] + moved).reshape(3, SEGS)

    def pick(values, direction):
        chosen = jnp.broadcast_to(lists[direction][None, :, :, :, None], (values.shape[0], N_SLAB, N_CELL, GHOST, 128))
        return jnp.take_along_axis(values, chosen, axis=3)

    def extend(values):
        width = values.shape[0]
        zero_slab = jnp.zeros((width, 1, N_CELL, GHOST, 128), values.dtype)
        zero_cell = jnp.zeros((width, N_SLAB, 1, GHOST, 128), values.dtype)
        from_lower = jnp.concatenate([zero_slab, pick(values, 0)[:, :-1]], axis=1)
        from_upper = jnp.concatenate([pick(values, 1)[:, 1:], zero_slab], axis=1)
        from_before = jnp.concatenate([zero_cell, pick(values, 2)[:, :, :-1]], axis=2)
        from_after = jnp.concatenate([pick(values, 3)[:, :, 1:], zero_cell], axis=2)
        joined = jnp.concatenate([values, from_lower, from_upper, from_before, from_after], axis=3)
        return joined.reshape(width, DEVICES, EXT, 128).transpose(1, 0, 2, 3)

    burg_grid = burgers.reshape(3, N_SLAB, N_CELL, BLK_DEV, 128)
    ext_burg = extend(burg_grid)
    lists_dev = near_list.reshape(DEVICES, BLK_DEV, NEAR)
    amounts = near_count.reshape(DEVICES, BLK_DEV)

    def short_range(places):
        grid = places.reshape(3, N_SLAB, N_CELL, BLK_DEV, 128)
        ext_places = extend(grid)
        own = grid.reshape(3, DEVICES, BLK_DEV, 128).transpose(1, 0, 2, 3)

        def one_device(items):
            own_places, table_places, table_burg, columns, live_count = items
            total = jnp.zeros((3, BLK_DEV, 128), jnp.float32)
            for slot in range(NEAR):
                total = total + pair_slot(own_places, table_places, table_burg, columns[:, slot], slot < live_count)
            return total

        forces = lax.map(one_device, (own, ext_places, ext_burg, lists_dev, amounts))
        return forces.transpose(1, 0, 2, 3).reshape(3, SEGS)

    moved_by = jnp.zeros(positions.shape, jnp.float32)
    for substep in range(SUBSTEPS):
        places = positions + moved_by
        moved_by = moved_by + time_step * mobility * (short_range(places) + far_force(places))
    places = positions + moved_by
    velocity = mobility * (short_range(places) + far_force(places))
    return moved_by, velocity
```

```python
import functools

import jax
import jax.numpy as jnp
from jax import lax
from jax.experimental import pallas as pl
from jax.experimental.pallas import tpu as pltpu
from jax.sharding import PartitionSpec as P

SUBSTEPS = 4
BLOCKS = 64
LANES = 128
NEAR = 6
GHOST = 48
EXT = 256
FEAT = 32
GROUP = 8
LEAD = GROUP
LIST = LEAD + BLOCKS * NEAR + 56

core_sq = 0.04
far_sq = 1.0
time_step = 0.2

f32 = jnp.float32
bf16 = jnp.bfloat16

vmem = pl.BlockSpec(memory_space=pltpu.VMEM)
smem = pl.BlockSpec(memory_space=pltpu.SMEM)
params = pltpu.CompilerParams(vmem_limit_bytes=48 * 2**20)


def round_bf16(x):
    return x.astype(bf16).astype(f32)


def split2(x):
    high = x.astype(bf16)
    return high, (x - high.astype(f32)).astype(bf16)


def split3(x):
    high = round_bf16(x)
    rest = x - high
    mid = round_bf16(rest)
    return high, mid, round_bf16(rest - mid)


def fill_sends(send_list, sources, sends):
    def body(n, carry):
        for d in range(4):
            block = send_list[d, n]
            for a, (ref, index) in enumerate(sources):
                sends[d][a, pl.ds(n, 1), :] = ref[index, pl.ds(block, 1), :]
        return carry

    lax.fori_loop(0, GHOST, body, 0, unroll=4)


def pack_kernel(send_list, centre, positions, burgers, places, *sends):
    for k in range(3):
        places[k] = positions[k] - centre[k]
    sources = [(places, k) for k in range(3)] + [(burgers, a) for a in range(3)]
    fill_sends(send_list, sources, sends)


def build_pairs(near_list, near_count, tb, ts, n_pairs):
    for i in range(LEAD):
        tb[i] = 0
        ts[i] = EXT

    def block(b, at):
        for slot in range(NEAR):
            tb[at + slot] = b
            ts[at + slot] = near_list[b, slot]
        return at + near_count[b]

    end = lax.fori_loop(0, BLOCKS, block, LEAD)
    for i in range(48):
        tb[end + i] = 0
        ts[end + i] = EXT
    n_pairs[0] = end - LEAD


def far_kernel(near_list, near_count, place, places, burgers, out, tb, ts, n_pairs, acc):
    build_pairs(near_list, near_count, tb, ts, n_pairs)
    acc[...] = jnp.zeros_like(acc)
    slab = place[0].astype(f32)
    cell = place[1].astype(f32)
    slabs = lax.broadcasted_iota(jnp.int32, (8, LANES), 0).astype(f32) - slab
    cells = lax.broadcasted_iota(jnp.int32, (32, LANES), 0).astype(f32) - cell
    column = lax.broadcasted_iota(jnp.int32, (LANES, LANES), 1)

    def body(b, carry):
        p = [places[k, pl.ds(b, 1), :] for k in range(3)]
        burg = [burgers[a, pl.ds(b, 1), :] for a in range(3)]
        high = [round_bf16(x) for x in burg]
        low = [x - h for x, h in zip(burg, high)]
        moment = [p[k] * burg[a] for k in range(3) for a in range(3)]
        m_high = [round_bf16(x) for x in moment]
        m_low = [x - h for x, h in zip(moment, m_high)]
        zero = jnp.zeros((LANES - 30, LANES), f32)
        rows = jnp.concatenate(high + low + high + low + m_high + m_low + [zero], axis=0)
        cols = rows.T
        first = jnp.where(column < 6, cols, 0.0).astype(bf16)
        second = jnp.where(column >= 6, cols, 0.0).astype(bf16)
        dx = slabs - p[0]
        dy = cells - p[1]
        along_slab = dx * dx
        along_cell = dy * dy + (p[2] * p[2] + far_sq)
        dist_sq = jnp.concatenate([along_slab[s : s + 1] + along_cell for s in range(8)], axis=0)
        r = lax.rsqrt(dist_sq)
        r2 = r * r
        w3 = r2 * r
        w5 = w3 * r2
        w3 = jnp.concatenate(split2(w3), axis=1)
        w5 = jnp.concatenate(split2(w5), axis=1)
        acc[...] += jnp.dot(
            w3, jnp.concatenate([first, first], axis=0), preferred_element_type=f32
        ) + jnp.dot(w5, jnp.concatenate([second, second], axis=0), preferred_element_type=f32)
        return carry

    lax.fori_loop(0, BLOCKS, body, 0)
    sums = jnp.concatenate([acc[:LANES].T, acc[LANES:].T], axis=1)
    target = lax.broadcasted_iota(jnp.int32, (1, 2 * LANES), 1)
    apart = [
        (target // 32).astype(f32) - slab,
        (target % 32).astype(f32) - cell,
        jnp.zeros((1, 2 * LANES), f32),
    ]

    def row(i):
        return sums[i : i + 1]

    direct = [row(a) + row(3 + a) for a in range(3)]
    total = [row(6 + a) + row(9 + a) for a in range(3)]
    gradient = []
    for a in range(3):
        for k in range(3):
            moment = row(12 + 3 * k + a) + row(21 + 3 * k + a)
            gradient.append(-3.0 * (apart[k] * total[a] - moment))
    zero = jnp.zeros((LANES - 12, 2 * LANES), f32)
    rows = jnp.concatenate(direct + gradient + [zero], axis=0)
    out[...] = jnp.concatenate([rows[:, :LANES].T, rows[:, LANES:].T], axis=0)


def tile_of(own, ghosts, index, tile):
    if tile < BLOCKS // 8:
        return own[index, 8 * tile : 8 * tile + 8, :]
    d, n = divmod(tile - BLOCKS // 8, GHOST // 8)
    return ghosts[d][index, 8 * n : 8 * n + 8, :]


def near_force(tb, ts, n_pairs, own, ghosts, burg, feat, left, right, acc, k_even, k_odd):
    shift = [(0, -1.0), (0, 1.0), (1, -1.0), (1, 1.0)]
    one = jnp.ones((8, LANES), f32)
    zero = jnp.zeros((8, LANES), f32)

    def store(ref, tile, values):
        for i, value in enumerate(values):
            ref[pl.ds(tile * 8 * FEAT + i, 8, stride=FEAT), :] = value

    right[...] = jnp.zeros_like(right)
    for tile in range(BLOCKS // 8):
        p = [tile_of(own, ghosts, k, tile) for k in range(3)]
        values = []
        for x in p:
            h, m, l = split3(-2.0 * x)
            values += [h, m, h, m, l, h]
        values += [one, one, one]
        values += list(split3(p[0] * p[0] + p[1] * p[1] + p[2] * p[2] + core_sq))
        store(feat, tile, values + [zero] * (FEAT - len(values)))
    for b in range(BLOCKS):
        right[LANES * b + 96 : LANES * b + 128, :] = feat[FEAT * b : FEAT * b + FEAT, :].astype(bf16)
    for tile in range(EXT // 8):
        p = [tile_of(own, ghosts, k, tile) for k in range(3)]
        if tile >= BLOCKS // 8:
            k, by = shift[(tile - BLOCKS // 8) // (GHOST // 8)]
            p[k] = p[k] + by
        values = []
        for x in p:
            h, m, l = split3(x)
            values += [h, h, m, m, h, l]
        values += list(split3(p[0] * p[0] + p[1] * p[1] + p[2] * p[2]))
        values += [one, one, one]
        store(feat, tile, values + [zero] * (FEAT - len(values)))
    left[EXT // 4] = jnp.zeros((LANES, LANES), bf16)
    for group in range(EXT // 4):
        left[group] = feat[LANES * group : LANES * group + LANES, :].T.astype(bf16)

    acc[...] = jnp.zeros_like(acc)
    k_odd[...] = jnp.zeros_like(k_odd)

    def half(step, k_now, k_before):
        for g in range(GROUP):
            if g % 2 == 0:
                i = (step - 1) * GROUP + g + LEAD
                t0, t1 = ts[i], ts[i + 1]
                rows = jnp.concatenate(
                    [burg[pl.ds(pl.multiple_of(8 * t, 8), 8), :] for t in (t0, t1)], axis=0
                ).astype(bf16)
                both = jnp.dot(
                    jnp.concatenate([rows, rows], axis=1),
                    jnp.concatenate([k_before[g], k_before[g + 1]], axis=1),
                    preferred_element_type=f32,
                )
                b0 = pl.ds(pl.multiple_of(8 * tb[i], 8), 8)
                acc[b0, :] = acc[b0, :] + both[:8, :LANES]
                b1 = pl.ds(pl.multiple_of(8 * tb[i + 1], 8), 8)
                acc[b1, :] = acc[b1, :] + both[8:, LANES:]
            i = step * GROUP + g + LEAD
            b, t = tb[i], ts[i]
            start = pl.multiple_of(LANES * b + 96 - FEAT * lax.rem(t, 4), FEAT)
            near_sq = jnp.dot(
                left[t // 4], right[pl.ds(start, LANES), :], preferred_element_type=f32
            )
            near_sq = jnp.maximum(near_sq, core_sq)
            r = lax.rsqrt(near_sq)
            q = lax.rsqrt(near_sq + (far_sq - core_sq))
            high, low = split2(r * r * r - q * q * q)
            k_now[g, :LANES, :] = high
            k_now[g, LANES:, :] = low

    def body(step, carry):
        half(2 * step, k_even, k_odd)
        half(2 * step + 1, k_odd, k_even)
        return carry

    steps = (n_pairs[0] + GROUP - 1) // GROUP + 1
    lax.fori_loop(0, (steps + 1) // 2, body, 0)


def component(acc, a):
    return acc[pl.ds(a, BLOCKS, stride=8), :] + acc[pl.ds(3 + a, BLOCKS, stride=8), :]


near_scratch = [
    pltpu.VMEM((EXT * FEAT, LANES), f32),
    pltpu.VMEM((EXT // 4 + 1, LANES, LANES), bf16),
    pltpu.VMEM((BLOCKS * LANES + 128, LANES), bf16),
    pltpu.VMEM((BLOCKS * 8, LANES), f32),
    pltpu.VMEM((GROUP, 2 * LANES, LANES), bf16),
    pltpu.VMEM((GROUP, 2 * LANES, LANES), bf16),
]


def first_kernel(tb, ts, n_pairs, exists, own, burgers, g0, g1, g2, g3, near, burg, *scratch):
    ghosts = (g0, g1, g2, g3)
    burg[...] = jnp.zeros_like(burg)
    for tile in range(EXT // 8):
        for a in range(3):
            if tile < BLOCKS // 8:
                value = burgers[a, 8 * tile : 8 * tile + 8, :]
            else:
                d = (tile - BLOCKS // 8) // (GHOST // 8)
                value = tile_of(None, ghosts, 3 + a, tile)
                value = jnp.where(exists[d] > 0, value, 0.0)
            high = round_bf16(value)
            burg[pl.ds(tile * 64 + a, 8, stride=8), :] = high
            burg[pl.ds(tile * 64 + 3 + a, 8, stride=8), :] = value - high
    near_force(tb, ts, n_pairs, own, ghosts, burg, *scratch)
    acc = scratch[3]
    for a in range(3):
        near[a] = component(acc, a)


def total_force(expansion, near, places):
    out = []
    for a in range(3):
        far = expansion[0:1, a : a + 1]
        for k in range(3):
            far = far + expansion[0:1, 3 + 3 * a + k : 4 + 3 * a + k] * places[k]
        out.append(near[a] + far)
    return out


def start_kernel(send_list, shares, near, places, mobility, expansion, moved, now, *sends):
    expansion[...] = jnp.broadcast_to(jnp.sum(shares[...], axis=0, keepdims=True), (8, LANES))
    values = expansion[...]
    p = [places[k] for k in range(3)]
    force = total_force(values, [near[a] for a in range(3)], p)
    for a in range(3):
        step = (time_step * mobility[...]) * force[a]
        moved[a] = step
        now[a] = p[a] + step
    fill_sends(send_list, [(now, k) for k in range(3)], sends)


def step_kernel(
    tb, ts, n_pairs, send_list, expansion, own, g0, g1, g2, g3, burg, mobility, places, moved,
    new_moved, now, s0, s1, s2, s3, *scratch
):
    near_force(tb, ts, n_pairs, own, (g0, g1, g2, g3), burg, *scratch)
    acc = scratch[3]
    force = total_force(
        expansion[...], [component(acc, a) for a in range(3)], [own[k] for k in range(3)]
    )
    for a in range(3):
        total = moved[a] + (time_step * mobility[...]) * force[a]
        new_moved[a] = total
        now[a] = places[a] + total
    fill_sends(send_list, [(now, k) for k in range(3)], (s0, s1, s2, s3))


def last_kernel(
    tb, ts, n_pairs, expansion, own, g0, g1, g2, g3, burg, mobility, velocity, *scratch
):
    near_force(tb, ts, n_pairs, own, (g0, g1, g2, g3), burg, *scratch)
    acc = scratch[3]
    force = total_force(
        expansion[...], [component(acc, a) for a in range(3)], [own[k] for k in range(3)]
    )
    for a in range(3):
        velocity[a] = mobility[...] * force[a]


def shape(*dims, dtype=f32):
    return jax.ShapeDtypeStruct(dims, dtype)


def exchange(sends):
    def moved(x, axis, by):
        n = lax.axis_size(axis)
        return lax.ppermute(x, axis, [(i, (i + by) % n) for i in range(n)])

    return [
        moved(sends[0], "slab", 1),
        moved(sends[1], "slab", -1),
        moved(sends[2], "cell", 1),
        moved(sends[3], "cell", -1),
    ]


def local(positions, burgers, mobility, near_list, near_count, send_list):
    n_slabs = lax.axis_size("slab")
    n_cells = lax.axis_size("cell")
    slab = lax.axis_index("slab")
    cell = lax.axis_index("cell")
    positions = positions.reshape(3, BLOCKS, LANES)
    burgers = burgers.reshape(3, BLOCKS, LANES)
    mobility = mobility.reshape(BLOCKS, LANES)
    place = jnp.stack([slab, cell]).astype(jnp.int32)
    centre = jnp.stack([slab + 0.5, cell + 0.5, jnp.float32(0.5)]).astype(f32)
    exists = jnp.stack([slab > 0, slab < n_slabs - 1, cell > 0, cell < n_cells - 1]).astype(
        jnp.int32
    )
    block = shape(3, BLOCKS, LANES)
    send = shape(3, GHOST, LANES)

    places, *sends = pl.pallas_call(
        pack_kernel,
        out_shape=[block] + [shape(6, GHOST, LANES)] * 4,
        in_specs=[smem, smem, vmem, vmem],
        out_specs=[vmem] * 5,
        compiler_params=params,
        name="pack",
    )(send_list, centre, positions, burgers)
    ghosts = exchange(sends)

    shares, tb, ts, n_pairs = pl.pallas_call(
        far_kernel,
        out_shape=[
            shape(EXT, LANES),
            shape(LIST, dtype=jnp.int32),
            shape(LIST, dtype=jnp.int32),
            shape(1, dtype=jnp.int32),
        ],
        in_specs=[smem, smem, smem, vmem, vmem],
        out_specs=[vmem, smem, smem, smem],
        scratch_shapes=[pltpu.VMEM((EXT, LANES), f32)],
        compiler_params=params,
        name="far",
    )(near_list, near_count, place, places, burgers)
    shares = lax.all_to_all(shares, ("slab", "cell"), 0, 0, tiled=True)

    near, burg = pl.pallas_call(
        first_kernel,
        out_shape=[block, shape((EXT + 1) * 8, LANES)],
        in_specs=[smem] * 4 + [vmem] * 6,
        out_specs=[vmem] * 2,
        scratch_shapes=near_scratch,
        compiler_params=params,
        name="near_first",
    )(tb, ts, n_pairs, exists, places, burgers, *ghosts)

    expansion, moved, now, *sends = pl.pallas_call(
        start_kernel,
        out_shape=[shape(8, LANES), block, block] + [send] * 4,
        in_specs=[smem] + [vmem] * 4,
        out_specs=[vmem] * 7,
        compiler_params=params,
        name="start",
    )(send_list, shares, near, places, mobility)

    for _ in range(1, SUBSTEPS):
        ghosts = exchange(sends)
        moved, now, *sends = pl.pallas_call(
            step_kernel,
            out_shape=[block, block] + [send] * 4,
            in_specs=[smem] * 4 + [vmem] * 10,
            out_specs=[vmem] * 6,
            scratch_shapes=near_scratch,
            compiler_params=params,
            name="near_step",
        )(tb, ts, n_pairs, send_list, expansion, now, *ghosts, burg, mobility, places, moved)

    ghosts = exchange(sends)
    velocity = pl.pallas_call(
        last_kernel,
        out_shape=block,
        in_specs=[smem] * 3 + [vmem] * 8,
        out_specs=vmem,
        scratch_shapes=near_scratch,
        compiler_params=params,
        name="near_last",
    )(tb, ts, n_pairs, expansion, now, *ghosts, burg, mobility)
    return moved.reshape(3, -1), velocity.reshape(3, -1)


def solution(mesh):
    return jax.shard_map(
        local,
        mesh=mesh,
        in_specs=(
            P(None, ("slab", "cell")),
            P(None, ("slab", "cell")),
            P(("slab", "cell")),
            P(("slab", "cell"), None),
            P(("slab", "cell")),
            P(None, ("slab", "cell")),
        ),
        out_specs=(P(None, ("slab", "cell")), P(None, ("slab", "cell"))),
        check_vma=False,
    )
```

```python
import functools

import jax
import jax.numpy as jnp
from jax import lax
from jax.experimental import pallas as pl
from jax.experimental.pallas import tpu as pltpu
from jax.sharding import PartitionSpec as P

SUBSTEPS = 4
BLOCKS = 64
LANES = 128
NEAR = 6
GHOST = 48
EXT = 256
GROUP = 8
LEAD = GROUP
LIST = LEAD + BLOCKS * NEAR + 64

core_sq = 0.04
far_sq = 1.0
time_step = 0.2

f32 = jnp.float32
bf16 = jnp.bfloat16

vmem = pl.BlockSpec(memory_space=pltpu.VMEM)
smem = pl.BlockSpec(memory_space=pltpu.SMEM)
params = pltpu.CompilerParams(vmem_limit_bytes=48 * 2**20)


def round_bf16(x):
    return x.astype(bf16).astype(f32)


def split2(x):
    high = x.astype(bf16)
    return high, (x - high.astype(f32)).astype(bf16)


def split3(x):
    high = round_bf16(x)
    rest = x - high
    mid = round_bf16(rest)
    return high, mid, round_bf16(rest - mid)


def fill_sends(send_list, sources, sends):
    def body(n, carry):
        for d in range(4):
            block = send_list[d, n]
            for a, (ref, index) in enumerate(sources):
                sends[d][a, pl.ds(n, 1), :] = ref[index, pl.ds(block, 1), :]
        return carry

    lax.fori_loop(0, GHOST, body, 0, unroll=4)


def centre_of():
    slab = lax.axis_index("slab").astype(f32)
    cell = lax.axis_index("cell").astype(f32)
    return slab, cell


def pack_kernel(send_list, positions, burgers, places, burg, *sends):
    slab, cell = centre_of()
    centre = (slab + 0.5, cell + 0.5, 0.5)
    for b in range(BLOCKS):
        for k in range(3):
            part = (pl.ds(k, 1), pl.ds(LANES * b, LANES))
            places[k, b : b + 1, :] = positions[part] - centre[k]
            burg[k, b : b + 1, :] = burgers[part]
    sources = [(places, k) for k in range(3)] + [(burg, a) for a in range(3)]
    fill_sends(send_list, sources, sends)


def put_rows(out, k, value):
    for b in range(BLOCKS):
        out[k : k + 1, LANES * b : LANES * b + LANES] = value[b : b + 1]


def build_pairs(near_list, near_count, tb, ts, first, count, at):
    for b in range(count):
        for slot in range(NEAR):
            tb[at + slot] = first + b
            ts[at + slot] = near_list[slot, first + b]
        at = at + near_count[first + b]
    return at


def halves(tile):
    low = lax.broadcasted_iota(jnp.int32, (8, LANES), 0) < 4
    turned = pltpu.roll(tile, 4, 0)
    return jnp.where(low, tile, turned), jnp.where(low, turned, tile)


def pair_rows(values):
    low = lax.broadcasted_iota(jnp.int32, (8, LANES), 0) < 4
    rows = [
        x if x is y else jnp.where(low, x, y) for x, y in zip(values[0::2], values[1::2])
    ]
    rows += [jnp.zeros((8, LANES), f32)] * (LANES // 8 - len(rows))
    return jnp.concatenate(rows, axis=0)


def far_kernel(
    near_list, near_count, places, burgers, out, tb, ts, n_pairs, acc, weights, w_even, w_odd, c_even, c_odd
):
    for i in range(LEAD):
        tb[i] = 0
        ts[i] = EXT
    for tile in range(BLOCKS // 8):
        p = [halves(places[k, 8 * tile : 8 * tile + 8, :]) for k in range(3)]
        burg = [halves(burgers[a, 8 * tile : 8 * tile + 8, :]) for a in range(3)]
        for half in range(2):
            sources = [x[half] for x in burg]
            moments = [p[k][half] * x for k in range(3) for x in sources]
            values = []
            for group in (sources, moments):
                high = [round_bf16(x) for x in group]
                values += high + [x - h for x, h in zip(group, high)]
            weights[2 * tile + half] = pair_rows(values).T.astype(bf16)
    acc[...] = jnp.zeros_like(acc)
    w_odd[...] = jnp.zeros_like(w_odd)
    c_odd[...] = jnp.zeros_like(c_odd)
    slab, cell = centre_of()
    slabs = lax.broadcasted_iota(jnp.int32, (8, LANES), 0).astype(f32) - slab
    cells = lax.broadcasted_iota(jnp.int32, (32, LANES), 0).astype(f32) - cell
    lane = lax.broadcasted_iota(jnp.int32, (LANES, LANES), 1) % 4

    def half(group, at, w_now, c_now, w_before, c_before):
        at = build_pairs(near_list, near_count, tb, ts, 4 * group, 4, at)
        shares = weights[group].astype(f32)
        for g in range(4):
            b = 4 * group + g
            p = [places[k, pl.ds(b, 1), :] for k in range(3)]
            dx = slabs - p[0]
            dy = cells - p[1]
            along_slab = dx * dx
            along_cell = dy * dy + (p[2] * p[2] + far_sq)
            for s in range(8):
                r = lax.rsqrt(along_slab[s : s + 1] + along_cell)
                r2 = r * r
                w3 = r2 * r
                for at_row, w in ((32 * s, w3), (EXT + 32 * s, w3 * r2)):
                    high, low = split2(w)
                    w_now[at_row : at_row + 32, 256 * g : 256 * g + 128] = high
                    w_now[at_row : at_row + 32, 256 * g + 128 : 256 * g + 256] = low
            mine = jnp.where(lane == g, shares, 0.0).astype(bf16)
            c_now[256 * g : 256 * g + 128, :] = mine
            c_now[256 * g + 128 : 256 * g + 256, :] = mine
        acc[...] += jnp.dot(w_before[...], c_before[...], preferred_element_type=f32)
        return at

    def body(step, at):
        at = half(2 * step, at, w_even, c_even, w_odd, c_odd)
        return half(2 * step + 1, at, w_odd, c_odd, w_even, c_even)

    end = lax.fori_loop(0, BLOCKS // 8, body, LEAD)
    acc[...] += jnp.dot(w_odd[...], c_odd[...], preferred_element_type=f32)
    for i in range(56):
        tb[end + i] = 0
        ts[end + i] = EXT
    n_pairs[0] = end - LEAD

    sums3, sums5 = (
        jnp.concatenate([acc[i : i + LANES].T, acc[i + LANES : i + 2 * LANES].T], axis=1)
        for i in (0, EXT)
    )
    target = lax.broadcasted_iota(jnp.int32, (1, 2 * LANES), 1)
    apart = [
        (target // 32).astype(f32) - slab,
        (target % 32).astype(f32) - cell,
        jnp.zeros((1, 2 * LANES), f32),
    ]

    def row(sums, i):
        return jnp.sum(sums[4 * i : 4 * i + 4], axis=0, keepdims=True)

    direct = [row(sums3, a) + row(sums3, 3 + a) for a in range(3)]
    total = [row(sums5, a) + row(sums5, 3 + a) for a in range(3)]
    gradient = []
    for a in range(3):
        for k in range(3):
            moment = row(sums5, 6 + 3 * k + a) + row(sums5, 15 + 3 * k + a)
            gradient.append(-3.0 * (apart[k] * total[a] - moment))
    zero = jnp.zeros((LANES - 12, 2 * LANES), f32)
    rows = jnp.concatenate(direct + gradient + [zero], axis=0)
    out[...] = jnp.concatenate([rows[:, :LANES].T, rows[:, LANES:].T], axis=0)


def tile_of(own, ghosts, index, tile):
    if tile < BLOCKS // 8:
        return own[index, 8 * tile : 8 * tile + 8, :]
    d, n = divmod(tile - BLOCKS // 8, GHOST // 8)
    return ghosts[d][index, 8 * n : 8 * n + 8, :]


def near_force(tb, ts, n_pairs, own, ghosts, burg, parts, left, right, mask, acc, k_even, k_odd):
    shift = [(0, -1.0), (0, 1.0), (1, -1.0), (1, 1.0)]
    one = jnp.ones((8, LANES), f32)
    low = lax.broadcasted_iota(jnp.int32, (8, LANES), 0) < 4

    for tile in range(EXT // 8):
        p = [tile_of(own, ghosts, k, tile) for k in range(3)]
        if tile >= BLOCKS // 8:
            k, by = shift[(tile - BLOCKS // 8) // (GHOST // 8)]
            p[k] = p[k] + by
        p = [halves(x) for x in p]
        for half in range(2):
            x = [v[half] for v in p]
            values = []
            for v in x:
                h, m, l = split3(v)
                values += [h, h, m, m, h, l]
            values += list(split3(x[0] * x[0] + x[1] * x[1] + x[2] * x[2]))
            values += [one, one, one]
            left[2 * tile + half] = pair_rows(values).T.astype(bf16)
    left[EXT // 4] = jnp.zeros((LANES, LANES), bf16)
    x = [own[k] for k in range(3)]
    for k in range(3):
        for i, part in enumerate(split3(-2.0 * x[k])):
            parts[3 * k + i] = part
    for i, part in enumerate(split3(x[0] * x[0] + x[1] * x[1] + x[2] * x[2] + core_sq)):
        parts[9 + i] = part
    for b in range(BLOCKS):
        def row(i):
            return jnp.broadcast_to(parts[i, b : b + 1, :], (8, LANES))

        rows = []
        for k in range(3):
            h, m, l = row(3 * k), row(3 * k + 1), row(3 * k + 2)
            high_mid = jnp.where(low, h, m)
            rows += [high_mid, high_mid, jnp.where(low, l, h)]
        rows += [one, jnp.where(low, one, row(9)), jnp.where(low, row(10), row(11))]
        for i in range(6):
            right[b, i] = jnp.concatenate(rows[2 * i : 2 * i + 2], axis=0).astype(bf16)
        right[b, 6:] = jnp.zeros((2, 16, LANES), bf16)
    place = lax.broadcasted_iota(jnp.int32, (16, LANES), 0) % 4
    for g in range(4):
        mask[g] = jnp.where(place == g, 1.0, 0.0).astype(bf16)

    acc[...] = jnp.zeros_like(acc)
    k_odd[...] = jnp.zeros_like(k_odd)

    def half(step, k_now, k_before):
        for g in range(GROUP):
            if g % 2 == 0:
                i = (step - 1) * GROUP + g + LEAD
                t0, t1 = ts[i], ts[i + 1]
                rows = jnp.concatenate(
                    [burg[pl.ds(pl.multiple_of(8 * t, 8), 8), :] for t in (t0, t1)], axis=0
                ).astype(bf16)
                both = jnp.dot(
                    jnp.concatenate([rows, rows], axis=1),
                    jnp.concatenate([k_before[g], k_before[g + 1]], axis=1),
                    preferred_element_type=f32,
                )
                b0 = pl.ds(pl.multiple_of(8 * tb[i], 8), 8)
                acc[b0, :] = acc[b0, :] + both[:8, :LANES]
                b1 = pl.ds(pl.multiple_of(8 * tb[i + 1], 8), 8)
                acc[b1, :] = acc[b1, :] + both[8:, LANES:]
            i = step * GROUP + g + LEAD
            b, t = tb[i], ts[i]
            features = (right[b] * mask[lax.rem(t, 4)][None]).reshape(LANES, LANES)
            near_sq = jnp.dot(left[t // 4], features, preferred_element_type=f32)
            near_sq = jnp.maximum(near_sq, core_sq)
            r = lax.rsqrt(near_sq)
            q = lax.rsqrt(near_sq + (far_sq - core_sq))
            high, low = split2(r * r * r - q * q * q)
            k_now[g, :LANES, :] = high
            k_now[g, LANES:, :] = low

    def body(step, carry):
        half(2 * step, k_even, k_odd)
        half(2 * step + 1, k_odd, k_even)
        return carry

    steps = (n_pairs[0] + GROUP - 1) // GROUP + 1
    lax.fori_loop(0, (steps + 1) // 2, body, 0)


def component(acc, a):
    return acc[pl.ds(a, BLOCKS, stride=8), :] + acc[pl.ds(3 + a, BLOCKS, stride=8), :]


near_scratch = [
    pltpu.VMEM((12, BLOCKS, LANES), f32),
    pltpu.VMEM((EXT // 4 + 1, LANES, LANES), bf16),
    pltpu.VMEM((BLOCKS, 8, 16, LANES), bf16),
    pltpu.VMEM((4, 16, LANES), bf16),
    pltpu.VMEM((BLOCKS * 8, LANES), f32),
    pltpu.VMEM((GROUP, 2 * LANES, LANES), bf16),
    pltpu.VMEM((GROUP, 2 * LANES, LANES), bf16),
]


def first_kernel(tb, ts, n_pairs, own, burgers, g0, g1, g2, g3, near, burg, *scratch):
    ghosts = (g0, g1, g2, g3)
    slab, cell = lax.axis_index("slab"), lax.axis_index("cell")
    n_slabs, n_cells = lax.axis_size("slab"), lax.axis_size("cell")
    exists = (slab > 0, slab < n_slabs - 1, cell > 0, cell < n_cells - 1)
    burg[...] = jnp.zeros_like(burg)
    for tile in range(EXT // 8):
        for a in range(3):
            if tile < BLOCKS // 8:
                value = burgers[a, 8 * tile : 8 * tile + 8, :]
            else:
                d = (tile - BLOCKS // 8) // (GHOST // 8)
                value = tile_of(None, ghosts, 3 + a, tile)
                value = jnp.where(exists[d], value, 0.0)
            high = round_bf16(value)
            burg[pl.ds(tile * 64 + a, 8, stride=8), :] = high
            burg[pl.ds(tile * 64 + 3 + a, 8, stride=8), :] = value - high
    near_force(tb, ts, n_pairs, own, ghosts, burg, *scratch)
    acc = scratch[4]
    for a in range(3):
        near[a] = component(acc, a)


def total_force(expansion, near, places):
    out = []
    for a in range(3):
        far = expansion[0:1, a : a + 1]
        for k in range(3):
            far = far + expansion[0:1, 3 + 3 * a + k : 4 + 3 * a + k] * places[k]
        out.append(near[a] + far)
    return out


def start_kernel(send_list, shares, near, places, mobility, expansion, moved, now, *sends):
    expansion[...] = jnp.broadcast_to(jnp.sum(shares[...], axis=0, keepdims=True), (8, LANES))
    values = expansion[...]
    p = [places[k] for k in range(3)]
    force = total_force(values, [near[a] for a in range(3)], p)
    for a in range(3):
        step = (time_step * mobility[...]) * force[a]
        moved[a] = step
        now[a] = p[a] + step
    fill_sends(send_list, [(now, k) for k in range(3)], sends)


def step_kernel(
    final, tb, ts, n_pairs, send_list, expansion, own, g0, g1, g2, g3, burg, mobility, places, moved,
    new_moved, now, s0, s1, s2, s3, *scratch
):
    near_force(tb, ts, n_pairs, own, (g0, g1, g2, g3), burg, *scratch)
    acc = scratch[4]
    force = total_force(
        expansion[...], [component(acc, a) for a in range(3)], [own[k] for k in range(3)]
    )
    for a in range(3):
        total = moved[a] + (time_step * mobility[...]) * force[a]
        if final:
            put_rows(new_moved, a, total)
        else:
            new_moved[a] = total
        now[a] = places[a] + total
    fill_sends(send_list, [(now, k) for k in range(3)], (s0, s1, s2, s3))


def last_kernel(
    tb, ts, n_pairs, expansion, own, g0, g1, g2, g3, burg, mobility, velocity, *scratch
):
    near_force(tb, ts, n_pairs, own, (g0, g1, g2, g3), burg, *scratch)
    acc = scratch[4]
    force = total_force(
        expansion[...], [component(acc, a) for a in range(3)], [own[k] for k in range(3)]
    )
    for a in range(3):
        put_rows(velocity, a, mobility[...] * force[a])


def cost(flops):
    return pl.CostEstimate(flops=int(flops), bytes_accessed=2**20, transcendentals=0)


def shape(*dims, dtype=f32):
    return jax.ShapeDtypeStruct(dims, dtype)


def exchange(sends):
    def moved(x, axis, by):
        n = lax.axis_size(axis)
        return lax.ppermute(x, axis, [(i, (i + by) % n) for i in range(n)])

    return [
        moved(sends[0], "slab", 1),
        moved(sends[1], "slab", -1),
        moved(sends[2], "cell", 1),
        moved(sends[3], "cell", -1),
    ]


def local(positions, burgers, mobility, near_list, near_count, send_list):
    mobility = mobility.reshape(BLOCKS, LANES)
    flat = shape(*positions.shape)
    block = shape(3, BLOCKS, LANES)
    send = shape(3, GHOST, LANES)

    places, burgers, *sends = pl.pallas_call(
        pack_kernel,
        out_shape=[block, block] + [shape(6, GHOST, LANES)] * 4,
        in_specs=[smem, vmem, vmem],
        out_specs=[vmem] * 6,
        compiler_params=params,
        name="pack",
    )(send_list, positions, burgers)
    ghosts = exchange(sends)

    shares, tb, ts, n_pairs = pl.pallas_call(
        far_kernel,
        out_shape=[
            shape(EXT, LANES),
            shape(LIST, dtype=jnp.int32),
            shape(LIST, dtype=jnp.int32),
            shape(1, dtype=jnp.int32),
        ],
        in_specs=[smem, smem, vmem, vmem],
        out_specs=[vmem, smem, smem, smem],
        scratch_shapes=[
            pltpu.VMEM((2 * EXT, LANES), f32),
            pltpu.VMEM((BLOCKS // 4, LANES, LANES), bf16),
            pltpu.VMEM((2 * EXT, 8 * LANES), bf16),
            pltpu.VMEM((2 * EXT, 8 * LANES), bf16),
            pltpu.VMEM((8 * LANES, LANES), bf16),
            pltpu.VMEM((8 * LANES, LANES), bf16),
        ],
        compiler_params=params,
        cost_estimate=cost(20e9),
        name="far",
    )(near_list.T, near_count, places, burgers)
    shares = lax.all_to_all(shares, ("slab", "cell"), 0, 0, tiled=True)

    near, burg = pl.pallas_call(
        first_kernel,
        out_shape=[block, shape((EXT + 1) * 8, LANES)],
        in_specs=[smem] * 3 + [vmem] * 6,
        out_specs=[vmem] * 2,
        scratch_shapes=near_scratch,
        compiler_params=params,
        cost_estimate=cost(20e9),
        name="near_first",
    )(tb, ts, n_pairs, places, burgers, *ghosts)

    expansion, moved, now, *sends = pl.pallas_call(
        start_kernel,
        out_shape=[shape(8, LANES), block, block] + [send] * 4,
        in_specs=[smem] + [vmem] * 4,
        out_specs=[vmem] * 7,
        compiler_params=params,
        name="start",
    )(send_list, shares, near, places, mobility)

    for substep in range(1, SUBSTEPS):
        final = substep == SUBSTEPS - 1
        ghosts = exchange(sends)
        moved, now, *sends = pl.pallas_call(
            functools.partial(step_kernel, final),
            out_shape=[flat if final else block, block] + [send] * 4,
            in_specs=[smem] * 4 + [vmem] * 10,
            out_specs=[vmem] * 6,
            scratch_shapes=near_scratch,
            compiler_params=params,
            cost_estimate=cost(20e9),
            name="near_step",
        )(tb, ts, n_pairs, send_list, expansion, now, *ghosts, burg, mobility, places, moved)

    ghosts = exchange(sends)
    velocity = pl.pallas_call(
        last_kernel,
        out_shape=flat,
        in_specs=[smem] * 3 + [vmem] * 8,
        out_specs=vmem,
        scratch_shapes=near_scratch,
        compiler_params=params,
        cost_estimate=cost(20e9),
        name="near_last",
    )(tb, ts, n_pairs, expansion, now, *ghosts, burg, mobility)
    return moved, velocity


def solution(mesh):
    return jax.shard_map(
        local,
        mesh=mesh,
        in_specs=(
            P(None, ("slab", "cell")),
            P(None, ("slab", "cell")),
            P(("slab", "cell")),
            P(("slab", "cell"), None),
            P(("slab", "cell")),
            P(None, ("slab", "cell")),
        ),
        out_specs=(P(None, ("slab", "cell")), P(None, ("slab", "cell"))),
        check_vma=False,
    )
```

```python
import functools

import jax
import jax.numpy as jnp
from jax import lax
from jax.experimental import pallas as pl
from jax.experimental.pallas import tpu as pltpu
from jax.sharding import PartitionSpec as P

SUBSTEPS = 4
BLOCKS = 64
LANES = 128
NEAR = 6
GHOST = 48
EXT = 256
GROUP = 8
LEAD = GROUP
TAIL = 56
AT_SENDS = 8
AT_PAIRS = AT_SENDS + 4 * GHOST + LEAD
CONTROL = AT_PAIRS + BLOCKS * NEAR + TAIL
SHARE = 9

core_sq = 0.04
far_sq = 1.0
time_step = 0.2

f32 = jnp.float32
bf16 = jnp.bfloat16

vmem = pl.BlockSpec(memory_space=pltpu.VMEM)
smem = pl.BlockSpec(memory_space=pltpu.SMEM)
params = pltpu.CompilerParams(vmem_limit_bytes=48 * 2**20)


def round_bf16(x):
    return x.astype(bf16).astype(f32)


def split2(x):
    high = x.astype(bf16)
    return high, (x - high.astype(f32)).astype(bf16)


def split3(x):
    high = round_bf16(x)
    rest = x - high
    mid = round_bf16(rest)
    return high, mid, round_bf16(rest - mid)


def parity():
    return lax.axis_index("slab") % 2, lax.axis_index("cell") % 2


def send_rows():
    odd_slab, odd_cell = parity()
    return odd_slab, 1 - odd_slab, 3 - odd_cell, 2 + odd_cell


def slot_moves():
    odd_slab, odd_cell = parity()
    return (
        GHOST * (1 - odd_slab),
        GHOST * (odd_slab - 1),
        GHOST * odd_cell,
        -GHOST * odd_cell,
    )


def slot_shifts():
    odd_slab, odd_cell = parity()
    along_slab = (1 - 2 * odd_slab).astype(f32)
    along_cell = (1 - 2 * odd_cell).astype(f32)
    return (0, along_slab), (0, -along_slab), (1, -along_cell), (1, along_cell)


def slot_exists():
    out = []
    for axis in ("slab", "cell"):
        i = lax.axis_index(axis)
        partner = i - 1 + 2 * (i % 2)
        out.append((partner >= 0) & (partner < lax.axis_size(axis)))
    return None, out[0], out[1], None


def fill_sends(block_of, sources, sends):
    def body(n, carry):
        for d in range(4):
            block = block_of(d, n)
            for a, (ref, index) in enumerate(sources):
                sends[d][a, pl.ds(n, 1), :] = ref[index, pl.ds(block, 1), :]
        return carry

    lax.fori_loop(0, GHOST, body, 0, unroll=4)


def send_now(control, now, sends):
    fill_sends(
        lambda d, n: control[AT_SENDS + GHOST * d + n], [(now, k) for k in range(3)], sends
    )


def centre_of():
    slab = lax.axis_index("slab").astype(f32)
    cell = lax.axis_index("cell").astype(f32)
    return slab, cell


def pack_kernel(send_list, positions, burgers, places, burg, *sends):
    slab, cell = centre_of()
    centre = (slab + 0.5, cell + 0.5, 0.5)
    for b in range(BLOCKS):
        for k in range(3):
            part = (pl.ds(k, 1), pl.ds(LANES * b, LANES))
            places[k, b : b + 1, :] = positions[part] - centre[k]
            burg[k, b : b + 1, :] = burgers[part]
    sources = [(places, k) for k in range(3)] + [(burg, a) for a in range(3)]
    rows = send_rows()
    fill_sends(lambda d, n: send_list[rows[d], n], sources, sends)


def put_rows(out, k, value):
    for b in range(BLOCKS):
        out[k : k + 1, LANES * b : LANES * b + LANES] = value[b : b + 1]


def pair_words(near_list):
    segment = (near_list + (GHOST - BLOCKS)) // GHOST
    moved = near_list
    for i, move in enumerate(slot_moves()):
        moved = moved + jnp.where(segment == 1 + i, move, 0)
    block = lax.broadcasted_iota(jnp.int32, near_list.shape, 0)
    return (2**SHARE * block + moved).reshape(-1)


def halves(tile):
    low = lax.broadcasted_iota(jnp.int32, (8, LANES), 0) < 4
    turned = pltpu.roll(tile, 4, 0)
    return jnp.where(low, tile, turned), jnp.where(low, turned, tile)


def pair_rows(values):
    low = lax.broadcasted_iota(jnp.int32, (8, LANES), 0) < 4
    rows = [
        x if x is y else jnp.where(low, x, y) for x, y in zip(values[0::2], values[1::2])
    ]
    rows += [jnp.zeros((8, LANES), f32)] * (LANES // 8 - len(rows))
    return jnp.concatenate(rows, axis=0)


def far_kernel(
    send_list, words, near_count, places, burgers, out, control, acc, rows, cols, apart_by, w_even, w_odd
):
    from_row = send_rows()
    for i in range(LEAD):
        control[AT_PAIRS - LEAD + i] = EXT
    for tile in range(BLOCKS // 8):
        p = [halves(places[k, 8 * tile : 8 * tile + 8, :]) for k in range(3)]
        burg = [halves(burgers[a, 8 * tile : 8 * tile + 8, :]) for a in range(3)]
        for half in range(2):
            here = [x[half] for x in p]
            sources = [x[half] for x in burg]
            moments = [x * y for x in here for y in sources]
            values = []
            for group in (sources, moments):
                high = [round_bf16(x) for x in group]
                values += high + [x - h for x, h in zip(group, high)]
            rows[2 * tile + half] = pair_rows(values)
            one = jnp.ones((8, LANES), f32)
            square = sum(x * x for x in here) + far_sq
            values = [part for x in (here[0], here[1], square) for part in split3(x)]
            cols[2 * tile + half] = pair_rows(values + [one, one, one]).T.astype(bf16)
    acc[...] = jnp.zeros_like(acc)
    w_odd[...] = jnp.zeros_like(w_odd)
    slab, cell = centre_of()
    target = lax.broadcasted_iota(jnp.int32, (1, EXT), 1)
    apart = [(target // 32).astype(f32) - slab, (target % 32).astype(f32) - cell]
    square = apart[0] * apart[0] + apart[1] * apart[1]
    square_high = round_bf16(square)
    place = lax.broadcasted_iota(jnp.int32, (LANES, EXT), 0)
    values = jnp.where(place < 36, 1.0, 0.0)
    for first, last, x in (
        (0, 12, -2.0 * apart[0]),
        (12, 24, -2.0 * apart[1]),
        (36, 40, square_high),
        (40, 44, square - square_high),
    ):
        values = jnp.where((place >= first) & (place < last), x, values)
    for g in range(4):
        apart_by[g] = jnp.where(place % 4 == g, values, 0.0).astype(bf16)

    def sums(group, g, w):
        mine = rows[group, pl.ds(g, 32, stride=4), :].astype(bf16)
        acc[...] += jnp.dot(
            jnp.concatenate([mine, mine], axis=1), w[g], preferred_element_type=f32
        )

    def half(group, at, w_now, w_before):
        for i in range(4):
            b = 4 * group + i
            for slot in range(NEAR):
                control[at + slot] = words[NEAR * b + slot]
            at = at + near_count[b]
        for d in range(4):
            for i in range(3):
                n = 3 * group + i
                control[AT_SENDS + GHOST * d + n] = send_list[from_row[d], n]
        for g in range(4):
            sums(jnp.maximum(group - 1, 0), g, w_before)
            r = lax.rsqrt(jnp.dot(cols[group], apart_by[g], preferred_element_type=f32))
            r2 = r * r
            w3 = r2 * r
            for k, w in enumerate((w3, w3 * r2)):
                high, low = split2(w)
                w_now[g, :LANES, EXT * k : EXT * k + EXT] = high
                w_now[g, LANES:, EXT * k : EXT * k + EXT] = low
        return at

    def body(step, at):
        at = half(2 * step, at, w_even, w_odd)
        return half(2 * step + 1, at, w_odd, w_even)

    end = lax.fori_loop(0, BLOCKS // 8, body, AT_PAIRS)
    for g in range(4):
        sums(BLOCKS // 4 - 1, g, w_odd)
    for i in range(TAIL):
        control[end + i] = EXT
    control[0] = end - AT_PAIRS

    apart = apart + [jnp.zeros((1, EXT), f32)]

    def row(k, i):
        return acc[i : i + 1, EXT * k : EXT * k + EXT]

    direct = [row(0, a) + row(0, 3 + a) for a in range(3)]
    total = [row(1, a) + row(1, 3 + a) for a in range(3)]
    gradient = []
    for a in range(3):
        for k in range(3):
            moment = row(1, 6 + 3 * k + a) + row(1, 15 + 3 * k + a)
            gradient.append(-3.0 * (apart[k] * total[a] - moment))
    zero = jnp.zeros((LANES - 12, 2 * LANES), f32)
    values = jnp.concatenate(direct + gradient + [zero], axis=0)
    out[...] = jnp.concatenate([values[:, :LANES].T, values[:, LANES:].T], axis=0)


def tile_of(own, ghosts, index, tile):
    if tile < BLOCKS // 8:
        return own[index, 8 * tile : 8 * tile + 8, :]
    d, n = divmod(tile - BLOCKS // 8, GHOST // 8)
    return ghosts[d][index, 8 * n : 8 * n + 8, :]


def near_force(control, own, ghosts, burg, parts, left, right, mask, acc, k_even, k_odd):
    shift = slot_shifts()
    one = jnp.ones((8, LANES), f32)
    low = lax.broadcasted_iota(jnp.int32, (8, LANES), 0) < 4

    for tile in range(EXT // 8):
        p = [tile_of(own, ghosts, k, tile) for k in range(3)]
        if tile >= BLOCKS // 8:
            k, by = shift[(tile - BLOCKS // 8) // (GHOST // 8)]
            p[k] = p[k] + by
        p = [halves(x) for x in p]
        for half in range(2):
            x = [v[half] for v in p]
            values = []
            for v in x:
                h, m, l = split3(v)
                values += [h, h, m, m, h, l]
            values += list(split3(x[0] * x[0] + x[1] * x[1] + x[2] * x[2]))
            values += [one, one, one]
            left[2 * tile + half] = pair_rows(values).T.astype(bf16)
    left[EXT // 4] = jnp.zeros((LANES, LANES), bf16)
    x = [own[k] for k in range(3)]
    for k in range(3):
        for i, part in enumerate(split3(-2.0 * x[k])):
            parts[3 * k + i] = part
    for i, part in enumerate(split3(x[0] * x[0] + x[1] * x[1] + x[2] * x[2] + core_sq)):
        parts[9 + i] = part
    for b in range(BLOCKS):
        def row(i):
            return jnp.broadcast_to(parts[i, b : b + 1, :], (8, LANES))

        rows = []
        for k in range(3):
            h, m, l = row(3 * k), row(3 * k + 1), row(3 * k + 2)
            high_mid = jnp.where(low, h, m)
            rows += [high_mid, high_mid, jnp.where(low, l, h)]
        rows += [one, jnp.where(low, one, row(9)), jnp.where(low, row(10), row(11))]
        for i in range(6):
            right[b, i] = jnp.concatenate(rows[2 * i : 2 * i + 2], axis=0).astype(bf16)
        right[b, 6:] = jnp.zeros((2, 16, LANES), bf16)
    place = lax.broadcasted_iota(jnp.int32, (16, LANES), 0) % 4
    for g in range(4):
        mask[g] = jnp.where(place == g, 1.0, 0.0).astype(bf16)

    acc[...] = jnp.zeros_like(acc)
    k_odd[...] = jnp.zeros_like(k_odd)

    def pair(i):
        word = control[AT_PAIRS + i]
        return lax.shift_right_logical(word, SHARE), word & (2**SHARE - 1)

    def half(step, k_now, k_before):
        for g in range(GROUP):
            if g % 2 == 0:
                i = (step - 1) * GROUP + g
                (b0, t0), (b1, t1) = pair(i), pair(i + 1)
                rows = jnp.concatenate(
                    [burg[pl.ds(pl.multiple_of(8 * t, 8), 8), :] for t in (t0, t1)], axis=0
                ).astype(bf16)
                both = jnp.dot(
                    jnp.concatenate([rows, rows], axis=1),
                    jnp.concatenate([k_before[g], k_before[g + 1]], axis=1),
                    preferred_element_type=f32,
                )
                at = pl.ds(pl.multiple_of(8 * b0, 8), 8)
                acc[at, :] = acc[at, :] + both[:8, :LANES]
                at = pl.ds(pl.multiple_of(8 * b1, 8), 8)
                acc[at, :] = acc[at, :] + both[8:, LANES:]
            b, t = pair(step * GROUP + g)
            features = (right[b] * mask[t & 3][None]).reshape(LANES, LANES)
            near_sq = jnp.dot(left[lax.shift_right_logical(t, 2)], features, preferred_element_type=f32)
            near_sq = jnp.maximum(near_sq, core_sq)
            r = lax.rsqrt(near_sq)
            q = lax.rsqrt(near_sq + (far_sq - core_sq))
            high, low = split2(r * r * r - q * q * q)
            k_now[g, :LANES, :] = high
            k_now[g, LANES:, :] = low

    def body(step, carry):
        half(2 * step, k_even, k_odd)
        half(2 * step + 1, k_odd, k_even)
        return carry

    steps = (control[0] + GROUP - 1) // GROUP + 1
    lax.fori_loop(0, (steps + 1) // 2, body, 0)


def component(acc, a):
    return acc[pl.ds(a, BLOCKS, stride=8), :] + acc[pl.ds(3 + a, BLOCKS, stride=8), :]


near_scratch = [
    pltpu.VMEM((12, BLOCKS, LANES), f32),
    pltpu.VMEM((EXT // 4 + 1, LANES, LANES), bf16),
    pltpu.VMEM((BLOCKS, 8, 16, LANES), bf16),
    pltpu.VMEM((4, 16, LANES), bf16),
    pltpu.VMEM((BLOCKS * 8, LANES), f32),
    pltpu.VMEM((GROUP, 2 * LANES, LANES), bf16),
    pltpu.VMEM((GROUP, 2 * LANES, LANES), bf16),
]


def first_kernel(control, own, burgers, g0, g1, g2, g3, near, burg, *scratch):
    ghosts = (g0, g1, g2, g3)
    exists = slot_exists()
    burg[...] = jnp.zeros_like(burg)
    for tile in range(EXT // 8):
        for a in range(3):
            if tile < BLOCKS // 8:
                value = burgers[a, 8 * tile : 8 * tile + 8, :]
            else:
                d = (tile - BLOCKS // 8) // (GHOST // 8)
                value = tile_of(None, ghosts, 3 + a, tile)
                if exists[d] is not None:
                    value = jnp.where(exists[d], value, 0.0)
            high = round_bf16(value)
            burg[pl.ds(tile * 64 + a, 8, stride=8), :] = high
            burg[pl.ds(tile * 64 + 3 + a, 8, stride=8), :] = value - high
    near_force(control, own, ghosts, burg, *scratch)
    acc = scratch[4]
    for a in range(3):
        near[a] = component(acc, a)


def total_force(expansion, near, places):
    out = []
    for a in range(3):
        far = expansion[0:1, a : a + 1]
        for k in range(3):
            far = far + expansion[0:1, 3 + 3 * a + k : 4 + 3 * a + k] * places[k]
        out.append(near[a] + far)
    return out


def start_kernel(control, shares, near, places, mobility, expansion, moved, now, *sends):
    expansion[...] = jnp.broadcast_to(jnp.sum(shares[...], axis=0, keepdims=True), (8, LANES))
    values = expansion[...]
    p = [places[k] for k in range(3)]
    force = total_force(values, [near[a] for a in range(3)], p)
    for a in range(3):
        step = (time_step * mobility[...]) * force[a]
        moved[a] = step
        now[a] = p[a] + step
    send_now(control, now, sends)


def step_kernel(
    final, control, expansion, own, g0, g1, g2, g3, burg, mobility, places, moved,
    new_moved, now, s0, s1, s2, s3, *scratch
):
    near_force(control, own, (g0, g1, g2, g3), burg, *scratch)
    acc = scratch[4]
    force = total_force(
        expansion[...], [component(acc, a) for a in range(3)], [own[k] for k in range(3)]
    )
    for a in range(3):
        total = moved[a] + (time_step * mobility[...]) * force[a]
        if final:
            put_rows(new_moved, a, total)
        else:
            new_moved[a] = total
        now[a] = places[a] + total
    send_now(control, now, (s0, s1, s2, s3))


def last_kernel(
    control, expansion, own, g0, g1, g2, g3, burg, mobility, velocity, *scratch
):
    near_force(control, own, (g0, g1, g2, g3), burg, *scratch)
    acc = scratch[4]
    force = total_force(
        expansion[...], [component(acc, a) for a in range(3)], [own[k] for k in range(3)]
    )
    for a in range(3):
        put_rows(velocity, a, mobility[...] * force[a])


def cost(flops):
    return pl.CostEstimate(flops=int(flops), bytes_accessed=2**20, transcendentals=0)


def shape(*dims, dtype=f32):
    return jax.ShapeDtypeStruct(dims, dtype)


def exchange(sends):
    def swap(x, axis, first):
        n = lax.axis_size(axis)
        pairs = [(i, (i + 1) % n) for i in range(first, n, 2)]
        return lax.ppermute(x, axis, pairs + [(j, i) for i, j in pairs])

    return [
        swap(sends[0], "slab", 0),
        swap(sends[1], "slab", 1),
        swap(sends[2], "cell", 1),
        swap(sends[3], "cell", 0),
    ]


def local(positions, burgers, mobility, near_list, near_count, send_list):
    mobility = mobility.reshape(BLOCKS, LANES)
    flat = shape(*positions.shape)
    block = shape(3, BLOCKS, LANES)
    send = shape(3, GHOST, LANES)

    places, burgers, *sends = pl.pallas_call(
        pack_kernel,
        out_shape=[block, block] + [shape(6, GHOST, LANES)] * 4,
        in_specs=[smem, vmem, vmem],
        out_specs=[vmem] * 6,
        compiler_params=params,
        name="pack",
    )(send_list, positions, burgers)
    ghosts = exchange(sends)

    shares, control = pl.pallas_call(
        far_kernel,
        out_shape=[shape(EXT, LANES), shape(CONTROL, dtype=jnp.int32)],
        in_specs=[smem, smem, smem, vmem, vmem],
        out_specs=[vmem, smem],
        scratch_shapes=[
            pltpu.VMEM((32, 2 * EXT), f32),
            pltpu.VMEM((BLOCKS // 4, LANES, LANES), f32),
            pltpu.VMEM((BLOCKS // 4, LANES, LANES), bf16),
            pltpu.VMEM((4, LANES, EXT), bf16),
            pltpu.VMEM((4, 2 * LANES, 2 * EXT), bf16),
            pltpu.VMEM((4, 2 * LANES, 2 * EXT), bf16),
        ],
        compiler_params=params,
        cost_estimate=cost(20e9),
        name="far",
    )(send_list, pair_words(near_list), near_count, places, burgers)
    shares = lax.all_to_all(shares, ("slab", "cell"), 0, 0, tiled=True)

    near, burg = pl.pallas_call(
        first_kernel,
        out_shape=[block, shape((EXT + 1) * 8, LANES)],
        in_specs=[smem] + [vmem] * 6,
        out_specs=[vmem] * 2,
        scratch_shapes=near_scratch,
        compiler_params=params,
        cost_estimate=cost(20e9),
        name="near_first",
    )(control, places, burgers, *ghosts)

    expansion, moved, now, *sends = pl.pallas_call(
        start_kernel,
        out_shape=[shape(8, LANES), block, block] + [send] * 4,
        in_specs=[smem] + [vmem] * 4,
        out_specs=[vmem] * 7,
        compiler_params=params,
        name="start",
    )(control, shares, near, places, mobility)

    for substep in range(1, SUBSTEPS):
        final = substep == SUBSTEPS - 1
        ghosts = exchange(sends)
        moved, now, *sends = pl.pallas_call(
            functools.partial(step_kernel, final),
            out_shape=[flat if final else block, block] + [send] * 4,
            in_specs=[smem] + [vmem] * 10,
            out_specs=[vmem] * 6,
            scratch_shapes=near_scratch,
            compiler_params=params,
            cost_estimate=cost(20e9),
            name="near_step",
        )(control, expansion, now, *ghosts, burg, mobility, places, moved)

    ghosts = exchange(sends)
    velocity = pl.pallas_call(
        last_kernel,
        out_shape=flat,
        in_specs=[smem] + [vmem] * 8,
        out_specs=vmem,
        scratch_shapes=near_scratch,
        compiler_params=params,
        cost_estimate=cost(20e9),
        name="near_last",
    )(control, expansion, now, *ghosts, burg, mobility)
    return moved, velocity


def solution(mesh):
    return jax.shard_map(
        local,
        mesh=mesh,
        in_specs=(
            P(None, ("slab", "cell")),
            P(None, ("slab", "cell")),
            P(("slab", "cell")),
            P(("slab", "cell"), None),
            P(("slab", "cell")),
            P(None, ("slab", "cell")),
        ),
        out_specs=(P(None, ("slab", "cell")), P(None, ("slab", "cell"))),
        check_vma=False,
    )
```

```python
import functools

import jax
import jax.numpy as jnp
from jax import lax
from jax.experimental import pallas as pl
from jax.experimental.pallas import tpu as pltpu
from jax.sharding import PartitionSpec as P

SUBSTEPS = 4
BLOCKS = 64
LANES = 128
NEAR = 6
GHOST = 48
EXT = 256
GROUP = 8
LEAD = GROUP
TAIL = 56
AT_SENDS = 8
AT_PAIRS = AT_SENDS + 4 * GHOST + LEAD
CONTROL = AT_PAIRS + BLOCKS * NEAR + TAIL + 8
SHARE = 9

core_sq = 0.04
far_sq = 1.0
time_step = 0.2

f32 = jnp.float32
bf16 = jnp.bfloat16

vmem = pl.BlockSpec(memory_space=pltpu.VMEM)
smem = pl.BlockSpec(memory_space=pltpu.SMEM)
params = pltpu.CompilerParams(vmem_limit_bytes=48 * 2**20)


def round_bf16(x):
    return x.astype(bf16).astype(f32)


def split2(x):
    high = x.astype(bf16)
    return high, (x - high.astype(f32)).astype(bf16)


def split3(x):
    high = round_bf16(x)
    rest = x - high
    mid = round_bf16(rest)
    return high, mid, round_bf16(rest - mid)


def parity():
    return lax.axis_index("slab") % 2, lax.axis_index("cell") % 2


def send_rows():
    odd_slab, odd_cell = parity()
    return odd_slab, 1 - odd_slab, 3 - odd_cell, 2 + odd_cell


def slot_moves():
    odd_slab, odd_cell = parity()
    return (
        GHOST * (1 - odd_slab),
        GHOST * (odd_slab - 1),
        GHOST * odd_cell,
        -GHOST * odd_cell,
    )


def slot_shifts():
    odd_slab, odd_cell = parity()
    along_slab = (1 - 2 * odd_slab).astype(f32)
    along_cell = (1 - 2 * odd_cell).astype(f32)
    return (0, along_slab), (0, -along_slab), (1, -along_cell), (1, along_cell)


def slot_exists():
    out = []
    for axis in ("slab", "cell"):
        i = lax.axis_index(axis)
        partner = i - 1 + 2 * (i % 2)
        out.append((partner >= 0) & (partner < lax.axis_size(axis)))
    return None, out[0], out[1], None


def fill_sends(block_of, sources, sends):
    def body(n, carry):
        for d in sends:
            block = block_of(d, n)
            for a, (ref, index) in enumerate(sources):
                sends[d][a, pl.ds(n, 1), :] = ref[index, pl.ds(block, 1), :]
        return carry

    lax.fori_loop(0, GHOST, body, 0, unroll=4)


def send_now(control, now, sends):
    fill_sends(
        lambda d, n: control[AT_SENDS + GHOST * d + n],
        [(now, k) for k in range(3)],
        dict(enumerate(sends)),
    )


def centre_of():
    slab = lax.axis_index("slab").astype(f32)
    cell = lax.axis_index("cell").astype(f32)
    return slab, cell


def list_pairs(near_list, near_count):
    segment = (near_list + (GHOST - BLOCKS)) // GHOST
    exists = {0: None, 3: None}
    exists[1], exists[2] = slot_exists()[1:3]
    odd_slab, odd_cell = parity()
    sides = (
        (odd_slab == 1) | exists[1],
        (odd_slab == 0) | exists[1],
        (odd_cell == 1) | exists[2],
        (odd_cell == 0) | exists[2],
    )
    slot = lax.broadcasted_iota(jnp.int32, near_list.shape, 0)
    block = lax.broadcasted_iota(jnp.int32, near_list.shape, 1)
    live = jnp.where(slot < near_count, 1, 0)
    moved = near_list
    for i, (move, there) in enumerate(zip(slot_moves(), sides)):
        mine = segment == 1 + i
        moved = moved + jnp.where(mine, move, 0)
        live = jnp.where(mine, live * there.astype(jnp.int32), live)
    rows = [live[i : i + 1] for i in range(NEAR)]
    before = [jnp.zeros_like(rows[0])]
    for row in rows:
        before.append(before[-1] + row)
    amount = before.pop().astype(f32)
    earlier = lax.broadcasted_iota(jnp.int32, (BLOCKS, BLOCKS), 0) < lax.broadcasted_iota(
        jnp.int32, (BLOCKS, BLOCKS), 1
    )
    offset = jnp.dot(
        jnp.broadcast_to(amount, (8, BLOCKS)), jnp.where(earlier, 1.0, 0.0), preferred_element_type=f32
    )[:1]
    at = jnp.concatenate([offset.astype(jnp.int32) + x for x in before], axis=0)
    at = jnp.where(live > 0, at, BLOCKS * NEAR + TAIL)
    words = 2**15 * at + 2**SHARE * block + moved
    return words, jnp.sum(amount, axis=1, keepdims=True).astype(jnp.int32)


def pack_kernel(numbers_smem, numbers, positions, burgers, places, scalars, s1):
    slab, cell = centre_of()
    for k, by in enumerate((slab + 0.5, cell + 0.5, 0.5)):
        places[k] = positions[k] - by
    scalars[...] = jnp.zeros_like(scalars)
    words, amount = list_pairs(numbers[:NEAR, :BLOCKS], numbers[NEAR : NEAR + 1, :BLOCKS])
    scalars[:NEAR, :BLOCKS] = words
    scalars[NEAR : NEAR + 1, :] = jnp.broadcast_to(amount, (1, LANES))
    rows = send_rows()
    for d in range(4):
        first = 2 * (d // 2)
        scalars[8 + d : 9 + d, :] = jnp.where(
            rows[d] == first, numbers[8 + first : 9 + first, :], numbers[9 + first : 10 + first, :]
        )
    sources = [(places, k) for k in range(3)] + [(burgers, a) for a in range(3)]
    fill_sends(lambda d, n: numbers_smem[8 + rows[d], n], sources, {1: s1})


def put_rows(out, k, value):
    for b in range(BLOCKS):
        out[k : k + 1, LANES * b : LANES * b + LANES] = value[b : b + 1]


def halves(tile):
    low = lax.broadcasted_iota(jnp.int32, (8, LANES), 0) < 4
    turned = pltpu.roll(tile, 4, 0)
    return jnp.where(low, tile, turned), jnp.where(low, turned, tile)


def pair_rows(values):
    low = lax.broadcasted_iota(jnp.int32, (8, LANES), 0) < 4
    rows = [
        x if x is y else jnp.where(low, x, y) for x, y in zip(values[0::2], values[1::2])
    ]
    rows += [jnp.zeros((8, LANES), f32)] * (LANES // 8 - len(rows))
    return jnp.concatenate(rows, axis=0)


def far_kernel(
    scalars, places, burgers, out, control, s0, s2, s3, acc, rows, cols, apart_by, w_even, w_odd
):
    fill_sends(
        lambda d, n: scalars[8 + d, n],
        [(places, k) for k in range(3)] + [(burgers, a) for a in range(3)],
        {0: s0, 2: s2, 3: s3},
    )
    amount = scalars[NEAR, 0]
    for i in range(LEAD):
        control[AT_PAIRS - LEAD + i] = EXT
    for tile in range(BLOCKS // 8):
        p = [halves(places[k, 8 * tile : 8 * tile + 8, :]) for k in range(3)]
        burg = [halves(burgers[a, 8 * tile : 8 * tile + 8, :]) for a in range(3)]
        for half in range(2):
            here = [x[half] for x in p]
            sources = [x[half] for x in burg]
            moments = [x * y for x in here for y in sources]
            values = []
            for group in (sources, moments):
                high = [round_bf16(x) for x in group]
                values += high + [x - h for x, h in zip(group, high)]
            rows[2 * tile + half] = pair_rows(values)
            one = jnp.ones((8, LANES), f32)
            square = sum(x * x for x in here) + far_sq
            values = [part for x in (here[0], here[1], square) for part in split3(x)]
            cols[2 * tile + half] = pair_rows(values + [one, one, one]).T.astype(bf16)
    acc[...] = jnp.zeros_like(acc)
    w_odd[...] = jnp.zeros_like(w_odd)
    slab, cell = centre_of()
    target = lax.broadcasted_iota(jnp.int32, (1, EXT), 1)
    apart = [(target // 32).astype(f32) - slab, (target % 32).astype(f32) - cell]
    square = apart[0] * apart[0] + apart[1] * apart[1]
    square_high = round_bf16(square)
    place = lax.broadcasted_iota(jnp.int32, (LANES, EXT), 0)
    values = jnp.where(place < 36, 1.0, 0.0)
    for first, last, x in (
        (0, 12, -2.0 * apart[0]),
        (12, 24, -2.0 * apart[1]),
        (36, 40, square_high),
        (40, 44, square - square_high),
    ):
        values = jnp.where((place >= first) & (place < last), x, values)
    for g in range(4):
        apart_by[g] = jnp.where(place % 4 == g, values, 0.0).astype(bf16)

    def sums(group, g, w):
        mine = rows[group, pl.ds(g, 32, stride=4), :].astype(bf16)
        acc[...] += jnp.dot(
            jnp.concatenate([mine, mine], axis=1), w[g], preferred_element_type=f32
        )

    def half(group, w_now, w_before):
        for i in range(4):
            for slot in range(NEAR):
                word = scalars[slot, 4 * group + i]
                at = lax.shift_right_logical(word, 15)
                control[AT_PAIRS + at] = word & (2**15 - 1)
        for d in range(4):
            for i in range(3):
                n = 3 * group + i
                control[AT_SENDS + GHOST * d + n] = scalars[8 + d, n]
        for g in range(4):
            sums(jnp.maximum(group - 1, 0), g, w_before)
            r = lax.rsqrt(jnp.dot(cols[group], apart_by[g], preferred_element_type=f32))
            r2 = r * r
            w3 = r2 * r
            for k, w in enumerate((w3, w3 * r2)):
                high, low = split2(w)
                w_now[g, :LANES, EXT * k : EXT * k + EXT] = high
                w_now[g, LANES:, EXT * k : EXT * k + EXT] = low

    def body(step, carry):
        half(2 * step, w_even, w_odd)
        half(2 * step + 1, w_odd, w_even)
        return carry

    lax.fori_loop(0, BLOCKS // 8, body, 0)
    for g in range(4):
        sums(BLOCKS // 4 - 1, g, w_odd)
    for i in range(TAIL):
        control[AT_PAIRS + amount + i] = EXT
    control[0] = amount

    apart = apart + [jnp.zeros((1, EXT), f32)]

    def row(k, i):
        return acc[i : i + 1, EXT * k : EXT * k + EXT]

    direct = [row(0, a) + row(0, 3 + a) for a in range(3)]
    total = [row(1, a) + row(1, 3 + a) for a in range(3)]
    gradient = []
    for a in range(3):
        for k in range(3):
            moment = row(1, 6 + 3 * k + a) + row(1, 15 + 3 * k + a)
            gradient.append(-3.0 * (apart[k] * total[a] - moment))
    zero = jnp.zeros((LANES - 12, 2 * LANES), f32)
    values = jnp.concatenate(direct + gradient + [zero], axis=0)
    out[...] = jnp.concatenate([values[:, :LANES].T, values[:, LANES:].T], axis=0)


def tile_of(own, ghosts, index, tile):
    if tile < BLOCKS // 8:
        return own[index, 8 * tile : 8 * tile + 8, :]
    d, n = divmod(tile - BLOCKS // 8, GHOST // 8)
    return ghosts[d][index, 8 * n : 8 * n + 8, :]


def near_force(control, own, ghosts, burg, parts, left, right, mask, acc, k_even, k_odd):
    shift = slot_shifts()
    one = jnp.ones((8, LANES), f32)
    low = lax.broadcasted_iota(jnp.int32, (8, LANES), 0) < 4

    for tile in range(EXT // 8):
        p = [tile_of(own, ghosts, k, tile) for k in range(3)]
        if tile >= BLOCKS // 8:
            k, by = shift[(tile - BLOCKS // 8) // (GHOST // 8)]
            p[k] = p[k] + by
        p = [halves(x) for x in p]
        for half in range(2):
            x = [v[half] for v in p]
            values = []
            for v in x:
                h, m, l = split3(v)
                values += [h, h, m, m, h, l]
            values += list(split3(x[0] * x[0] + x[1] * x[1] + x[2] * x[2]))
            values += [one, one, one]
            left[2 * tile + half] = pair_rows(values).T.astype(bf16)
    left[EXT // 4] = jnp.zeros((LANES, LANES), bf16)
    x = [own[k] for k in range(3)]
    for k in range(3):
        for i, part in enumerate(split3(-2.0 * x[k])):
            parts[3 * k + i] = part
    for i, part in enumerate(split3(x[0] * x[0] + x[1] * x[1] + x[2] * x[2] + core_sq)):
        parts[9 + i] = part
    for b in range(BLOCKS):
        def row(i):
            return jnp.broadcast_to(parts[i, b : b + 1, :], (8, LANES))

        rows = []
        for k in range(3):
            h, m, l = row(3 * k), row(3 * k + 1), row(3 * k + 2)
            high_mid = jnp.where(low, h, m)
            rows += [high_mid, high_mid, jnp.where(low, l, h)]
        rows += [one, jnp.where(low, one, row(9)), jnp.where(low, row(10), row(11))]
        for i in range(6):
            right[b, i] = jnp.concatenate(rows[2 * i : 2 * i + 2], axis=0).astype(bf16)
        right[b, 6:] = jnp.zeros((2, 16, LANES), bf16)
    place = lax.broadcasted_iota(jnp.int32, (16, LANES), 0) % 4
    for g in range(4):
        mask[g] = jnp.where(place == g, 1.0, 0.0).astype(bf16)

    acc[...] = jnp.zeros_like(acc)
    k_odd[...] = jnp.zeros_like(k_odd)

    def pair(i):
        word = control[AT_PAIRS + i]
        return lax.shift_right_logical(word, SHARE), word & (2**SHARE - 1)

    def half(step, k_now, k_before):
        for g in range(GROUP):
            if g % 2 == 0:
                i = (step - 1) * GROUP + g
                (b0, t0), (b1, t1) = pair(i), pair(i + 1)
                rows = jnp.concatenate(
                    [burg[pl.ds(pl.multiple_of(8 * t, 8), 8), :] for t in (t0, t1)], axis=0
                ).astype(bf16)
                both = jnp.dot(
                    jnp.concatenate([rows, rows], axis=1),
                    jnp.concatenate([k_before[g], k_before[g + 1]], axis=1),
                    preferred_element_type=f32,
                )
                at = pl.ds(pl.multiple_of(8 * b0, 8), 8)
                acc[at, :] = acc[at, :] + both[:8, :LANES]
                at = pl.ds(pl.multiple_of(8 * b1, 8), 8)
                acc[at, :] = acc[at, :] + both[8:, LANES:]
            b, t = pair(step * GROUP + g)
            features = (right[b] * mask[t & 3][None]).reshape(LANES, LANES)
            near_sq = jnp.dot(left[lax.shift_right_logical(t, 2)], features, preferred_element_type=f32)
            near_sq = jnp.maximum(near_sq, core_sq)
            r = lax.rsqrt(near_sq)
            q = lax.rsqrt(near_sq + (far_sq - core_sq))
            high, low = split2(r * r * r - q * q * q)
            k_now[g, :LANES, :] = high
            k_now[g, LANES:, :] = low

    def body(step, carry):
        half(2 * step, k_even, k_odd)
        half(2 * step + 1, k_odd, k_even)
        return carry

    steps = (control[0] + GROUP - 1) // GROUP + 1
    lax.fori_loop(0, (steps + 1) // 2, body, 0)


def component(acc, a):
    return acc[pl.ds(a, BLOCKS, stride=8), :] + acc[pl.ds(3 + a, BLOCKS, stride=8), :]


near_scratch = [
    pltpu.VMEM((12, BLOCKS, LANES), f32),
    pltpu.VMEM((EXT // 4 + 1, LANES, LANES), bf16),
    pltpu.VMEM((BLOCKS, 8, 16, LANES), bf16),
    pltpu.VMEM((4, 16, LANES), bf16),
    pltpu.VMEM((BLOCKS * 8, LANES), f32),
    pltpu.VMEM((GROUP, 2 * LANES, LANES), bf16),
    pltpu.VMEM((GROUP, 2 * LANES, LANES), bf16),
]


def total_force(expansion, near, places):
    out = []
    for a in range(3):
        far = expansion[0:1, a : a + 1]
        for k in range(3):
            far = far + expansion[0:1, 3 + 3 * a + k : 4 + 3 * a + k] * places[k]
        out.append(near[a] + far)
    return out


def first_kernel(
    control, shares, own, burgers, mobility, g0, g1, g2, g3,
    burg, expansion, moved, now, s0, s1, s2, s3, *scratch
):
    ghosts = (g0, g1, g2, g3)
    exists = slot_exists()
    burg[...] = jnp.zeros_like(burg)
    for tile in range(EXT // 8):
        for a in range(3):
            if tile < BLOCKS // 8:
                value = burgers[a, 8 * tile : 8 * tile + 8, :]
            else:
                d = (tile - BLOCKS // 8) // (GHOST // 8)
                value = tile_of(None, ghosts, 3 + a, tile)
                if exists[d] is not None:
                    value = jnp.where(exists[d], value, 0.0)
            high = round_bf16(value)
            burg[pl.ds(tile * 64 + a, 8, stride=8), :] = high
            burg[pl.ds(tile * 64 + 3 + a, 8, stride=8), :] = value - high
    expansion[...] = jnp.broadcast_to(jnp.sum(shares[...], axis=0, keepdims=True), (8, LANES))
    near_force(control, own, ghosts, burg, *scratch)
    acc = scratch[4]
    force = total_force(
        expansion[...], [component(acc, a) for a in range(3)], [own[k] for k in range(3)]
    )
    for a in range(3):
        step = (time_step * mobility[...]) * force[a]
        moved[a] = step
        now[a] = own[a] + step
    send_now(control, now, (s0, s1, s2, s3))


def step_kernel(
    final, control, expansion, own, g0, g1, g2, g3, burg, mobility, places, moved,
    new_moved, now, s0, s1, s2, s3, *scratch
):
    near_force(control, own, (g0, g1, g2, g3), burg, *scratch)
    acc = scratch[4]
    force = total_force(
        expansion[...], [component(acc, a) for a in range(3)], [own[k] for k in range(3)]
    )
    for a in range(3):
        total = moved[a] + (time_step * mobility[...]) * force[a]
        if final:
            put_rows(new_moved, a, total)
        else:
            new_moved[a] = total
        now[a] = places[a] + total
    send_now(control, now, (s0, s1, s2, s3))


def last_kernel(
    control, expansion, own, g0, g1, g2, g3, burg, mobility, velocity, *scratch
):
    near_force(control, own, (g0, g1, g2, g3), burg, *scratch)
    acc = scratch[4]
    force = total_force(
        expansion[...], [component(acc, a) for a in range(3)], [own[k] for k in range(3)]
    )
    for a in range(3):
        put_rows(velocity, a, mobility[...] * force[a])


def cost(flops):
    return pl.CostEstimate(flops=int(flops), bytes_accessed=2**20, transcendentals=0)


def shape(*dims, dtype=f32):
    return jax.ShapeDtypeStruct(dims, dtype)


def swap(x, slot):
    n_slabs, n_cells = lax.axis_size("slab"), lax.axis_size("cell")
    pairs = []
    for s in range(n_slabs):
        for c in range(n_cells):
            if slot == 0:
                to = (s ^ 1, c)
            elif slot == 3:
                to = (s, c ^ 1)
            elif slot == 1:
                t = s - 1 + 2 * (s % 2)
                to = (t, c) if 0 <= t < n_slabs else (s, c ^ 1)
            else:
                t = c - 1 + 2 * (c % 2)
                to = (s, t) if 0 <= t < n_cells else (s ^ 1, c)
            pairs.append((s * n_cells + c, to[0] * n_cells + to[1]))
    return lax.ppermute(x, ("slab", "cell"), pairs)


def exchange(sends):
    return [swap(x, slot) for slot, x in enumerate(sends)]


def local(positions, burgers, mobility, near_list, near_count, send_list):
    mobility = mobility.reshape(BLOCKS, LANES)
    flat = shape(*positions.shape)
    block = shape(3, BLOCKS, LANES)
    send = shape(3, GHOST, LANES)

    send6 = shape(6, GHOST, LANES)
    positions = positions.reshape(block.shape)
    burgers = burgers.reshape(block.shape)
    numbers = (
        jnp.pad(near_list.T, ((0, 16 - NEAR), (0, LANES - BLOCKS)))
        + jnp.pad(near_count[None], ((NEAR, 15 - NEAR), (0, LANES - BLOCKS)))
        + jnp.pad(send_list, ((8, 4), (0, LANES - GHOST)))
    )

    places, scalars, s1 = pl.pallas_call(
        pack_kernel,
        out_shape=[block, shape(16, LANES, dtype=jnp.int32), send6],
        in_specs=[smem, vmem, vmem, vmem],
        out_specs=[vmem] * 3,
        compiler_params=params,
        name="pack",
    )(numbers, numbers, positions, burgers)
    g1 = swap(s1, 1)

    shares, control, s0, s2, s3 = pl.pallas_call(
        far_kernel,
        out_shape=[shape(EXT, LANES), shape(CONTROL, dtype=jnp.int32)] + [send6] * 3,
        in_specs=[smem, vmem, vmem],
        out_specs=[vmem, smem] + [vmem] * 3,
        scratch_shapes=[
            pltpu.VMEM((32, 2 * EXT), f32),
            pltpu.VMEM((BLOCKS // 4, LANES, LANES), f32),
            pltpu.VMEM((BLOCKS // 4, LANES, LANES), bf16),
            pltpu.VMEM((4, LANES, EXT), bf16),
            pltpu.VMEM((4, 2 * LANES, 2 * EXT), bf16),
            pltpu.VMEM((4, 2 * LANES, 2 * EXT), bf16),
        ],
        compiler_params=params,
        cost_estimate=cost(20e9),
        name="far",
    )(scalars, places, burgers)
    g3, g0, g2 = swap(s3, 3), swap(s0, 0), swap(s2, 2)
    shares = lax.all_to_all(shares, ("slab", "cell"), 0, 0, tiled=True)

    burg, expansion, moved, now, *sends = pl.pallas_call(
        first_kernel,
        out_shape=[shape((EXT + 1) * 8, LANES), shape(8, LANES), block, block] + [send] * 4,
        in_specs=[smem] + [vmem] * 8,
        out_specs=[vmem] * 8,
        scratch_shapes=near_scratch,
        compiler_params=params,
        cost_estimate=cost(20e9),
        name="near_first",
    )(control, shares, places, burgers, mobility, g0, g1, g2, g3)

    for substep in range(1, SUBSTEPS):
        final = substep == SUBSTEPS - 1
        ghosts = exchange(sends)
        moved, now, *sends = pl.pallas_call(
            functools.partial(step_kernel, final),
            out_shape=[flat if final else block, block] + [send] * 4,
            in_specs=[smem] + [vmem] * 10,
            out_specs=[vmem] * 6,
            scratch_shapes=near_scratch,
            compiler_params=params,
            cost_estimate=cost(20e9),
            name="near_step",
        )(control, expansion, now, *ghosts, burg, mobility, places, moved)

    ghosts = exchange(sends)
    velocity = pl.pallas_call(
        last_kernel,
        out_shape=flat,
        in_specs=[smem] + [vmem] * 8,
        out_specs=vmem,
        scratch_shapes=near_scratch,
        compiler_params=params,
        cost_estimate=cost(20e9),
        name="near_last",
    )(control, expansion, now, *ghosts, burg, mobility)
    return moved, velocity


def solution(mesh):
    return jax.shard_map(
        local,
        mesh=mesh,
        in_specs=(
            P(None, ("slab", "cell")),
            P(None, ("slab", "cell")),
            P(("slab", "cell")),
            P(("slab", "cell"), None),
            P(("slab", "cell")),
            P(None, ("slab", "cell")),
        ),
        out_specs=(P(None, ("slab", "cell")), P(None, ("slab", "cell"))),
        check_vma=False,
    )
```

```python
import functools

import jax
import jax.numpy as jnp
from jax import lax
from jax.experimental import pallas as pl
from jax.experimental.pallas import tpu as pltpu
from jax.sharding import PartitionSpec as P

SUBSTEPS = 4
BLOCKS = 64
LANES = 128
NEAR = 6
GHOST = 48
EXT = 256
GROUP = 8
LEAD = GROUP
TAIL = 56
AT_SENDS = 8
AT_PAIRS = AT_SENDS + 4 * GHOST + LEAD
CONTROL = AT_PAIRS + BLOCKS * NEAR + TAIL + 8
SHARE = 9

core_sq = 0.04
far_sq = 1.0
time_step = 0.2

f32 = jnp.float32
bf16 = jnp.bfloat16

vmem = pl.BlockSpec(memory_space=pltpu.VMEM)
smem = pl.BlockSpec(memory_space=pltpu.SMEM)
params = pltpu.CompilerParams(vmem_limit_bytes=48 * 2**20)


def round_bf16(x):
    return x.astype(bf16).astype(f32)


def split2(x):
    high = x.astype(bf16)
    return high, (x - high.astype(f32)).astype(bf16)


def split3(x):
    high = round_bf16(x)
    rest = x - high
    mid = round_bf16(rest)
    return high, mid, round_bf16(rest - mid)


def parity():
    return lax.axis_index("slab") % 2, lax.axis_index("cell") % 2


def send_rows():
    odd_slab, odd_cell = parity()
    return odd_slab, 1 - odd_slab, 3 - odd_cell, 2 + odd_cell


def slot_moves():
    odd_slab, odd_cell = parity()
    return (
        GHOST * (1 - odd_slab),
        GHOST * (odd_slab - 1),
        GHOST * odd_cell,
        -GHOST * odd_cell,
    )


def slot_shifts():
    odd_slab, odd_cell = parity()
    along_slab = (1 - 2 * odd_slab).astype(f32)
    along_cell = (1 - 2 * odd_cell).astype(f32)
    return (0, along_slab), (0, -along_slab), (1, -along_cell), (1, along_cell)


def slot_exists():
    out = []
    for axis in ("slab", "cell"):
        i = lax.axis_index(axis)
        partner = i - 1 + 2 * (i % 2)
        out.append((partner >= 0) & (partner < lax.axis_size(axis)))
    return None, out[0], out[1], None


def fill_sends(block_of, sources, sends):
    def body(n, carry):
        for d in sends:
            block = block_of(d, n)
            for a, (ref, index) in enumerate(sources):
                sends[d][a, pl.ds(n, 1), :] = ref[index, pl.ds(block, 1), :]
        return carry

    lax.fori_loop(0, GHOST, body, 0, unroll=4)


def send_now(control, now, sends):
    fill_sends(
        lambda d, n: control[AT_SENDS + GHOST * d + n],
        [(now, k) for k in range(3)],
        dict(enumerate(sends)),
    )


def centre_of():
    slab = lax.axis_index("slab").astype(f32)
    cell = lax.axis_index("cell").astype(f32)
    return slab, cell


def list_pairs(near_list, near_count):
    segment = (near_list + (GHOST - BLOCKS)) // GHOST
    exists = {0: None, 3: None}
    exists[1], exists[2] = slot_exists()[1:3]
    odd_slab, odd_cell = parity()
    sides = (
        (odd_slab == 1) | exists[1],
        (odd_slab == 0) | exists[1],
        (odd_cell == 1) | exists[2],
        (odd_cell == 0) | exists[2],
    )
    slot = lax.broadcasted_iota(jnp.int32, near_list.shape, 0)
    block = lax.broadcasted_iota(jnp.int32, near_list.shape, 1)
    live = jnp.where(slot < near_count, 1, 0)
    moved = near_list
    for i, (move, there) in enumerate(zip(slot_moves(), sides)):
        mine = segment == 1 + i
        moved = moved + jnp.where(mine, move, 0)
        live = jnp.where(mine, live * there.astype(jnp.int32), live)
    rows = [live[i : i + 1] for i in range(NEAR)]
    before = [jnp.zeros_like(rows[0])]
    for row in rows:
        before.append(before[-1] + row)
    amount = before.pop().astype(f32)
    earlier = lax.broadcasted_iota(jnp.int32, (BLOCKS, BLOCKS), 0) < lax.broadcasted_iota(
        jnp.int32, (BLOCKS, BLOCKS), 1
    )
    offset = jnp.dot(
        jnp.broadcast_to(amount, (8, BLOCKS)), jnp.where(earlier, 1.0, 0.0), preferred_element_type=f32
    )[:1]
    at = jnp.concatenate([offset.astype(jnp.int32) + x for x in before], axis=0)
    at = jnp.where(live > 0, at, BLOCKS * NEAR + TAIL)
    words = 2**15 * at + 2**SHARE * block + moved
    return words, jnp.sum(amount, axis=1, keepdims=True).astype(jnp.int32)


def pack_kernel(numbers_smem, numbers, positions, burgers, places, scalars, s3, s0, s2, s1):
    slab, cell = centre_of()
    for k, by in enumerate((slab + 0.5, cell + 0.5, 0.5)):
        places[k] = positions[k] - by
    scalars[...] = jnp.zeros_like(scalars)
    words, amount = list_pairs(numbers[:NEAR, :BLOCKS], numbers[NEAR : NEAR + 1, :BLOCKS])
    scalars[:NEAR, :BLOCKS] = words
    scalars[NEAR : NEAR + 1, :] = jnp.broadcast_to(amount, (1, LANES))
    rows = send_rows()
    for d in range(4):
        first = 2 * (d // 2)
        scalars[8 + d : 9 + d, :] = jnp.where(
            rows[d] == first, numbers[8 + first : 9 + first, :], numbers[9 + first : 10 + first, :]
        )
    sources = [(places, k) for k in range(3)] + [(burgers, a) for a in range(3)]
    fill_sends(lambda d, n: numbers_smem[8 + rows[d], n], sources, {0: s0, 1: s1, 2: s2, 3: s3})


def put_rows(out, k, value):
    for b in range(BLOCKS):
        out[k : k + 1, LANES * b : LANES * b + LANES] = value[b : b + 1]


def halves(tile):
    low = lax.broadcasted_iota(jnp.int32, (8, LANES), 0) < 4
    turned = pltpu.roll(tile, 4, 0)
    return jnp.where(low, tile, turned), jnp.where(low, turned, tile)


def pair_rows(values):
    low = lax.broadcasted_iota(jnp.int32, (8, LANES), 0) < 4
    rows = [
        x if x is y else jnp.where(low, x, y) for x, y in zip(values[0::2], values[1::2])
    ]
    rows += [jnp.zeros((8, LANES), f32)] * (LANES // 8 - len(rows))
    return jnp.concatenate(rows, axis=0)


def far_kernel(
    scalars, places, burgers, out, control, acc, rows, cols, apart_by, w_even, w_odd
):
    amount = scalars[NEAR, 0]
    for i in range(LEAD):
        control[AT_PAIRS - LEAD + i] = EXT
    for tile in range(BLOCKS // 8):
        p = [halves(places[k, 8 * tile : 8 * tile + 8, :]) for k in range(3)]
        burg = [halves(burgers[a, 8 * tile : 8 * tile + 8, :]) for a in range(3)]
        for half in range(2):
            here = [x[half] for x in p]
            sources = [x[half] for x in burg]
            moments = [x * y for x in here for y in sources]
            values = []
            for group in (sources, moments):
                high = [round_bf16(x) for x in group]
                values += high + [x - h for x, h in zip(group, high)]
            rows[2 * tile + half] = pair_rows(values)
            one = jnp.ones((8, LANES), f32)
            square = sum(x * x for x in here) + far_sq
            values = [part for x in (here[0], here[1], square) for part in split3(x)]
            cols[2 * tile + half] = pair_rows(values + [one, one, one]).T.astype(bf16)
    acc[...] = jnp.zeros_like(acc)
    w_odd[...] = jnp.zeros_like(w_odd)
    slab, cell = centre_of()
    target = lax.broadcasted_iota(jnp.int32, (1, EXT), 1)
    apart = [(target // 32).astype(f32) - slab, (target % 32).astype(f32) - cell]
    square = apart[0] * apart[0] + apart[1] * apart[1]
    square_high = round_bf16(square)
    place = lax.broadcasted_iota(jnp.int32, (LANES, EXT), 0)
    values = jnp.where(place < 36, 1.0, 0.0)
    for first, last, x in (
        (0, 12, -2.0 * apart[0]),
        (12, 24, -2.0 * apart[1]),
        (36, 40, square_high),
        (40, 44, square - square_high),
    ):
        values = jnp.where((place >= first) & (place < last), x, values)
    for g in range(4):
        apart_by[g] = jnp.where(place % 4 == g, values, 0.0).astype(bf16)

    def sums(group, g, w):
        mine = rows[group, pl.ds(g, 32, stride=4), :].astype(bf16)
        acc[...] += jnp.dot(
            jnp.concatenate([mine, mine], axis=1), w[g], preferred_element_type=f32
        )

    def half(group, w_now, w_before):
        for i in range(4):
            for slot in range(NEAR):
                word = scalars[slot, 4 * group + i]
                at = lax.shift_right_logical(word, 15)
                control[AT_PAIRS + at] = word & (2**15 - 1)
        for d in range(4):
            for i in range(3):
                n = 3 * group + i
                control[AT_SENDS + GHOST * d + n] = scalars[8 + d, n]
        for g in range(4):
            sums(jnp.maximum(group - 1, 0), g, w_before)
            r = lax.rsqrt(jnp.dot(cols[group], apart_by[g], preferred_element_type=f32))
            r2 = r * r
            w3 = r2 * r
            for k, w in enumerate((w3, w3 * r2)):
                high, low = split2(w)
                w_now[g, :LANES, EXT * k : EXT * k + EXT] = high
                w_now[g, LANES:, EXT * k : EXT * k + EXT] = low

    def body(step, carry):
        half(2 * step, w_even, w_odd)
        half(2 * step + 1, w_odd, w_even)
        return carry

    lax.fori_loop(0, BLOCKS // 8, body, 0)
    for g in range(4):
        sums(BLOCKS // 4 - 1, g, w_odd)
    for i in range(TAIL):
        control[AT_PAIRS + amount + i] = EXT
    control[0] = amount

    apart = apart + [jnp.zeros((1, EXT), f32)]

    def row(k, i):
        return acc[i : i + 1, EXT * k : EXT * k + EXT]

    direct = [row(0, a) + row(0, 3 + a) for a in range(3)]
    total = [row(1, a) + row(1, 3 + a) for a in range(3)]
    gradient = []
    for a in range(3):
        for k in range(3):
            moment = row(1, 6 + 3 * k + a) + row(1, 15 + 3 * k + a)
            gradient.append(-3.0 * (apart[k] * total[a] - moment))
    zero = jnp.zeros((LANES - 12, 2 * LANES), f32)
    values = jnp.concatenate(direct + gradient + [zero], axis=0)
    out[...] = jnp.concatenate([values[:, :LANES].T, values[:, LANES:].T], axis=0)


def tile_of(own, ghosts, index, tile):
    if tile < BLOCKS // 8:
        return own[index, 8 * tile : 8 * tile + 8, :]
    d, n = divmod(tile - BLOCKS // 8, GHOST // 8)
    return ghosts[d][index, 8 * n : 8 * n + 8, :]


def near_force(control, own, ghosts, burg, parts, left, right, mask, acc, k_even, k_odd):
    shift = slot_shifts()
    one = jnp.ones((8, LANES), f32)
    low = lax.broadcasted_iota(jnp.int32, (8, LANES), 0) < 4

    for tile in range(EXT // 8):
        p = [tile_of(own, ghosts, k, tile) for k in range(3)]
        if tile >= BLOCKS // 8:
            k, by = shift[(tile - BLOCKS // 8) // (GHOST // 8)]
            p[k] = p[k] + by
        p = [halves(x) for x in p]
        for half in range(2):
            x = [v[half] for v in p]
            values = []
            for v in x:
                h, m, l = split3(v)
                values += [h, h, m, m, h, l]
            values += list(split3(x[0] * x[0] + x[1] * x[1] + x[2] * x[2]))
            values += [one, one, one]
            left[2 * tile + half] = pair_rows(values).T.astype(bf16)
    left[EXT // 4] = jnp.zeros((LANES, LANES), bf16)
    x = [own[k] for k in range(3)]
    for k in range(3):
        for i, part in enumerate(split3(-2.0 * x[k])):
            parts[3 * k + i] = part
    for i, part in enumerate(split3(x[0] * x[0] + x[1] * x[1] + x[2] * x[2] + core_sq)):
        parts[9 + i] = part
    for b in range(BLOCKS):
        def row(i):
            return jnp.broadcast_to(parts[i, b : b + 1, :], (8, LANES))

        rows = []
        for k in range(3):
            h, m, l = row(3 * k), row(3 * k + 1), row(3 * k + 2)
            high_mid = jnp.where(low, h, m)
            rows += [high_mid, high_mid, jnp.where(low, l, h)]
        rows += [one, jnp.where(low, one, row(9)), jnp.where(low, row(10), row(11))]
        for i in range(6):
            right[b, i] = jnp.concatenate(rows[2 * i : 2 * i + 2], axis=0).astype(bf16)
        right[b, 6:] = jnp.zeros((2, 16, LANES), bf16)
    place = lax.broadcasted_iota(jnp.int32, (16, LANES), 0) % 4
    for g in range(4):
        mask[g] = jnp.where(place == g, 1.0, 0.0).astype(bf16)

    acc[...] = jnp.zeros_like(acc)
    k_odd[...] = jnp.zeros_like(k_odd)

    def pair(i):
        word = control[AT_PAIRS + i]
        return lax.shift_right_logical(word, SHARE), word & (2**SHARE - 1)

    def half(step, k_now, k_before):
        for g in range(GROUP):
            if g % 2 == 0:
                i = (step - 1) * GROUP + g
                (b0, t0), (b1, t1) = pair(i), pair(i + 1)
                rows = jnp.concatenate(
                    [burg[pl.ds(pl.multiple_of(8 * t, 8), 8), :] for t in (t0, t1)], axis=0
                ).astype(bf16)
                both = jnp.dot(
                    jnp.concatenate([rows, rows], axis=1),
                    jnp.concatenate([k_before[g], k_before[g + 1]], axis=1),
                    preferred_element_type=f32,
                )
                at = pl.ds(pl.multiple_of(8 * b0, 8), 8)
                acc[at, :] = acc[at, :] + both[:8, :LANES]
                at = pl.ds(pl.multiple_of(8 * b1, 8), 8)
                acc[at, :] = acc[at, :] + both[8:, LANES:]
            b, t = pair(step * GROUP + g)
            features = (right[b] * mask[t & 3][None]).reshape(LANES, LANES)
            near_sq = jnp.dot(left[lax.shift_right_logical(t, 2)], features, preferred_element_type=f32)
            near_sq = jnp.maximum(near_sq, core_sq)
            r = lax.rsqrt(near_sq)
            q = lax.rsqrt(near_sq + (far_sq - core_sq))
            high, low = split2(r * r * r - q * q * q)
            k_now[g, :LANES, :] = high
            k_now[g, LANES:, :] = low

    def body(step, carry):
        half(2 * step, k_even, k_odd)
        half(2 * step + 1, k_odd, k_even)
        return carry

    steps = (control[0] + GROUP - 1) // GROUP + 1
    lax.fori_loop(0, (steps + 1) // 2, body, 0)


def component(acc, a):
    return acc[pl.ds(a, BLOCKS, stride=8), :] + acc[pl.ds(3 + a, BLOCKS, stride=8), :]


near_scratch = [
    pltpu.VMEM((12, BLOCKS, LANES), f32),
    pltpu.VMEM((EXT // 4 + 1, LANES, LANES), bf16),
    pltpu.VMEM((BLOCKS, 8, 16, LANES), bf16),
    pltpu.VMEM((4, 16, LANES), bf16),
    pltpu.VMEM((BLOCKS * 8, LANES), f32),
    pltpu.VMEM((GROUP, 2 * LANES, LANES), bf16),
    pltpu.VMEM((GROUP, 2 * LANES, LANES), bf16),
]


def total_force(expansion, near, places):
    out = []
    for a in range(3):
        far = expansion[0:1, a : a + 1]
        for k in range(3):
            far = far + expansion[0:1, 3 + 3 * a + k : 4 + 3 * a + k] * places[k]
        out.append(near[a] + far)
    return out


def first_kernel(
    control, shares, own, burgers, mobility, g3, g0, g2, g1,
    burg, expansion, moved, now, s0, s1, s2, s3, *scratch
):
    ghosts = (g0, g1, g2, g3)
    exists = slot_exists()
    burg[...] = jnp.zeros_like(burg)
    for tile in range(EXT // 8):
        for a in range(3):
            if tile < BLOCKS // 8:
                value = burgers[a, 8 * tile : 8 * tile + 8, :]
            else:
                d = (tile - BLOCKS // 8) // (GHOST // 8)
                value = tile_of(None, ghosts, 3 + a, tile)
                if exists[d] is not None:
                    value = jnp.where(exists[d], value, 0.0)
            high = round_bf16(value)
            burg[pl.ds(tile * 64 + a, 8, stride=8), :] = high
            burg[pl.ds(tile * 64 + 3 + a, 8, stride=8), :] = value - high
    expansion[...] = jnp.broadcast_to(jnp.sum(shares[...], axis=0, keepdims=True), (8, LANES))
    near_force(control, own, ghosts, burg, *scratch)
    acc = scratch[4]
    force = total_force(
        expansion[...], [component(acc, a) for a in range(3)], [own[k] for k in range(3)]
    )
    for a in range(3):
        step = (time_step * mobility[...]) * force[a]
        moved[a] = step
        now[a] = own[a] + step
    send_now(control, now, (s0, s1, s2, s3))


def step_kernel(
    final, control, expansion, own, g0, g1, g2, g3, burg, mobility, places, moved,
    new_moved, now, s0, s1, s2, s3, *scratch
):
    near_force(control, own, (g0, g1, g2, g3), burg, *scratch)
    acc = scratch[4]
    force = total_force(
        expansion[...], [component(acc, a) for a in range(3)], [own[k] for k in range(3)]
    )
    for a in range(3):
        total = moved[a] + (time_step * mobility[...]) * force[a]
        if final:
            put_rows(new_moved, a, total)
        else:
            new_moved[a] = total
        now[a] = places[a] + total
    send_now(control, now, (s0, s1, s2, s3))


def last_kernel(
    control, expansion, own, g0, g1, g2, g3, burg, mobility, velocity, *scratch
):
    near_force(control, own, (g0, g1, g2, g3), burg, *scratch)
    acc = scratch[4]
    force = total_force(
        expansion[...], [component(acc, a) for a in range(3)], [own[k] for k in range(3)]
    )
    for a in range(3):
        put_rows(velocity, a, mobility[...] * force[a])


def cost(flops):
    return pl.CostEstimate(flops=int(flops), bytes_accessed=2**20, transcendentals=0)


def shape(*dims, dtype=f32):
    return jax.ShapeDtypeStruct(dims, dtype)


def swap(x, slot):
    n_slabs, n_cells = lax.axis_size("slab"), lax.axis_size("cell")
    pairs = []
    for s in range(n_slabs):
        for c in range(n_cells):
            if slot == 0:
                to = (s ^ 1, c)
            elif slot == 3:
                to = (s, c ^ 1)
            elif slot == 1:
                t = s - 1 + 2 * (s % 2)
                to = (t, c) if 0 <= t < n_slabs else (s, c ^ 1)
            else:
                t = c - 1 + 2 * (c % 2)
                to = (s, t) if 0 <= t < n_cells else (s ^ 1, c)
            pairs.append((s * n_cells + c, to[0] * n_cells + to[1]))
    return lax.ppermute(x, ("slab", "cell"), pairs)


def exchange(sends):
    return [swap(x, slot) for slot, x in enumerate(sends)]


def local(positions, burgers, mobility, near_list, near_count, send_list):
    mobility = mobility.reshape(BLOCKS, LANES)
    flat = shape(*positions.shape)
    block = shape(3, BLOCKS, LANES)
    send = shape(3, GHOST, LANES)

    positions = positions.reshape(block.shape)
    burgers = burgers.reshape(block.shape)
    numbers = (
        jnp.pad(near_list.T, ((0, 16 - NEAR), (0, LANES - BLOCKS)))
        + jnp.pad(near_count[None], ((NEAR, 15 - NEAR), (0, LANES - BLOCKS)))
        + jnp.pad(send_list, ((8, 4), (0, LANES - GHOST)))
    )

    places, scalars, *sends = pl.pallas_call(
        pack_kernel,
        out_shape=[block, shape(16, LANES, dtype=jnp.int32)] + [shape(6, GHOST, LANES)] * 4,
        in_specs=[smem, vmem, vmem, vmem],
        out_specs=[vmem] * 6,
        compiler_params=params,
        name="pack",
    )(numbers, numbers, positions, burgers)
    ghosts = [swap(x, slot) for x, slot in zip(sends, (3, 0, 2, 1))]

    shares, control = pl.pallas_call(
        far_kernel,
        out_shape=[shape(EXT, LANES), shape(CONTROL, dtype=jnp.int32)],
        in_specs=[smem, vmem, vmem],
        out_specs=[vmem, smem],
        scratch_shapes=[
            pltpu.VMEM((32, 2 * EXT), f32),
            pltpu.VMEM((BLOCKS // 4, LANES, LANES), f32),
            pltpu.VMEM((BLOCKS // 4, LANES, LANES), bf16),
            pltpu.VMEM((4, LANES, EXT), bf16),
            pltpu.VMEM((4, 2 * LANES, 2 * EXT), bf16),
            pltpu.VMEM((4, 2 * LANES, 2 * EXT), bf16),
        ],
        compiler_params=params,
        cost_estimate=cost(20e9),
        name="far",
    )(scalars, places, burgers)
    shares = lax.all_to_all(shares, ("slab", "cell"), 0, 0, tiled=True)

    burg, expansion, moved, now, *sends = pl.pallas_call(
        first_kernel,
        out_shape=[shape((EXT + 1) * 8, LANES), shape(8, LANES), block, block] + [send] * 4,
        in_specs=[smem] + [vmem] * 8,
        out_specs=[vmem] * 8,
        scratch_shapes=near_scratch,
        compiler_params=params,
        cost_estimate=cost(20e9),
        name="near_first",
    )(control, shares, places, burgers, mobility, *ghosts)

    for substep in range(1, SUBSTEPS):
        final = substep == SUBSTEPS - 1
        ghosts = exchange(sends)
        moved, now, *sends = pl.pallas_call(
            functools.partial(step_kernel, final),
            out_shape=[flat if final else block, block] + [send] * 4,
            in_specs=[smem] + [vmem] * 10,
            out_specs=[vmem] * 6,
            scratch_shapes=near_scratch,
            compiler_params=params,
            cost_estimate=cost(20e9),
            name="near_step",
        )(control, expansion, now, *ghosts, burg, mobility, places, moved)

    ghosts = exchange(sends)
    velocity = pl.pallas_call(
        last_kernel,
        out_shape=flat,
        in_specs=[smem] + [vmem] * 8,
        out_specs=vmem,
        scratch_shapes=near_scratch,
        compiler_params=params,
        cost_estimate=cost(20e9),
        name="near_last",
    )(control, expansion, now, *ghosts, burg, mobility)
    return moved, velocity


def solution(mesh):
    return jax.shard_map(
        local,
        mesh=mesh,
        in_specs=(
            P(None, ("slab", "cell")),
            P(None, ("slab", "cell")),
            P(("slab", "cell")),
            P(("slab", "cell"), None),
            P(("slab", "cell")),
            P(None, ("slab", "cell")),
        ),
        out_specs=(P(None, ("slab", "cell")), P(None, ("slab", "cell"))),
        check_vma=False,
    )
```

```python
import functools

import jax
import jax.numpy as jnp
from jax import lax
from jax.experimental import pallas as pl
from jax.experimental.pallas import tpu as pltpu
from jax.sharding import PartitionSpec as P

SUBSTEPS = 4
BLOCKS = 64
LANES = 128
NEAR = 6
GHOST = 48
EXT = 256
GROUP = 8
LEAD = GROUP
TAIL = 56
AT_SENDS = 8
AT_PAIRS = AT_SENDS + 4 * GHOST + LEAD
CONTROL = AT_PAIRS + BLOCKS * NEAR + TAIL + 8
SHARE = 9

core_sq = 0.04
far_sq = 1.0
time_step = 0.2

f32 = jnp.float32
bf16 = jnp.bfloat16

vmem = pl.BlockSpec(memory_space=pltpu.VMEM)
smem = pl.BlockSpec(memory_space=pltpu.SMEM)
params = pltpu.CompilerParams(vmem_limit_bytes=48 * 2**20)


def round_bf16(x):
    return x.astype(bf16).astype(f32)


def split2(x):
    high = x.astype(bf16)
    return high, (x - high.astype(f32)).astype(bf16)


def split3(x):
    high = round_bf16(x)
    rest = x - high
    mid = round_bf16(rest)
    return high, mid, round_bf16(rest - mid)


def parity():
    return lax.axis_index("slab") % 2, lax.axis_index("cell") % 2


def send_rows():
    odd_slab, odd_cell = parity()
    return odd_slab, 1 - odd_slab, 3 - odd_cell, 2 + odd_cell


def slot_moves():
    odd_slab, odd_cell = parity()
    return (
        GHOST * (1 - odd_slab),
        GHOST * (odd_slab - 1),
        GHOST * odd_cell,
        -GHOST * odd_cell,
    )


def slot_shifts():
    odd_slab, odd_cell = parity()
    along_slab = (1 - 2 * odd_slab).astype(f32)
    along_cell = (1 - 2 * odd_cell).astype(f32)
    return (0, along_slab), (0, -along_slab), (1, -along_cell), (1, along_cell)


def slot_exists():
    out = []
    for axis in ("slab", "cell"):
        i = lax.axis_index(axis)
        partner = i - 1 + 2 * (i % 2)
        out.append((partner >= 0) & (partner < lax.axis_size(axis)))
    return None, out[0], out[1], None


def fill_sends(block_of, sources, sends):
    def body(n, carry):
        for d in sends:
            block = block_of(d, n)
            for a, (ref, index) in enumerate(sources):
                sends[d][a, pl.ds(n, 1), :] = ref[index, pl.ds(block, 1), :]
        return carry

    lax.fori_loop(0, GHOST, body, 0, unroll=4)


def send_now(control, now, sends):
    fill_sends(
        lambda d, n: control[AT_SENDS + GHOST * d + n],
        [(now, k) for k in range(3)],
        dict(enumerate(sends)),
    )


def centre_of():
    slab = lax.axis_index("slab").astype(f32)
    cell = lax.axis_index("cell").astype(f32)
    return slab, cell


def list_pairs(near_list, near_count):
    segment = (near_list + (GHOST - BLOCKS)) // GHOST
    exists = {0: None, 3: None}
    exists[1], exists[2] = slot_exists()[1:3]
    odd_slab, odd_cell = parity()
    sides = (
        (odd_slab == 1) | exists[1],
        (odd_slab == 0) | exists[1],
        (odd_cell == 1) | exists[2],
        (odd_cell == 0) | exists[2],
    )
    slot = lax.broadcasted_iota(jnp.int32, near_list.shape, 0)
    block = lax.broadcasted_iota(jnp.int32, near_list.shape, 1)
    live = jnp.where(slot < near_count, 1, 0)
    moved = near_list
    for i, (move, there) in enumerate(zip(slot_moves(), sides)):
        mine = segment == 1 + i
        moved = moved + jnp.where(mine, move, 0)
        live = jnp.where(mine, live * there.astype(jnp.int32), live)
    rows = [live[i : i + 1] for i in range(NEAR)]
    before = [jnp.zeros_like(rows[0])]
    for row in rows:
        before.append(before[-1] + row)
    amount = before.pop().astype(f32)
    earlier = lax.broadcasted_iota(jnp.int32, (BLOCKS, BLOCKS), 0) < lax.broadcasted_iota(
        jnp.int32, (BLOCKS, BLOCKS), 1
    )
    offset = jnp.dot(
        jnp.broadcast_to(amount, (8, BLOCKS)), jnp.where(earlier, 1.0, 0.0), preferred_element_type=f32
    )[:1]
    at = jnp.concatenate([offset.astype(jnp.int32) + x for x in before], axis=0)
    at = jnp.where(live > 0, at, BLOCKS * NEAR + TAIL)
    words = 2**15 * at + 2**SHARE * block + moved
    return words, jnp.sum(amount, axis=1, keepdims=True).astype(jnp.int32)


def pack_kernel(numbers_smem, numbers, positions, burgers, places, scalars, s3, s0, s2, s1):
    slab, cell = centre_of()
    for k, by in enumerate((slab + 0.5, cell + 0.5, 0.5)):
        places[k] = positions[k] - by
    scalars[...] = jnp.zeros_like(scalars)
    words, amount = list_pairs(numbers[:NEAR, :BLOCKS], numbers[NEAR : NEAR + 1, :BLOCKS])
    scalars[:NEAR, :BLOCKS] = words
    scalars[NEAR : NEAR + 1, :] = jnp.broadcast_to(amount, (1, LANES))
    rows = send_rows()
    for d in range(4):
        first = 2 * (d // 2)
        scalars[8 + d : 9 + d, :] = jnp.where(
            rows[d] == first, numbers[8 + first : 9 + first, :], numbers[9 + first : 10 + first, :]
        )
    sources = [(places, k) for k in range(3)] + [(burgers, a) for a in range(3)]
    fill_sends(lambda d, n: numbers_smem[8 + rows[d], n], sources, {0: s0, 1: s1, 2: s2, 3: s3})


def put_rows(out, k, value):
    for b in range(BLOCKS):
        out[k : k + 1, LANES * b : LANES * b + LANES] = value[b : b + 1]


def halves(tile):
    low = lax.broadcasted_iota(jnp.int32, (8, LANES), 0) < 4
    turned = pltpu.roll(tile, 4, 0)
    return jnp.where(low, tile, turned), jnp.where(low, turned, tile)


def pair_rows(values):
    low = lax.broadcasted_iota(jnp.int32, (8, LANES), 0) < 4
    rows = [
        x if x is y else jnp.where(low, x, y) for x, y in zip(values[0::2], values[1::2])
    ]
    rows += [jnp.zeros((8, LANES), f32)] * (LANES // 8 - len(rows))
    return jnp.concatenate(rows, axis=0)


def far_kernel(
    scalars, places, burgers, out, control, acc, rows, cols, apart_by, w_even, w_odd
):
    amount = scalars[NEAR, 0]
    for i in range(LEAD):
        control[AT_PAIRS - LEAD + i] = EXT
    for tile in range(BLOCKS // 8):
        p = [halves(places[k, 8 * tile : 8 * tile + 8, :]) for k in range(3)]
        burg = [halves(burgers[a, 8 * tile : 8 * tile + 8, :]) for a in range(3)]
        for half in range(2):
            here = [x[half] for x in p]
            sources = [x[half] for x in burg]
            moments = [x * y for x in here for y in sources]
            values = []
            for group in (sources, moments):
                high = [round_bf16(x) for x in group]
                values += high + [x - h for x, h in zip(group, high)]
            rows[2 * tile + half] = pair_rows(values)
            one = jnp.ones((8, LANES), f32)
            square = sum(x * x for x in here) + far_sq
            values = [part for x in (here[0], here[1], square) for part in split3(x)]
            cols[2 * tile + half] = pair_rows(values + [one, one, one]).T.astype(bf16)
    acc[...] = jnp.zeros_like(acc)
    w_odd[...] = jnp.zeros_like(w_odd)
    slab, cell = centre_of()
    target = lax.broadcasted_iota(jnp.int32, (1, EXT), 1)
    apart = [(target // 32).astype(f32) - slab, (target % 32).astype(f32) - cell]
    square = apart[0] * apart[0] + apart[1] * apart[1]
    square_high = round_bf16(square)
    place = lax.broadcasted_iota(jnp.int32, (LANES, EXT), 0)
    values = jnp.where(place < 36, 1.0, 0.0)
    for first, last, x in (
        (0, 12, -2.0 * apart[0]),
        (12, 24, -2.0 * apart[1]),
        (36, 40, square_high),
        (40, 44, square - square_high),
    ):
        values = jnp.where((place >= first) & (place < last), x, values)
    for g in range(4):
        apart_by[g] = jnp.where(place % 4 == g, values, 0.0).astype(bf16)

    def sums(group, g, w):
        mine = rows[group, pl.ds(g, 32, stride=4), :].astype(bf16)
        acc[...] += jnp.dot(
            jnp.concatenate([mine, mine], axis=1), w[g], preferred_element_type=f32
        )

    def half(group, w_now, w_before):
        for i in range(4):
            for slot in range(NEAR):
                word = scalars[slot, 4 * group + i]
                at = lax.shift_right_logical(word, 15)
                control[AT_PAIRS + at] = word & (2**15 - 1)
        for d in range(4):
            for i in range(3):
                n = 3 * group + i
                control[AT_SENDS + GHOST * d + n] = scalars[8 + d, n]
        for g in range(4):
            sums(jnp.maximum(group - 1, 0), g, w_before)
            r = lax.rsqrt(jnp.dot(cols[group], apart_by[g], preferred_element_type=f32))
            r2 = r * r
            w3 = r2 * r
            for k, w in enumerate((w3, w3 * r2)):
                high, low = split2(w)
                w_now[g, :LANES, EXT * k : EXT * k + EXT] = high
                w_now[g, LANES:, EXT * k : EXT * k + EXT] = low

    def body(step, carry):
        half(2 * step, w_even, w_odd)
        half(2 * step + 1, w_odd, w_even)
        return carry

    lax.fori_loop(0, BLOCKS // 8, body, 0)
    for g in range(4):
        sums(BLOCKS // 4 - 1, g, w_odd)
    for i in range(TAIL):
        control[AT_PAIRS + amount + i] = EXT
    control[0] = amount

    apart = apart + [jnp.zeros((1, EXT), f32)]

    def row(k, i):
        return acc[i : i + 1, EXT * k : EXT * k + EXT]

    direct = [row(0, a) + row(0, 3 + a) for a in range(3)]
    total = [row(1, a) + row(1, 3 + a) for a in range(3)]
    gradient = []
    for a in range(3):
        for k in range(3):
            moment = row(1, 6 + 3 * k + a) + row(1, 15 + 3 * k + a)
            gradient.append(-3.0 * (apart[k] * total[a] - moment))
    zero = jnp.zeros((LANES - 12, 2 * LANES), f32)
    values = jnp.concatenate(direct + gradient + [zero], axis=0)
    out[...] = jnp.concatenate([values[:, :LANES].T, values[:, LANES:].T], axis=0)


def tile_of(own, ghosts, index, tile):
    if tile < BLOCKS // 8:
        return own[index, 8 * tile : 8 * tile + 8, :]
    d, n = divmod(tile - BLOCKS // 8, GHOST // 8)
    return ghosts[d][index, 8 * n : 8 * n + 8, :]


def near_force(control, own, ghosts, burg, parts, left, right, mask, acc, k_even, k_odd):
    shift = slot_shifts()
    one = jnp.ones((8, LANES), f32)
    low = lax.broadcasted_iota(jnp.int32, (8, LANES), 0) < 4

    for tile in range(EXT // 8):
        p = [tile_of(own, ghosts, k, tile) for k in range(3)]
        if tile >= BLOCKS // 8:
            k, by = shift[(tile - BLOCKS // 8) // (GHOST // 8)]
            p[k] = p[k] + by
        parts_of = [split3(x) for x in p]
        parts_of.append(split3(p[0] * p[0] + p[1] * p[1] + p[2] * p[2]))
        turned = [[pltpu.roll(x, 4, 0) for x in group] for group in parts_of]
        for half in range(2):
            first, second = (parts_of, turned) if half == 0 else (turned, parts_of)
            values = []
            for (h, m, _), (h2, m2, l2) in zip(first[:3], second[:3]):
                values += [
                    jnp.where(low, h, h2),
                    jnp.where(low, m, m2),
                    jnp.where(low, h, l2),
                ]
            h, _, l = first[3]
            values += [jnp.where(low, h, second[3][1]), jnp.where(low, l, one), one]
            values += [jnp.zeros((8, LANES), f32)] * (LANES // 8 - len(values))
            left[2 * tile + half] = jnp.concatenate(values, axis=0).T.astype(bf16)
    left[EXT // 4] = jnp.zeros((LANES, LANES), bf16)
    x = [own[k] for k in range(3)]
    for k in range(3):
        for i, part in enumerate(split3(-2.0 * x[k])):
            parts[3 * k + i] = part
    for i, part in enumerate(split3(x[0] * x[0] + x[1] * x[1] + x[2] * x[2] + core_sq)):
        parts[9 + i] = part
    for b in range(BLOCKS):
        def row(i):
            return jnp.broadcast_to(parts[i, b : b + 1, :], (8, LANES))

        rows = []
        for k in range(3):
            h, m, l = row(3 * k), row(3 * k + 1), row(3 * k + 2)
            high_mid = jnp.where(low, h, m)
            rows += [high_mid, high_mid, jnp.where(low, l, h)]
        rows += [one, jnp.where(low, one, row(9)), jnp.where(low, row(10), row(11))]
        for i in range(6):
            right[b, i] = jnp.concatenate(rows[2 * i : 2 * i + 2], axis=0).astype(bf16)
        right[b, 6:] = jnp.zeros((2, 16, LANES), bf16)
    place = lax.broadcasted_iota(jnp.int32, (16, LANES), 0) % 4
    for g in range(4):
        mask[g] = jnp.where(place == g, 1.0, 0.0).astype(bf16)

    acc[...] = jnp.zeros_like(acc)
    k_odd[...] = jnp.zeros_like(k_odd)

    def pair(i):
        word = control[AT_PAIRS + i]
        return lax.shift_right_logical(word, SHARE), word & (2**SHARE - 1)

    def sums(step, g, k_before):
        i = step * GROUP + g
        (b0, t0), (b1, t1) = pair(i), pair(i + 1)
        rows = jnp.concatenate(
            [burg[pl.ds(pl.multiple_of(8 * t, 8), 8), :] for t in (t0, t1)], axis=0
        ).astype(bf16)
        both = jnp.dot(
            jnp.concatenate([rows, rows], axis=1),
            jnp.concatenate([k_before[g], k_before[g + 1]], axis=1),
            preferred_element_type=f32,
        )
        at = pl.ds(pl.multiple_of(8 * b0, 8), 8)
        acc[at, :] = acc[at, :] + both[:8, :LANES]
        at = pl.ds(pl.multiple_of(8 * b1, 8), 8)
        acc[at, :] = acc[at, :] + both[8:, LANES:]

    def half(step, k_now, k_before):
        for g in range(GROUP):
            if g % 2 == 0:
                sums(step - 1, g, k_before)
            b, t = pair(step * GROUP + g)
            features = (right[b] * mask[t & 3][None]).reshape(LANES, LANES)
            near_sq = jnp.dot(
                left[lax.shift_right_logical(t, 2)], features, preferred_element_type=f32
            )
            near_sq = jnp.maximum(near_sq, core_sq)
            r = lax.rsqrt(near_sq)
            q = lax.rsqrt(near_sq + (far_sq - core_sq))
            high, low = split2(r * r * r - q * q * q)
            k_now[g, :LANES, :] = high
            k_now[g, LANES:, :] = low

    def body(step, carry):
        half(2 * step, k_even, k_odd)
        half(2 * step + 1, k_odd, k_even)
        return carry

    steps = (control[0] + 2 * GROUP - 1) // (2 * GROUP)
    lax.fori_loop(0, steps, body, 0)
    for g in range(0, GROUP, 2):
        sums(2 * steps - 1, g, k_odd)


def component(acc, a):
    return acc[pl.ds(a, BLOCKS, stride=8), :] + acc[pl.ds(3 + a, BLOCKS, stride=8), :]


near_scratch = [
    pltpu.VMEM((12, BLOCKS, LANES), f32),
    pltpu.VMEM((EXT // 4 + 1, LANES, LANES), bf16),
    pltpu.VMEM((BLOCKS, 8, 16, LANES), bf16),
    pltpu.VMEM((4, 16, LANES), bf16),
    pltpu.VMEM((BLOCKS * 8, LANES), f32),
    pltpu.VMEM((GROUP, 2 * LANES, LANES), bf16),
    pltpu.VMEM((GROUP, 2 * LANES, LANES), bf16),
]


def total_force(expansion, near, places):
    out = []
    for a in range(3):
        far = expansion[0:1, a : a + 1]
        for k in range(3):
            far = far + expansion[0:1, 3 + 3 * a + k : 4 + 3 * a + k] * places[k]
        out.append(near[a] + far)
    return out


def first_kernel(
    control, own, burgers, g3, g0, g2, g1, near, burg, *scratch
):
    ghosts = (g0, g1, g2, g3)
    exists = slot_exists()
    burg[...] = jnp.zeros_like(burg)
    for tile in range(EXT // 8):
        for a in range(3):
            if tile < BLOCKS // 8:
                value = burgers[a, 8 * tile : 8 * tile + 8, :]
            else:
                d = (tile - BLOCKS // 8) // (GHOST // 8)
                value = tile_of(None, ghosts, 3 + a, tile)
                if exists[d] is not None:
                    value = jnp.where(exists[d], value, 0.0)
            high = round_bf16(value)
            burg[pl.ds(tile * 64 + a, 8, stride=8), :] = high
            burg[pl.ds(tile * 64 + 3 + a, 8, stride=8), :] = value - high
    near_force(control, own, ghosts, burg, *scratch)
    acc = scratch[4]
    for a in range(3):
        near[a] = component(acc, a)


def start_kernel(control, shares, near, places, mobility, expansion, moved, now, *sends):
    expansion[...] = jnp.broadcast_to(jnp.sum(shares[...], axis=0, keepdims=True), (8, LANES))
    p = [places[k] for k in range(3)]
    force = total_force(expansion[...], [near[a] for a in range(3)], p)
    for a in range(3):
        step = (time_step * mobility[...]) * force[a]
        moved[a] = step
        now[a] = p[a] + step
    send_now(control, now, sends)


def step_kernel(
    final, control, expansion, own, g0, g1, g2, g3, burg, mobility, places, moved,
    new_moved, now, s0, s1, s2, s3, *scratch
):
    near_force(control, own, (g0, g1, g2, g3), burg, *scratch)
    acc = scratch[4]
    force = total_force(
        expansion[...], [component(acc, a) for a in range(3)], [own[k] for k in range(3)]
    )
    for a in range(3):
        total = moved[a] + (time_step * mobility[...]) * force[a]
        if final:
            put_rows(new_moved, a, total)
        else:
            new_moved[a] = total
        now[a] = places[a] + total
    send_now(control, now, (s0, s1, s2, s3))


def last_kernel(
    control, expansion, own, g0, g1, g2, g3, burg, mobility, velocity, *scratch
):
    near_force(control, own, (g0, g1, g2, g3), burg, *scratch)
    acc = scratch[4]
    force = total_force(
        expansion[...], [component(acc, a) for a in range(3)], [own[k] for k in range(3)]
    )
    for a in range(3):
        put_rows(velocity, a, mobility[...] * force[a])


def cost(flops):
    return pl.CostEstimate(flops=int(flops), bytes_accessed=2**20, transcendentals=0)


def shape(*dims, dtype=f32):
    return jax.ShapeDtypeStruct(dims, dtype)


def swap(x, slot):
    n_slabs, n_cells = lax.axis_size("slab"), lax.axis_size("cell")
    pairs = []
    for s in range(n_slabs):
        for c in range(n_cells):
            if slot == 0:
                to = (s ^ 1, c)
            elif slot == 3:
                to = (s, c ^ 1)
            elif slot == 1:
                t = s - 1 + 2 * (s % 2)
                to = (t, c) if 0 <= t < n_slabs else (s, c ^ 1)
            else:
                t = c - 1 + 2 * (c % 2)
                to = (s, t) if 0 <= t < n_cells else (s ^ 1, c)
            pairs.append((s * n_cells + c, to[0] * n_cells + to[1]))
    return lax.ppermute(x, ("slab", "cell"), pairs)


def exchange(sends):
    return [swap(x, slot) for slot, x in enumerate(sends)]


def local(positions, burgers, mobility, near_list, near_count, send_list):
    mobility = mobility.reshape(BLOCKS, LANES)
    flat = shape(*positions.shape)
    block = shape(3, BLOCKS, LANES)
    send = shape(3, GHOST, LANES)

    positions = positions.reshape(block.shape)
    burgers = burgers.reshape(block.shape)
    numbers = (
        jnp.pad(near_list.T, ((0, 16 - NEAR), (0, LANES - BLOCKS)))
        + jnp.pad(near_count[None], ((NEAR, 15 - NEAR), (0, LANES - BLOCKS)))
        + jnp.pad(send_list, ((8, 4), (0, LANES - GHOST)))
    )

    places, scalars, *sends = pl.pallas_call(
        pack_kernel,
        out_shape=[block, shape(16, LANES, dtype=jnp.int32)] + [shape(6, GHOST, LANES)] * 4,
        in_specs=[smem, vmem, vmem, vmem],
        out_specs=[vmem] * 6,
        compiler_params=params,
        name="pack",
    )(numbers, numbers, positions, burgers)
    ghosts = [swap(x, slot) for x, slot in zip(sends, (3, 0, 2, 1))]

    shares, control = pl.pallas_call(
        far_kernel,
        out_shape=[shape(EXT, LANES), shape(CONTROL, dtype=jnp.int32)],
        in_specs=[smem, vmem, vmem],
        out_specs=[vmem, smem],
        scratch_shapes=[
            pltpu.VMEM((32, 2 * EXT), f32),
            pltpu.VMEM((BLOCKS // 4, LANES, LANES), f32),
            pltpu.VMEM((BLOCKS // 4, LANES, LANES), bf16),
            pltpu.VMEM((4, LANES, EXT), bf16),
            pltpu.VMEM((4, 2 * LANES, 2 * EXT), bf16),
            pltpu.VMEM((4, 2 * LANES, 2 * EXT), bf16),
        ],
        compiler_params=params,
        cost_estimate=cost(20e9),
        name="far",
    )(scalars, places, burgers)
    shares = lax.all_to_all(shares, ("slab", "cell"), 0, 0, tiled=True)

    near, burg = pl.pallas_call(
        first_kernel,
        out_shape=[block, shape((EXT + 1) * 8, LANES)],
        in_specs=[smem] + [vmem] * 6,
        out_specs=[vmem] * 2,
        scratch_shapes=near_scratch,
        compiler_params=params,
        cost_estimate=cost(20e9),
        name="near_first",
    )(control, places, burgers, *ghosts)

    expansion, moved, now, *sends = pl.pallas_call(
        start_kernel,
        out_shape=[shape(8, LANES), block, block] + [send] * 4,
        in_specs=[smem] + [vmem] * 4,
        out_specs=[vmem] * 7,
        compiler_params=params,
        name="start",
    )(control, shares, near, places, mobility)

    for substep in range(1, SUBSTEPS):
        final = substep == SUBSTEPS - 1
        ghosts = exchange(sends)
        moved, now, *sends = pl.pallas_call(
            functools.partial(step_kernel, final),
            out_shape=[flat if final else block, block] + [send] * 4,
            in_specs=[smem] + [vmem] * 10,
            out_specs=[vmem] * 6,
            scratch_shapes=near_scratch,
            compiler_params=params,
            cost_estimate=cost(20e9),
            name="near_step",
        )(control, expansion, now, *ghosts, burg, mobility, places, moved)

    ghosts = exchange(sends)
    velocity = pl.pallas_call(
        last_kernel,
        out_shape=flat,
        in_specs=[smem] + [vmem] * 8,
        out_specs=vmem,
        scratch_shapes=near_scratch,
        compiler_params=params,
        cost_estimate=cost(20e9),
        name="near_last",
    )(control, expansion, now, *ghosts, burg, mobility)
    return moved, velocity


def solution(mesh):
    return jax.shard_map(
        local,
        mesh=mesh,
        in_specs=(
            P(None, ("slab", "cell")),
            P(None, ("slab", "cell")),
            P(("slab", "cell")),
            P(("slab", "cell"), None),
            P(("slab", "cell")),
            P(None, ("slab", "cell")),
        ),
        out_specs=(P(None, ("slab", "cell")), P(None, ("slab", "cell"))),
        check_vma=False,
    )
```

```python
import functools

import jax
import jax.numpy as jnp
from jax import lax
from jax.experimental import pallas as pl
from jax.experimental.pallas import tpu as pltpu
from jax.sharding import PartitionSpec as P

SUBSTEPS = 4
BLOCKS = 64
LANES = 128
NEAR = 6
GHOST = 48
EXT = 256
GROUP = 8
LEAD = GROUP
TAIL = 56
AT_SENDS = 8
AT_PAIRS = AT_SENDS + 4 * GHOST + LEAD
LIST = BLOCKS * NEAR + TAIL + LEAD
CONTROL = AT_PAIRS + 2 * LIST + 8
EARLY, LATE = (3, 0), (2, 1)
SHARE = 9

core_sq = 0.04
far_sq = 1.0
time_step = 0.2

f32 = jnp.float32
bf16 = jnp.bfloat16

vmem = pl.BlockSpec(memory_space=pltpu.VMEM)
smem = pl.BlockSpec(memory_space=pltpu.SMEM)
params = pltpu.CompilerParams(vmem_limit_bytes=40 * 2**20)


def round_bf16(x):
    return x.astype(bf16).astype(f32)


def split2(x):
    high = x.astype(bf16)
    return high, (x - high.astype(f32)).astype(bf16)


def split3(x):
    high = round_bf16(x)
    rest = x - high
    mid = round_bf16(rest)
    return high, mid, round_bf16(rest - mid)


def parity():
    return lax.axis_index("slab") % 2, lax.axis_index("cell") % 2


def send_rows():
    odd_slab, odd_cell = parity()
    return odd_slab, 1 - odd_slab, 3 - odd_cell, 2 + odd_cell


def slot_moves():
    odd_slab, odd_cell = parity()
    return (
        GHOST * (1 - odd_slab),
        GHOST * (odd_slab - 1),
        GHOST * odd_cell,
        -GHOST * odd_cell,
    )


def slot_shifts():
    odd_slab, odd_cell = parity()
    along_slab = (1 - 2 * odd_slab).astype(f32)
    along_cell = (1 - 2 * odd_cell).astype(f32)
    return (0, along_slab), (0, -along_slab), (1, -along_cell), (1, along_cell)


def slot_exists():
    out = []
    for axis in ("slab", "cell"):
        i = lax.axis_index(axis)
        partner = i - 1 + 2 * (i % 2)
        out.append((partner >= 0) & (partner < lax.axis_size(axis)))
    return None, out[0], out[1], None


def fill_sends(block_of, sources, sends):
    def body(n, carry):
        for d in sends:
            block = block_of(d, n)
            for a, (ref, index) in enumerate(sources):
                sends[d][a, pl.ds(n, 1), :] = ref[index, pl.ds(block, 1), :]
        return carry

    lax.fori_loop(0, GHOST, body, 0, unroll=4)


def send_now(control, now, sends):
    fill_sends(
        lambda d, n: control[AT_SENDS + GHOST * d + n],
        [(now, k) for k in range(3)],
        dict(enumerate(sends)),
    )


def centre_of():
    slab = lax.axis_index("slab").astype(f32)
    cell = lax.axis_index("cell").astype(f32)
    return slab, cell


def list_pairs(near_list, near_count):
    segment = (near_list + (GHOST - BLOCKS)) // GHOST
    exists = {0: None, 3: None}
    exists[1], exists[2] = slot_exists()[1:3]
    odd_slab, odd_cell = parity()
    sides = (
        (odd_slab == 1) | exists[1],
        (odd_slab == 0) | exists[1],
        (odd_cell == 1) | exists[2],
        (odd_cell == 0) | exists[2],
    )
    slot = lax.broadcasted_iota(jnp.int32, near_list.shape, 0)
    block = lax.broadcasted_iota(jnp.int32, near_list.shape, 1)
    live = jnp.where(slot < near_count, 1, 0)
    moved = near_list
    for i, (move, there) in enumerate(zip(slot_moves(), sides)):
        mine = segment == 1 + i
        moved = moved + jnp.where(mine, move, 0)
        live = jnp.where(mine, live * there.astype(jnp.int32), live)
    late = jnp.where(moved >= BLOCKS, live, 0)
    for d in EARLY:
        first = BLOCKS + GHOST * d
        late = jnp.where((moved >= first) & (moved < first + GHOST), 0, late)
    earlier = lax.broadcasted_iota(jnp.int32, (BLOCKS, BLOCKS), 0) < lax.broadcasted_iota(
        jnp.int32, (BLOCKS, BLOCKS), 1
    )
    place = jnp.full(near_list.shape, 2 * LIST, jnp.int32)
    amounts = []
    for i, mine in enumerate((live - late, late)):
        rows = [mine[n : n + 1] for n in range(NEAR)]
        before = [jnp.zeros_like(rows[0])]
        for row in rows:
            before.append(before[-1] + row)
        amount = before.pop().astype(f32)
        offset = jnp.dot(
            jnp.broadcast_to(amount, (8, BLOCKS)),
            jnp.where(earlier, 1.0, 0.0),
            preferred_element_type=f32,
        )[:1]
        at = jnp.concatenate([offset.astype(jnp.int32) + x for x in before], axis=0)
        place = jnp.where(mine > 0, at + LIST * i, place)
        amounts.append(jnp.sum(amount, axis=1, keepdims=True).astype(jnp.int32))
    words = 2**15 * place + 2**SHARE * block + moved
    return words, amounts


def pack_kernel(numbers_smem, numbers, positions, burgers, places, scalars, s3, s0, s2, s1):
    slab, cell = centre_of()
    for k, by in enumerate((slab + 0.5, cell + 0.5, 0.5)):
        places[k] = positions[k] - by
    scalars[...] = jnp.zeros_like(scalars)
    words, amounts = list_pairs(numbers[:NEAR, :BLOCKS], numbers[NEAR : NEAR + 1, :BLOCKS])
    scalars[:NEAR, :BLOCKS] = words
    for i in range(2):
        scalars[NEAR + i : NEAR + i + 1, :] = jnp.broadcast_to(amounts[i], (1, LANES))
    rows = send_rows()
    for d in range(4):
        first = 2 * (d // 2)
        scalars[8 + d : 9 + d, :] = jnp.where(
            rows[d] == first, numbers[8 + first : 9 + first, :], numbers[9 + first : 10 + first, :]
        )
    sources = [(places, k) for k in range(3)] + [(burgers, a) for a in range(3)]
    fill_sends(lambda d, n: numbers_smem[8 + rows[d], n], sources, {0: s0, 1: s1, 2: s2, 3: s3})


def put_rows(out, k, value):
    for b in range(BLOCKS):
        out[k : k + 1, LANES * b : LANES * b + LANES] = value[b : b + 1]


def halves(tile):
    low = lax.broadcasted_iota(jnp.int32, (8, LANES), 0) < 4
    turned = pltpu.roll(tile, 4, 0)
    return jnp.where(low, tile, turned), jnp.where(low, turned, tile)


def pair_rows(values):
    low = lax.broadcasted_iota(jnp.int32, (8, LANES), 0) < 4
    rows = [
        x if x is y else jnp.where(low, x, y) for x, y in zip(values[0::2], values[1::2])
    ]
    rows += [jnp.zeros((8, LANES), f32)] * (LANES // 8 - len(rows))
    return jnp.concatenate(rows, axis=0)


def far_kernel(
    scalars, places, burgers, out, control, acc, rows, cols, apart_by, w_even, w_odd
):
    amounts = [scalars[NEAR, 0], scalars[NEAR + 1, 0]]
    for i in range(LEAD):
        control[AT_PAIRS - LEAD + i] = EXT
        control[AT_PAIRS + LIST - LEAD + i] = EXT
    for tile in range(BLOCKS // 8):
        p = [halves(places[k, 8 * tile : 8 * tile + 8, :]) for k in range(3)]
        burg = [halves(burgers[a, 8 * tile : 8 * tile + 8, :]) for a in range(3)]
        for half in range(2):
            here = [x[half] for x in p]
            sources = [x[half] for x in burg]
            moments = [x * y for x in here for y in sources]
            values = []
            for group in (sources, moments):
                high = [round_bf16(x) for x in group]
                values += high + [x - h for x, h in zip(group, high)]
            rows[2 * tile + half] = pair_rows(values)
            one = jnp.ones((8, LANES), f32)
            square = sum(x * x for x in here) + far_sq
            values = [part for x in (here[0], here[1], square) for part in split3(x)]
            cols[2 * tile + half] = pair_rows(values + [one, one, one]).T.astype(bf16)
    acc[...] = jnp.zeros_like(acc)
    w_odd[...] = jnp.zeros_like(w_odd)
    slab, cell = centre_of()
    target = lax.broadcasted_iota(jnp.int32, (1, EXT), 1)
    apart = [(target // 32).astype(f32) - slab, (target % 32).astype(f32) - cell]
    square = apart[0] * apart[0] + apart[1] * apart[1]
    square_high = round_bf16(square)
    place = lax.broadcasted_iota(jnp.int32, (LANES, EXT), 0)
    values = jnp.where(place < 36, 1.0, 0.0)
    for first, last, x in (
        (0, 12, -2.0 * apart[0]),
        (12, 24, -2.0 * apart[1]),
        (36, 40, square_high),
        (40, 44, square - square_high),
    ):
        values = jnp.where((place >= first) & (place < last), x, values)
    for g in range(4):
        apart_by[g] = jnp.where(place % 4 == g, values, 0.0).astype(bf16)

    def sums(group, g, w):
        mine = rows[group, pl.ds(g, 32, stride=4), :].astype(bf16)
        acc[...] += jnp.dot(
            jnp.concatenate([mine, mine], axis=1), w[g], preferred_element_type=f32
        )

    def half(group, w_now, w_before):
        for i in range(4):
            for slot in range(NEAR):
                word = scalars[slot, 4 * group + i]
                at = lax.shift_right_logical(word, 15)
                control[AT_PAIRS + at] = word & (2**15 - 1)
        for d in range(4):
            for i in range(3):
                n = 3 * group + i
                control[AT_SENDS + GHOST * d + n] = scalars[8 + d, n]
        for g in range(4):
            sums(jnp.maximum(group - 1, 0), g, w_before)
            r = lax.rsqrt(jnp.dot(cols[group], apart_by[g], preferred_element_type=f32))
            r2 = r * r
            w3 = r2 * r
            for k, w in enumerate((w3, w3 * r2)):
                high, low = split2(w)
                w_now[g, :LANES, EXT * k : EXT * k + EXT] = high
                w_now[g, LANES:, EXT * k : EXT * k + EXT] = low

    def body(step, carry):
        half(2 * step, w_even, w_odd)
        half(2 * step + 1, w_odd, w_even)
        return carry

    lax.fori_loop(0, BLOCKS // 8, body, 0)
    for g in range(4):
        sums(BLOCKS // 4 - 1, g, w_odd)
    for k in range(2):
        for i in range(TAIL):
            control[AT_PAIRS + LIST * k + amounts[k] + i] = EXT
        control[k] = amounts[k]

    apart = apart + [jnp.zeros((1, EXT), f32)]

    def row(k, i):
        return acc[i : i + 1, EXT * k : EXT * k + EXT]

    direct = [row(0, a) + row(0, 3 + a) for a in range(3)]
    total = [row(1, a) + row(1, 3 + a) for a in range(3)]
    gradient = []
    for a in range(3):
        for k in range(3):
            moment = row(1, 6 + 3 * k + a) + row(1, 15 + 3 * k + a)
            gradient.append(-3.0 * (apart[k] * total[a] - moment))
    zero = jnp.zeros((LANES - 12, 2 * LANES), f32)
    values = jnp.concatenate(direct + gradient + [zero], axis=0)
    out[...] = jnp.concatenate([values[:, :LANES].T, values[:, LANES:].T], axis=0)


def tile_of(own, ghosts, index, tile):
    if tile < BLOCKS // 8:
        return own[index, 8 * tile : 8 * tile + 8, :]
    d, n = divmod(tile - BLOCKS // 8, GHOST // 8)
    return ghosts[d][index, 8 * n : 8 * n + 8, :]


def tiles_of(slots):
    n = GHOST // 8
    return [BLOCKS // 8 + n * d + i for d in slots for i in range(n)]


def prepare_sources(own, ghosts, tiles, left):
    shift = slot_shifts()
    one = jnp.ones((8, LANES), f32)
    low = lax.broadcasted_iota(jnp.int32, (8, LANES), 0) < 4

    for tile in tiles:
        p = [tile_of(own, ghosts, k, tile) for k in range(3)]
        if tile >= BLOCKS // 8:
            k, by = shift[(tile - BLOCKS // 8) // (GHOST // 8)]
            p[k] = p[k] + by
        parts_of = [split3(x) for x in p]
        parts_of.append(split3(p[0] * p[0] + p[1] * p[1] + p[2] * p[2]))
        turned = [[pltpu.roll(x, 4, 0) for x in group] for group in parts_of]
        for half in range(2):
            first, second = (parts_of, turned) if half == 0 else (turned, parts_of)
            values = []
            for (h, m, _), (h2, m2, l2) in zip(first[:3], second[:3]):
                values += [
                    jnp.where(low, h, h2),
                    jnp.where(low, m, m2),
                    jnp.where(low, h, l2),
                ]
            h, _, l = first[3]
            values += [jnp.where(low, h, second[3][1]), jnp.where(low, l, one), one]
            values += [jnp.zeros((8, LANES), f32)] * (LANES // 8 - len(values))
            left[2 * tile + half] = jnp.concatenate(values, axis=0).T.astype(bf16)
    left[EXT // 4] = jnp.zeros((LANES, LANES), bf16)


def prepare_targets(own, parts, right):
    one = jnp.ones((8, LANES), f32)
    low = lax.broadcasted_iota(jnp.int32, (8, LANES), 0) < 4

    x = [own[k] for k in range(3)]
    for k in range(3):
        for i, part in enumerate(split3(-2.0 * x[k])):
            parts[3 * k + i] = part
    for i, part in enumerate(split3(x[0] * x[0] + x[1] * x[1] + x[2] * x[2] + core_sq)):
        parts[9 + i] = part
    for b in range(BLOCKS):
        def row(i):
            return jnp.broadcast_to(parts[i, b : b + 1, :], (8, LANES))

        rows = []
        for k in range(3):
            h, m, l = row(3 * k), row(3 * k + 1), row(3 * k + 2)
            high_mid = jnp.where(low, h, m)
            rows += [high_mid, high_mid, jnp.where(low, l, h)]
        rows += [one, jnp.where(low, one, row(9)), jnp.where(low, row(10), row(11))]
        for i in range(6):
            right[b, i] = jnp.concatenate(rows[2 * i : 2 * i + 2], axis=0).astype(bf16)
        right[b, 6:] = jnp.zeros((2, 16, LANES), bf16)


def add_pairs(control, which, burg, left, right, mask, acc, k_even, k_odd):
    place = lax.broadcasted_iota(jnp.int32, (16, LANES), 0) % 4
    for g in range(4):
        mask[g] = jnp.where(place == g, 1.0, 0.0).astype(bf16)

    k_odd[...] = jnp.zeros_like(k_odd)

    def pair(i):
        word = control[AT_PAIRS + LIST * which + i]
        return lax.shift_right_logical(word, SHARE), word & (2**SHARE - 1)

    def sums(step, g, k_before):
        i = step * GROUP + g
        (b0, t0), (b1, t1) = pair(i), pair(i + 1)
        rows = jnp.concatenate(
            [burg[pl.ds(pl.multiple_of(8 * t, 8), 8), :] for t in (t0, t1)], axis=0
        ).astype(bf16)
        both = jnp.dot(
            jnp.concatenate([rows, rows], axis=1),
            jnp.concatenate([k_before[g], k_before[g + 1]], axis=1),
            preferred_element_type=f32,
        )
        at = pl.ds(pl.multiple_of(8 * b0, 8), 8)
        acc[at, :] = acc[at, :] + both[:8, :LANES]
        at = pl.ds(pl.multiple_of(8 * b1, 8), 8)
        acc[at, :] = acc[at, :] + both[8:, LANES:]

    def half(step, k_now, k_before):
        for g in range(GROUP):
            if g % 2 == 0:
                sums(step - 1, g, k_before)
            b, t = pair(step * GROUP + g)
            features = (right[b] * mask[t & 3][None]).reshape(LANES, LANES)
            near_sq = jnp.dot(
                left[lax.shift_right_logical(t, 2)], features, preferred_element_type=f32
            )
            near_sq = jnp.maximum(near_sq, core_sq)
            r = lax.rsqrt(near_sq)
            q = lax.rsqrt(near_sq + (far_sq - core_sq))
            high, low = split2(r * r * r - q * q * q)
            k_now[g, :LANES, :] = high
            k_now[g, LANES:, :] = low

    def body(step, carry):
        half(2 * step, k_even, k_odd)
        half(2 * step + 1, k_odd, k_even)
        return carry

    steps = (control[which] + 2 * GROUP - 1) // (2 * GROUP)
    lax.fori_loop(0, steps, body, 0)
    for g in range(0, GROUP, 2):
        sums(2 * steps - 1, g, k_odd)


def component(acc, a):
    return acc[pl.ds(a, BLOCKS, stride=8), :] + acc[pl.ds(3 + a, BLOCKS, stride=8), :]


parts_scratch = pltpu.VMEM((12, BLOCKS, LANES), f32)
right_shape = (BLOCKS, 8, 16, LANES)
acc_shape = (BLOCKS * 8, LANES)
near_scratch = [
    pltpu.VMEM((EXT // 4 + 1, LANES, LANES), bf16),
    pltpu.VMEM((4, 16, LANES), bf16),
    pltpu.VMEM((GROUP, 2 * LANES, LANES), bf16),
    pltpu.VMEM((GROUP, 2 * LANES, LANES), bf16),
]


def total_force(expansion, near, places):
    out = []
    for a in range(3):
        far = expansion[0:1, a : a + 1]
        for k in range(3):
            far = far + expansion[0:1, 3 + 3 * a + k : 4 + 3 * a + k] * places[k]
        out.append(near[a] + far)
    return out


def first_kernel(
    control, own, burgers, g3, g0, g2, g1, near, burg, left, mask, k_even, k_odd, parts, right, acc
):
    ghosts = (g0, g1, g2, g3)
    exists = slot_exists()
    burg[...] = jnp.zeros_like(burg)
    for tile in range(EXT // 8):
        for a in range(3):
            if tile < BLOCKS // 8:
                value = burgers[a, 8 * tile : 8 * tile + 8, :]
            else:
                d = (tile - BLOCKS // 8) // (GHOST // 8)
                value = tile_of(None, ghosts, 3 + a, tile)
                if exists[d] is not None:
                    value = jnp.where(exists[d], value, 0.0)
            high = round_bf16(value)
            burg[pl.ds(tile * 64 + a, 8, stride=8), :] = high
            burg[pl.ds(tile * 64 + 3 + a, 8, stride=8), :] = value - high
    prepare_sources(own, ghosts, range(EXT // 8), left)
    prepare_targets(own, parts, right)
    acc[...] = jnp.zeros_like(acc)
    for which in range(2):
        add_pairs(control, which, burg, left, right, mask, acc, k_even, k_odd)
    for a in range(3):
        near[a] = component(acc, a)


def start_kernel(control, shares, near, places, mobility, expansion, moved, now, *sends):
    expansion[...] = jnp.broadcast_to(jnp.sum(shares[...], axis=0, keepdims=True), (8, LANES))
    p = [places[k] for k in range(3)]
    force = total_force(expansion[...], [near[a] for a in range(3)], p)
    for a in range(3):
        step = (time_step * mobility[...]) * force[a]
        moved[a] = step
        now[a] = p[a] + step
    send_now(control, now, sends)


def early_kernel(control, own, g3, g0, burg, right, acc, left, mask, k_even, k_odd, parts):
    ghosts = (g0, None, None, g3)
    prepare_sources(own, ghosts, list(range(BLOCKS // 8)) + tiles_of(EARLY), left)
    prepare_targets(own, parts, right)
    acc[...] = jnp.zeros_like(acc)
    add_pairs(control, 0, burg, left, right, mask, acc, k_even, k_odd)


def late_force(control, expansion, own, g2, g1, burg, right, acc_in, left, mask, k_even, k_odd, acc):
    prepare_sources(own, (None, g1, g2, None), tiles_of(LATE), left)
    acc[...] = acc_in[...]
    add_pairs(control, 1, burg, left, right, mask, acc, k_even, k_odd)
    return total_force(
        expansion[...], [component(acc, a) for a in range(3)], [own[k] for k in range(3)]
    )


def step_kernel(
    final, control, expansion, own, g2, g1, burg, right, acc_in, mobility, places, moved,
    new_moved, now, s0, s1, s2, s3, *scratch
):
    force = late_force(control, expansion, own, g2, g1, burg, right, acc_in, *scratch)
    for a in range(3):
        total = moved[a] + (time_step * mobility[...]) * force[a]
        if final:
            put_rows(new_moved, a, total)
        else:
            new_moved[a] = total
        now[a] = places[a] + total
    send_now(control, now, (s0, s1, s2, s3))


def last_kernel(
    control, expansion, own, g2, g1, burg, right, acc_in, mobility, velocity, *scratch
):
    force = late_force(control, expansion, own, g2, g1, burg, right, acc_in, *scratch)
    for a in range(3):
        put_rows(velocity, a, mobility[...] * force[a])


def cost(flops):
    return pl.CostEstimate(flops=int(flops), bytes_accessed=2**20, transcendentals=0)


def shape(*dims, dtype=f32):
    return jax.ShapeDtypeStruct(dims, dtype)


def swap(x, slot):
    n_slabs, n_cells = lax.axis_size("slab"), lax.axis_size("cell")
    pairs = []
    for s in range(n_slabs):
        for c in range(n_cells):
            if slot == 0:
                to = (s ^ 1, c)
            elif slot == 3:
                to = (s, c ^ 1)
            elif slot == 1:
                t = s - 1 + 2 * (s % 2)
                to = (t, c) if 0 <= t < n_slabs else (s, c ^ 1)
            else:
                t = c - 1 + 2 * (c % 2)
                to = (s, t) if 0 <= t < n_cells else (s ^ 1, c)
            pairs.append((s * n_cells + c, to[0] * n_cells + to[1]))
    return lax.ppermute(x, ("slab", "cell"), pairs)


def exchange(sends):
    return [swap(sends[slot], slot) for slot in EARLY + LATE]


def local(positions, burgers, mobility, near_list, near_count, send_list):
    mobility = mobility.reshape(BLOCKS, LANES)
    flat = shape(*positions.shape)
    block = shape(3, BLOCKS, LANES)
    send = shape(3, GHOST, LANES)

    positions = positions.reshape(block.shape)
    burgers = burgers.reshape(block.shape)
    numbers = (
        jnp.pad(near_list.T, ((0, 16 - NEAR), (0, LANES - BLOCKS)))
        + jnp.pad(near_count[None], ((NEAR, 15 - NEAR), (0, LANES - BLOCKS)))
        + jnp.pad(send_list, ((8, 4), (0, LANES - GHOST)))
    )

    places, scalars, *sends = pl.pallas_call(
        pack_kernel,
        out_shape=[block, shape(16, LANES, dtype=jnp.int32)] + [shape(6, GHOST, LANES)] * 4,
        in_specs=[smem, vmem, vmem, vmem],
        out_specs=[vmem] * 6,
        compiler_params=params,
        name="pack",
    )(numbers, numbers, positions, burgers)
    ghosts = [swap(x, slot) for x, slot in zip(sends, (3, 0, 2, 1))]

    shares, control = pl.pallas_call(
        far_kernel,
        out_shape=[shape(EXT, LANES), shape(CONTROL, dtype=jnp.int32)],
        in_specs=[smem, vmem, vmem],
        out_specs=[vmem, smem],
        scratch_shapes=[
            pltpu.VMEM((32, 2 * EXT), f32),
            pltpu.VMEM((BLOCKS // 4, LANES, LANES), f32),
            pltpu.VMEM((BLOCKS // 4, LANES, LANES), bf16),
            pltpu.VMEM((4, LANES, EXT), bf16),
            pltpu.VMEM((4, 2 * LANES, 2 * EXT), bf16),
            pltpu.VMEM((4, 2 * LANES, 2 * EXT), bf16),
        ],
        compiler_params=params,
        cost_estimate=cost(20e9),
        name="far",
    )(scalars, places, burgers)
    shares = lax.all_to_all(shares, ("slab", "cell"), 0, 0, tiled=True)

    near, burg = pl.pallas_call(
        first_kernel,
        out_shape=[block, shape((EXT + 1) * 8, LANES)],
        in_specs=[smem] + [vmem] * 6,
        out_specs=[vmem] * 2,
        scratch_shapes=near_scratch
        + [parts_scratch, pltpu.VMEM(right_shape, bf16), pltpu.VMEM(acc_shape, f32)],
        compiler_params=params,
        cost_estimate=cost(20e9),
        name="near_first",
    )(control, places, burgers, *ghosts)

    expansion, moved, now, *sends = pl.pallas_call(
        start_kernel,
        out_shape=[shape(8, LANES), block, block] + [send] * 4,
        in_specs=[smem] + [vmem] * 4,
        out_specs=[vmem] * 7,
        compiler_params=params,
        name="start",
    )(control, shares, near, places, mobility)

    def evaluate(kernel, out_shape, name, *more):
        ghosts = exchange(sends)
        right, acc = pl.pallas_call(
            early_kernel,
            out_shape=[shape(*right_shape, dtype=bf16), shape(*acc_shape)],
            in_specs=[smem] + [vmem] * 4,
            out_specs=[vmem] * 2,
            scratch_shapes=near_scratch + [parts_scratch],
            compiler_params=params,
            cost_estimate=cost(20e9),
            name="near_early",
        )(control, now, *ghosts[:2], burg)
        return pl.pallas_call(
            kernel,
            out_shape=out_shape,
            in_specs=[smem] + [vmem] * (8 + len(more)),
            out_specs=jax.tree.map(lambda _: vmem, out_shape),
            scratch_shapes=near_scratch + [pltpu.VMEM(acc_shape, f32)],
            compiler_params=params,
            cost_estimate=cost(10e9),
            name=name,
        )(control, expansion, now, *ghosts[2:], burg, right, acc, mobility, *more)

    for substep in range(1, SUBSTEPS):
        final = substep == SUBSTEPS - 1
        moved, now, *sends = evaluate(
            functools.partial(step_kernel, final),
            [flat if final else block, block] + [send] * 4,
            "near_step",
            places,
            moved,
        )
    velocity = evaluate(last_kernel, flat, "near_last")
    return moved, velocity


def solution(mesh):
    return jax.shard_map(
        local,
        mesh=mesh,
        in_specs=(
            P(None, ("slab", "cell")),
            P(None, ("slab", "cell")),
            P(("slab", "cell")),
            P(("slab", "cell"), None),
            P(("slab", "cell")),
            P(None, ("slab", "cell")),
        ),
        out_specs=(P(None, ("slab", "cell")), P(None, ("slab", "cell"))),
        check_vma=False,
    )
```

```python
import functools

import jax
import jax.numpy as jnp
from jax import lax
from jax.experimental import pallas as pl
from jax.experimental.pallas import tpu as pltpu
from jax.sharding import PartitionSpec as P

SUBSTEPS = 4
BLOCKS = 64
LANES = 128
NEAR = 6
GHOST = 48
EXT = 256
GROUP = 8
LEAD = GROUP
TAIL = 56
AT_SENDS = 8
AT_PAIRS = AT_SENDS + 4 * GHOST + LEAD
LIST = BLOCKS * NEAR + TAIL + LEAD
CONTROL = AT_PAIRS + 2 * LIST + 8
EARLY, LATE = (3,), (0, 2, 1)
SHARE = 9

core_sq = 0.04
far_sq = 1.0
time_step = 0.2

f32 = jnp.float32
bf16 = jnp.bfloat16

vmem = pl.BlockSpec(memory_space=pltpu.VMEM)
smem = pl.BlockSpec(memory_space=pltpu.SMEM)
params = pltpu.CompilerParams(vmem_limit_bytes=40 * 2**20)


def round_bf16(x):
    return x.astype(bf16).astype(f32)


def split2(x):
    high = x.astype(bf16)
    return high, (x - high.astype(f32)).astype(bf16)


def split3(x):
    high = round_bf16(x)
    rest = x - high
    mid = round_bf16(rest)
    return high, mid, round_bf16(rest - mid)


def parity():
    return lax.axis_index("slab") % 2, lax.axis_index("cell") % 2


def send_rows():
    odd_slab, odd_cell = parity()
    return odd_slab, 1 - odd_slab, 3 - odd_cell, 2 + odd_cell


def slot_moves():
    odd_slab, odd_cell = parity()
    return (
        GHOST * (1 - odd_slab),
        GHOST * (odd_slab - 1),
        GHOST * odd_cell,
        -GHOST * odd_cell,
    )


def slot_shifts():
    odd_slab, odd_cell = parity()
    along_slab = (1 - 2 * odd_slab).astype(f32)
    along_cell = (1 - 2 * odd_cell).astype(f32)
    return (0, along_slab), (0, -along_slab), (1, -along_cell), (1, along_cell)


def slot_exists():
    out = []
    for axis in ("slab", "cell"):
        i = lax.axis_index(axis)
        partner = i - 1 + 2 * (i % 2)
        out.append((partner >= 0) & (partner < lax.axis_size(axis)))
    return None, out[0], out[1], None


def fill_sends(block_of, sources, sends):
    def body(n, carry):
        for d in sends:
            block = block_of(d, n)
            for a, (ref, index) in enumerate(sources):
                sends[d][a, pl.ds(n, 1), :] = ref[index, pl.ds(block, 1), :]
        return carry

    lax.fori_loop(0, GHOST, body, 0, unroll=4)


def send_now(control, now, sends):
    fill_sends(
        lambda d, n: control[AT_SENDS + GHOST * d + n],
        [(now, k) for k in range(3)],
        dict(enumerate(sends)),
    )


def centre_of():
    slab = lax.axis_index("slab").astype(f32)
    cell = lax.axis_index("cell").astype(f32)
    return slab, cell


def list_pairs(near_list, near_count):
    segment = (near_list + (GHOST - BLOCKS)) // GHOST
    exists = {0: None, 3: None}
    exists[1], exists[2] = slot_exists()[1:3]
    odd_slab, odd_cell = parity()
    sides = (
        (odd_slab == 1) | exists[1],
        (odd_slab == 0) | exists[1],
        (odd_cell == 1) | exists[2],
        (odd_cell == 0) | exists[2],
    )
    slot = lax.broadcasted_iota(jnp.int32, near_list.shape, 0)
    block = lax.broadcasted_iota(jnp.int32, near_list.shape, 1)
    live = jnp.where(slot < near_count, 1, 0)
    moved = near_list
    for i, (move, there) in enumerate(zip(slot_moves(), sides)):
        mine = segment == 1 + i
        moved = moved + jnp.where(mine, move, 0)
        live = jnp.where(mine, live * there.astype(jnp.int32), live)
    late = jnp.where(moved >= BLOCKS, live, 0)
    for d in EARLY:
        first = BLOCKS + GHOST * d
        late = jnp.where((moved >= first) & (moved < first + GHOST), 0, late)
    earlier = lax.broadcasted_iota(jnp.int32, (BLOCKS, BLOCKS), 0) < lax.broadcasted_iota(
        jnp.int32, (BLOCKS, BLOCKS), 1
    )
    place = jnp.full(near_list.shape, 2 * LIST, jnp.int32)
    amounts = []
    for i, mine in enumerate((live - late, late)):
        rows = [mine[n : n + 1] for n in range(NEAR)]
        before = [jnp.zeros_like(rows[0])]
        for row in rows:
            before.append(before[-1] + row)
        amount = before.pop().astype(f32)
        offset = jnp.dot(
            jnp.broadcast_to(amount, (8, BLOCKS)),
            jnp.where(earlier, 1.0, 0.0),
            preferred_element_type=f32,
        )[:1]
        at = jnp.concatenate([offset.astype(jnp.int32) + x for x in before], axis=0)
        place = jnp.where(mine > 0, at + LIST * i, place)
        amounts.append(jnp.sum(amount, axis=1, keepdims=True).astype(jnp.int32))
    words = 2**15 * place + 2**SHARE * block + moved
    return words, amounts


def pack_kernel(numbers_smem, numbers, positions, burgers, places, scalars, s3, s0, s2, s1):
    slab, cell = centre_of()
    for k, by in enumerate((slab + 0.5, cell + 0.5, 0.5)):
        places[k] = positions[k] - by
    scalars[...] = jnp.zeros_like(scalars)
    words, amounts = list_pairs(numbers[:NEAR, :BLOCKS], numbers[NEAR : NEAR + 1, :BLOCKS])
    scalars[:NEAR, :BLOCKS] = words
    for i in range(2):
        scalars[NEAR + i : NEAR + i + 1, :] = jnp.broadcast_to(amounts[i], (1, LANES))
    rows = send_rows()
    for d in range(4):
        first = 2 * (d // 2)
        scalars[8 + d : 9 + d, :] = jnp.where(
            rows[d] == first, numbers[8 + first : 9 + first, :], numbers[9 + first : 10 + first, :]
        )
    sources = [(places, k) for k in range(3)] + [(burgers, a) for a in range(3)]
    fill_sends(lambda d, n: numbers_smem[8 + rows[d], n], sources, {0: s0, 1: s1, 2: s2, 3: s3})


def put_rows(out, k, value):
    for b in range(BLOCKS):
        out[k : k + 1, LANES * b : LANES * b + LANES] = value[b : b + 1]


def halves(tile):
    low = lax.broadcasted_iota(jnp.int32, (8, LANES), 0) < 4
    turned = pltpu.roll(tile, 4, 0)
    return jnp.where(low, tile, turned), jnp.where(low, turned, tile)


def pair_rows(values):
    low = lax.broadcasted_iota(jnp.int32, (8, LANES), 0) < 4
    rows = [
        x if x is y else jnp.where(low, x, y) for x, y in zip(values[0::2], values[1::2])
    ]
    rows += [jnp.zeros((8, LANES), f32)] * (LANES // 8 - len(rows))
    return jnp.concatenate(rows, axis=0)


def far_kernel(
    scalars, places, burgers, out, control, acc, rows, cols, apart_by, w_even, w_odd
):
    amounts = [scalars[NEAR, 0], scalars[NEAR + 1, 0]]
    for i in range(LEAD):
        control[AT_PAIRS - LEAD + i] = EXT
        control[AT_PAIRS + LIST - LEAD + i] = EXT
    for tile in range(BLOCKS // 8):
        p = [halves(places[k, 8 * tile : 8 * tile + 8, :]) for k in range(3)]
        burg = [halves(burgers[a, 8 * tile : 8 * tile + 8, :]) for a in range(3)]
        for half in range(2):
            here = [x[half] for x in p]
            sources = [x[half] for x in burg]
            moments = [x * y for x in here for y in sources]
            values = []
            for group in (sources, moments):
                high = [round_bf16(x) for x in group]
                values += high + [x - h for x, h in zip(group, high)]
            rows[2 * tile + half] = pair_rows(values)
            one = jnp.ones((8, LANES), f32)
            square = sum(x * x for x in here) + far_sq
            values = [part for x in (here[0], here[1], square) for part in split3(x)]
            cols[2 * tile + half] = pair_rows(values + [one, one, one]).T.astype(bf16)
    acc[...] = jnp.zeros_like(acc)
    w_odd[...] = jnp.zeros_like(w_odd)
    slab, cell = centre_of()
    target = lax.broadcasted_iota(jnp.int32, (1, EXT), 1)
    apart = [(target // 32).astype(f32) - slab, (target % 32).astype(f32) - cell]
    square = apart[0] * apart[0] + apart[1] * apart[1]
    square_high = round_bf16(square)
    place = lax.broadcasted_iota(jnp.int32, (LANES, EXT), 0)
    values = jnp.where(place < 36, 1.0, 0.0)
    for first, last, x in (
        (0, 12, -2.0 * apart[0]),
        (12, 24, -2.0 * apart[1]),
        (36, 40, square_high),
        (40, 44, square - square_high),
    ):
        values = jnp.where((place >= first) & (place < last), x, values)
    for g in range(4):
        apart_by[g] = jnp.where(place % 4 == g, values, 0.0).astype(bf16)

    def sums(group, g, w):
        mine = rows[group, pl.ds(g, 32, stride=4), :].astype(bf16)
        acc[...] += jnp.dot(
            jnp.concatenate([mine, mine], axis=1), w[g], preferred_element_type=f32
        )

    def half(group, w_now, w_before):
        for i in range(4):
            for slot in range(NEAR):
                word = scalars[slot, 4 * group + i]
                at = lax.shift_right_logical(word, 15)
                control[AT_PAIRS + at] = word & (2**15 - 1)
        for d in range(4):
            for i in range(3):
                n = 3 * group + i
                control[AT_SENDS + GHOST * d + n] = scalars[8 + d, n]
        for g in range(4):
            sums(jnp.maximum(group - 1, 0), g, w_before)
            r = lax.rsqrt(jnp.dot(cols[group], apart_by[g], preferred_element_type=f32))
            r2 = r * r
            w3 = r2 * r
            for k, w in enumerate((w3, w3 * r2)):
                high, low = split2(w)
                w_now[g, :LANES, EXT * k : EXT * k + EXT] = high
                w_now[g, LANES:, EXT * k : EXT * k + EXT] = low

    def body(step, carry):
        half(2 * step, w_even, w_odd)
        half(2 * step + 1, w_odd, w_even)
        return carry

    lax.fori_loop(0, BLOCKS // 8, body, 0)
    for g in range(4):
        sums(BLOCKS // 4 - 1, g, w_odd)
    for k in range(2):
        for i in range(TAIL):
            control[AT_PAIRS + LIST * k + amounts[k] + i] = EXT
        control[k] = amounts[k]

    apart = apart + [jnp.zeros((1, EXT), f32)]

    def row(k, i):
        return acc[i : i + 1, EXT * k : EXT * k + EXT]

    direct = [row(0, a) + row(0, 3 + a) for a in range(3)]
    total = [row(1, a) + row(1, 3 + a) for a in range(3)]
    gradient = []
    for a in range(3):
        for k in range(3):
            moment = row(1, 6 + 3 * k + a) + row(1, 15 + 3 * k + a)
            gradient.append(-3.0 * (apart[k] * total[a] - moment))
    zero = jnp.zeros((LANES - 12, 2 * LANES), f32)
    values = jnp.concatenate(direct + gradient + [zero], axis=0)
    out[...] = jnp.concatenate([values[:, :LANES].T, values[:, LANES:].T], axis=0)


def tile_of(own, ghosts, index, tile):
    if tile < BLOCKS // 8:
        return own[index, 8 * tile : 8 * tile + 8, :]
    d, n = divmod(tile - BLOCKS // 8, GHOST // 8)
    return ghosts[d][index, 8 * n : 8 * n + 8, :]


def tiles_of(slots):
    n = GHOST // 8
    return [BLOCKS // 8 + n * d + i for d in slots for i in range(n)]


def prepare_sources(own, ghosts, tiles, left):
    shift = slot_shifts()
    one = jnp.ones((8, LANES), f32)
    low = lax.broadcasted_iota(jnp.int32, (8, LANES), 0) < 4

    for tile in tiles:
        p = [tile_of(own, ghosts, k, tile) for k in range(3)]
        if tile >= BLOCKS // 8:
            k, by = shift[(tile - BLOCKS // 8) // (GHOST // 8)]
            p[k] = p[k] + by
        parts_of = [split3(x) for x in p]
        parts_of.append(split3(p[0] * p[0] + p[1] * p[1] + p[2] * p[2]))
        turned = [[pltpu.roll(x, 4, 0) for x in group] for group in parts_of]
        for half in range(2):
            first, second = (parts_of, turned) if half == 0 else (turned, parts_of)
            values = []
            for (h, m, _), (h2, m2, l2) in zip(first[:3], second[:3]):
                values += [
                    jnp.where(low, h, h2),
                    jnp.where(low, m, m2),
                    jnp.where(low, h, l2),
                ]
            h, _, l = first[3]
            values += [jnp.where(low, h, second[3][1]), jnp.where(low, l, one), one]
            values += [jnp.zeros((8, LANES), f32)] * (LANES // 8 - len(values))
            left[2 * tile + half] = jnp.concatenate(values, axis=0).T.astype(bf16)
    left[EXT // 4] = jnp.zeros((LANES, LANES), bf16)


def prepare_targets(own, parts, right):
    one = jnp.ones((8, LANES), f32)
    low = lax.broadcasted_iota(jnp.int32, (8, LANES), 0) < 4

    x = [own[k] for k in range(3)]
    for k in range(3):
        for i, part in enumerate(split3(-2.0 * x[k])):
            parts[3 * k + i] = part
    for i, part in enumerate(split3(x[0] * x[0] + x[1] * x[1] + x[2] * x[2] + core_sq)):
        parts[9 + i] = part
    for b in range(BLOCKS):
        def row(i):
            return jnp.broadcast_to(parts[i, b : b + 1, :], (8, LANES))

        rows = []
        for k in range(3):
            h, m, l = row(3 * k), row(3 * k + 1), row(3 * k + 2)
            high_mid = jnp.where(low, h, m)
            rows += [high_mid, high_mid, jnp.where(low, l, h)]
        rows += [one, jnp.where(low, one, row(9)), jnp.where(low, row(10), row(11))]
        for i in range(6):
            right[b, i] = jnp.concatenate(rows[2 * i : 2 * i + 2], axis=0).astype(bf16)
        right[b, 6:] = jnp.zeros((2, 16, LANES), bf16)


def add_pairs(control, which, burg, left, right, mask, acc, k_even, k_odd):
    place = lax.broadcasted_iota(jnp.int32, (16, LANES), 0) % 4
    for g in range(4):
        mask[g] = jnp.where(place == g, 1.0, 0.0).astype(bf16)

    k_odd[...] = jnp.zeros_like(k_odd)

    def pair(i):
        word = control[AT_PAIRS + LIST * which + i]
        return lax.shift_right_logical(word, SHARE), word & (2**SHARE - 1)

    def sums(step, g, k_before):
        i = step * GROUP + g
        (b0, t0), (b1, t1) = pair(i), pair(i + 1)
        rows = jnp.concatenate(
            [burg[pl.ds(pl.multiple_of(8 * t, 8), 8), :] for t in (t0, t1)], axis=0
        ).astype(bf16)
        both = jnp.dot(
            jnp.concatenate([rows, rows], axis=1),
            jnp.concatenate([k_before[g], k_before[g + 1]], axis=1),
            preferred_element_type=f32,
        )
        at = pl.ds(pl.multiple_of(8 * b0, 8), 8)
        acc[at, :] = acc[at, :] + both[:8, :LANES]
        at = pl.ds(pl.multiple_of(8 * b1, 8), 8)
        acc[at, :] = acc[at, :] + both[8:, LANES:]

    def half(step, k_now, k_before):
        for g in range(GROUP):
            if g % 2 == 0:
                sums(step - 1, g, k_before)
            b, t = pair(step * GROUP + g)
            features = (right[b] * mask[t & 3][None]).reshape(LANES, LANES)
            near_sq = jnp.dot(
                left[lax.shift_right_logical(t, 2)], features, preferred_element_type=f32
            )
            near_sq = jnp.maximum(near_sq, core_sq)
            r = lax.rsqrt(near_sq)
            q = lax.rsqrt(near_sq + (far_sq - core_sq))
            high, low = split2(r * r * r - q * q * q)
            k_now[g, :LANES, :] = high
            k_now[g, LANES:, :] = low

    def body(step, carry):
        half(2 * step, k_even, k_odd)
        half(2 * step + 1, k_odd, k_even)
        return carry

    steps = (control[which] + 2 * GROUP - 1) // (2 * GROUP)
    lax.fori_loop(0, steps, body, 0)
    for g in range(0, GROUP, 2):
        sums(2 * steps - 1, g, k_odd)


def component(acc, a):
    return acc[pl.ds(a, BLOCKS, stride=8), :] + acc[pl.ds(3 + a, BLOCKS, stride=8), :]


parts_scratch = pltpu.VMEM((12, BLOCKS, LANES), f32)
right_shape = (BLOCKS, 8, 16, LANES)
acc_shape = (BLOCKS * 8, LANES)
near_scratch = [
    pltpu.VMEM((EXT // 4 + 1, LANES, LANES), bf16),
    pltpu.VMEM((4, 16, LANES), bf16),
    pltpu.VMEM((GROUP, 2 * LANES, LANES), bf16),
    pltpu.VMEM((GROUP, 2 * LANES, LANES), bf16),
]


def total_force(expansion, near, places):
    out = []
    for a in range(3):
        far = expansion[0:1, a : a + 1]
        for k in range(3):
            far = far + expansion[0:1, 3 + 3 * a + k : 4 + 3 * a + k] * places[k]
        out.append(near[a] + far)
    return out


def first_kernel(
    control, own, burgers, g3, g0, g2, g1, near, burg, left, mask, k_even, k_odd, parts, right, acc
):
    ghosts = (g0, g1, g2, g3)
    exists = slot_exists()
    burg[...] = jnp.zeros_like(burg)
    for tile in range(EXT // 8):
        for a in range(3):
            if tile < BLOCKS // 8:
                value = burgers[a, 8 * tile : 8 * tile + 8, :]
            else:
                d = (tile - BLOCKS // 8) // (GHOST // 8)
                value = tile_of(None, ghosts, 3 + a, tile)
                if exists[d] is not None:
                    value = jnp.where(exists[d], value, 0.0)
            high = round_bf16(value)
            burg[pl.ds(tile * 64 + a, 8, stride=8), :] = high
            burg[pl.ds(tile * 64 + 3 + a, 8, stride=8), :] = value - high
    prepare_sources(own, ghosts, range(EXT // 8), left)
    prepare_targets(own, parts, right)
    acc[...] = jnp.zeros_like(acc)
    for which in range(2):
        add_pairs(control, which, burg, left, right, mask, acc, k_even, k_odd)
    for a in range(3):
        near[a] = component(acc, a)


def start_kernel(control, shares, near, places, mobility, expansion, moved, now, *sends):
    expansion[...] = jnp.broadcast_to(jnp.sum(shares[...], axis=0, keepdims=True), (8, LANES))
    p = [places[k] for k in range(3)]
    force = total_force(expansion[...], [near[a] for a in range(3)], p)
    for a in range(3):
        step = (time_step * mobility[...]) * force[a]
        moved[a] = step
        now[a] = p[a] + step
    send_now(control, now, sends)


def early_kernel(control, own, g3, burg, right, acc, left, mask, k_even, k_odd, parts):
    ghosts = (None, None, None, g3)
    prepare_sources(own, ghosts, list(range(BLOCKS // 8)) + tiles_of(EARLY), left)
    prepare_targets(own, parts, right)
    acc[...] = jnp.zeros_like(acc)
    add_pairs(control, 0, burg, left, right, mask, acc, k_even, k_odd)


def late_force(control, expansion, own, g0, g2, g1, burg, right, acc_in, left, mask, k_even, k_odd, acc):
    prepare_sources(own, (g0, g1, g2, None), tiles_of(LATE), left)
    acc[...] = acc_in[...]
    add_pairs(control, 1, burg, left, right, mask, acc, k_even, k_odd)
    return total_force(
        expansion[...], [component(acc, a) for a in range(3)], [own[k] for k in range(3)]
    )


def step_kernel(
    final, control, expansion, own, g0, g2, g1, burg, right, acc_in, mobility, places, moved,
    new_moved, now, s0, s1, s2, s3, *scratch
):
    force = late_force(control, expansion, own, g0, g2, g1, burg, right, acc_in, *scratch)
    for a in range(3):
        total = moved[a] + (time_step * mobility[...]) * force[a]
        if final:
            put_rows(new_moved, a, total)
        else:
            new_moved[a] = total
        now[a] = places[a] + total
    send_now(control, now, (s0, s1, s2, s3))


def last_kernel(
    control, expansion, own, g0, g2, g1, burg, right, acc_in, mobility, velocity, *scratch
):
    force = late_force(control, expansion, own, g0, g2, g1, burg, right, acc_in, *scratch)
    for a in range(3):
        put_rows(velocity, a, mobility[...] * force[a])


def cost(flops):
    return pl.CostEstimate(flops=int(flops), bytes_accessed=2**20, transcendentals=0)


def shape(*dims, dtype=f32):
    return jax.ShapeDtypeStruct(dims, dtype)


def swap(x, slot):
    n_slabs, n_cells = lax.axis_size("slab"), lax.axis_size("cell")
    pairs = []
    for s in range(n_slabs):
        for c in range(n_cells):
            if slot == 0:
                to = (s ^ 1, c)
            elif slot == 3:
                to = (s, c ^ 1)
            elif slot == 1:
                t = s - 1 + 2 * (s % 2)
                to = (t, c) if 0 <= t < n_slabs else (s, c ^ 1)
            else:
                t = c - 1 + 2 * (c % 2)
                to = (s, t) if 0 <= t < n_cells else (s ^ 1, c)
            pairs.append((s * n_cells + c, to[0] * n_cells + to[1]))
    return lax.ppermute(x, ("slab", "cell"), pairs)


def exchange(sends):
    return [swap(sends[slot], slot) for slot in EARLY + LATE]


def local(positions, burgers, mobility, near_list, near_count, send_list):
    mobility = mobility.reshape(BLOCKS, LANES)
    flat = shape(*positions.shape)
    block = shape(3, BLOCKS, LANES)
    send = shape(3, GHOST, LANES)

    positions = positions.reshape(block.shape)
    burgers = burgers.reshape(block.shape)
    numbers = (
        jnp.pad(near_list.T, ((0, 16 - NEAR), (0, LANES - BLOCKS)))
        + jnp.pad(near_count[None], ((NEAR, 15 - NEAR), (0, LANES - BLOCKS)))
        + jnp.pad(send_list, ((8, 4), (0, LANES - GHOST)))
    )

    places, scalars, *sends = pl.pallas_call(
        pack_kernel,
        out_shape=[block, shape(16, LANES, dtype=jnp.int32)] + [shape(6, GHOST, LANES)] * 4,
        in_specs=[smem, vmem, vmem, vmem],
        out_specs=[vmem] * 6,
        compiler_params=params,
        name="pack",
    )(numbers, numbers, positions, burgers)
    ghosts = [swap(x, slot) for x, slot in zip(sends, (3, 0, 2, 1))]

    shares, control = pl.pallas_call(
        far_kernel,
        out_shape=[shape(EXT, LANES), shape(CONTROL, dtype=jnp.int32)],
        in_specs=[smem, vmem, vmem],
        out_specs=[vmem, smem],
        scratch_shapes=[
            pltpu.VMEM((32, 2 * EXT), f32),
            pltpu.VMEM((BLOCKS // 4, LANES, LANES), f32),
            pltpu.VMEM((BLOCKS // 4, LANES, LANES), bf16),
            pltpu.VMEM((4, LANES, EXT), bf16),
            pltpu.VMEM((4, 2 * LANES, 2 * EXT), bf16),
            pltpu.VMEM((4, 2 * LANES, 2 * EXT), bf16),
        ],
        compiler_params=params,
        cost_estimate=cost(20e9),
        name="far",
    )(scalars, places, burgers)
    shares = lax.all_to_all(shares, ("slab", "cell"), 0, 0, tiled=True)

    near, burg = pl.pallas_call(
        first_kernel,
        out_shape=[block, shape((EXT + 1) * 8, LANES)],
        in_specs=[smem] + [vmem] * 6,
        out_specs=[vmem] * 2,
        scratch_shapes=near_scratch
        + [parts_scratch, pltpu.VMEM(right_shape, bf16), pltpu.VMEM(acc_shape, f32)],
        compiler_params=params,
        cost_estimate=cost(20e9),
        name="near_first",
    )(control, places, burgers, *ghosts)

    expansion, moved, now, *sends = pl.pallas_call(
        start_kernel,
        out_shape=[shape(8, LANES), block, block] + [send] * 4,
        in_specs=[smem] + [vmem] * 4,
        out_specs=[vmem] * 7,
        compiler_params=params,
        name="start",
    )(control, shares, near, places, mobility)

    def evaluate(kernel, out_shape, name, *more):
        ghosts = exchange(sends)
        right, acc = pl.pallas_call(
            early_kernel,
            out_shape=[shape(*right_shape, dtype=bf16), shape(*acc_shape)],
            in_specs=[smem] + [vmem] * 3,
            out_specs=[vmem] * 2,
            scratch_shapes=near_scratch + [parts_scratch],
            compiler_params=params,
            cost_estimate=cost(20e9),
            name="near_early",
        )(control, now, *ghosts[: len(EARLY)], burg)
        return pl.pallas_call(
            kernel,
            out_shape=out_shape,
            in_specs=[smem] + [vmem] * (6 + len(LATE) + len(more)),
            out_specs=jax.tree.map(lambda _: vmem, out_shape),
            scratch_shapes=near_scratch + [pltpu.VMEM(acc_shape, f32)],
            compiler_params=params,
            cost_estimate=cost(10e9),
            name=name,
        )(control, expansion, now, *ghosts[len(EARLY) :], burg, right, acc, mobility, *more)

    for substep in range(1, SUBSTEPS):
        final = substep == SUBSTEPS - 1
        moved, now, *sends = evaluate(
            functools.partial(step_kernel, final),
            [flat if final else block, block] + [send] * 4,
            "near_step",
            places,
            moved,
        )
    velocity = evaluate(last_kernel, flat, "near_last")
    return moved, velocity


def solution(mesh):
    return jax.shard_map(
        local,
        mesh=mesh,
        in_specs=(
            P(None, ("slab", "cell")),
            P(None, ("slab", "cell")),
            P(("slab", "cell")),
            P(("slab", "cell"), None),
            P(("slab", "cell")),
            P(None, ("slab", "cell")),
        ),
        out_specs=(P(None, ("slab", "cell")), P(None, ("slab", "cell"))),
        check_vma=False,
    )
```

```python
import functools

import jax
import jax.numpy as jnp
from jax import lax
from jax.experimental import pallas as pl
from jax.experimental.pallas import tpu as pltpu
from jax.sharding import PartitionSpec as P

SUBSTEPS = 4
BLOCKS = 64
LANES = 128
NEAR = 6
GHOST = 48
EXT = 256
GROUP = 8
LEAD = GROUP
TAIL = 56
AT_SENDS = 8
AT_PAIRS = AT_SENDS + 4 * GHOST + LEAD
LIST = BLOCKS * NEAR + TAIL + LEAD
CONTROL = AT_PAIRS + 2 * LIST + 8
EARLY, LATE = (3,), (0, 2, 1)
SHARE = 9

core_sq = 0.04
far_sq = 1.0
time_step = 0.2

f32 = jnp.float32
bf16 = jnp.bfloat16

vmem = pl.BlockSpec(memory_space=pltpu.VMEM)
params = pltpu.CompilerParams(vmem_limit_bytes=40 * 2**20)


def round_bf16(x):
    return x.astype(bf16).astype(f32)


def split2(x):
    high = x.astype(bf16)
    return high, (x - high.astype(f32)).astype(bf16)


def split3(x):
    high = round_bf16(x)
    rest = x - high
    mid = round_bf16(rest)
    return high, mid, round_bf16(rest - mid)


def parity():
    return lax.axis_index("slab") % 2, lax.axis_index("cell") % 2


def send_rows():
    odd_slab, odd_cell = parity()
    return odd_slab, 1 - odd_slab, 3 - odd_cell, 2 + odd_cell


def slot_moves():
    odd_slab, odd_cell = parity()
    return (
        GHOST * (1 - odd_slab),
        GHOST * (odd_slab - 1),
        GHOST * odd_cell,
        -GHOST * odd_cell,
    )


def slot_shifts():
    odd_slab, odd_cell = parity()
    along_slab = (1 - 2 * odd_slab).astype(f32)
    along_cell = (1 - 2 * odd_cell).astype(f32)
    return (0, along_slab), (0, -along_slab), (1, -along_cell), (1, along_cell)


def slot_exists():
    out = []
    for axis in ("slab", "cell"):
        i = lax.axis_index(axis)
        partner = i - 1 + 2 * (i % 2)
        out.append((partner >= 0) & (partner < lax.axis_size(axis)))
    return None, out[0], out[1], None


def fill_sends(block_of, sources, sends):
    def body(n, carry):
        for d in sends:
            block = block_of(d, n)
            for a, (ref, index) in enumerate(sources):
                sends[d][a, pl.ds(n, 1), :] = ref[index, pl.ds(block, 1), :]
        return carry

    lax.fori_loop(0, GHOST, body, 0, unroll=4)


def send_now(control, now, sends):
    fill_sends(
        lambda d, n: control[AT_SENDS + GHOST * d + n],
        [(now, k) for k in range(3)],
        dict(enumerate(sends)),
    )


def centre_of():
    slab = lax.axis_index("slab").astype(f32)
    cell = lax.axis_index("cell").astype(f32)
    return slab, cell


def list_pairs(near_list, near_count):
    segment = (near_list + (GHOST - BLOCKS)) // GHOST
    exists = {0: None, 3: None}
    exists[1], exists[2] = slot_exists()[1:3]
    odd_slab, odd_cell = parity()
    sides = (
        (odd_slab == 1) | exists[1],
        (odd_slab == 0) | exists[1],
        (odd_cell == 1) | exists[2],
        (odd_cell == 0) | exists[2],
    )
    slot = lax.broadcasted_iota(jnp.int32, near_list.shape, 0)
    block = lax.broadcasted_iota(jnp.int32, near_list.shape, 1)
    live = jnp.where(slot < near_count, 1, 0)
    moved = near_list
    for i, (move, there) in enumerate(zip(slot_moves(), sides)):
        mine = segment == 1 + i
        moved = moved + jnp.where(mine, move, 0)
        live = jnp.where(mine, live * there.astype(jnp.int32), live)
    late = jnp.where(moved >= BLOCKS, live, 0)
    for d in EARLY:
        first = BLOCKS + GHOST * d
        late = jnp.where((moved >= first) & (moved < first + GHOST), 0, late)
    earlier = lax.broadcasted_iota(jnp.int32, (BLOCKS, BLOCKS), 0) < lax.broadcasted_iota(
        jnp.int32, (BLOCKS, BLOCKS), 1
    )
    place = jnp.full(near_list.shape, 2 * LIST, jnp.int32)
    amounts = []
    for i, mine in enumerate((live - late, late)):
        rows = [mine[n : n + 1] for n in range(NEAR)]
        before = [jnp.zeros_like(rows[0])]
        for row in rows:
            before.append(before[-1] + row)
        amount = before.pop().astype(f32)
        offset = jnp.dot(
            jnp.broadcast_to(amount, (8, BLOCKS)),
            jnp.where(earlier, 1.0, 0.0),
            preferred_element_type=f32,
        )[:1]
        at = jnp.concatenate([offset.astype(jnp.int32) + x for x in before], axis=0)
        place = jnp.where(mine > 0, at + LIST * i, place)
        amounts.append(jnp.sum(amount, axis=1, keepdims=True).astype(jnp.int32))
    words = 2**15 * place + 2**SHARE * block + moved
    return words, amounts


def pack_kernel(
    numbers, positions, burgers, places, scalars, s3, s0, s2, s1, numbers_smem, sem
):
    copy = pltpu.make_async_copy(numbers, numbers_smem, sem)
    copy.start()
    slab, cell = centre_of()
    for k, by in enumerate((slab + 0.5, cell + 0.5, 0.5)):
        places[k] = positions[k] - by
    scalars[...] = jnp.zeros_like(scalars)
    words, amounts = list_pairs(numbers[:NEAR, :BLOCKS], numbers[NEAR : NEAR + 1, :BLOCKS])
    scalars[:NEAR, :BLOCKS] = words
    for i in range(2):
        scalars[NEAR + i : NEAR + i + 1, :] = jnp.broadcast_to(amounts[i], (1, LANES))
    rows = send_rows()
    for d in range(4):
        first = 2 * (d // 2)
        scalars[8 + d : 9 + d, :] = jnp.where(
            rows[d] == first, numbers[8 + first : 9 + first, :], numbers[9 + first : 10 + first, :]
        )
    sources = [(places, k) for k in range(3)] + [(burgers, a) for a in range(3)]
    copy.wait()
    fill_sends(lambda d, n: numbers_smem[8 + rows[d], n], sources, {0: s0, 1: s1, 2: s2, 3: s3})


def put_rows(out, k, value):
    for b in range(BLOCKS):
        out[k : k + 1, LANES * b : LANES * b + LANES] = value[b : b + 1]


def halves(tile):
    low = lax.broadcasted_iota(jnp.int32, (8, LANES), 0) < 4
    turned = pltpu.roll(tile, 4, 0)
    return jnp.where(low, tile, turned), jnp.where(low, turned, tile)


def pair_rows(values):
    low = lax.broadcasted_iota(jnp.int32, (8, LANES), 0) < 4
    rows = [
        x if x is y else jnp.where(low, x, y) for x, y in zip(values[0::2], values[1::2])
    ]
    rows += [jnp.zeros((8, LANES), f32)] * (LANES // 8 - len(rows))
    return jnp.concatenate(rows, axis=0)


def far_kernel(
    scalars_in, places, burgers, out, control_out, acc, rows, cols, apart_by, w_even, w_odd,
    scalars, control, sems
):
    copy = pltpu.make_async_copy(scalars_in, scalars, sems.at[0])
    copy.start()
    for i in range(LEAD):
        control[AT_PAIRS - LEAD + i] = EXT
        control[AT_PAIRS + LIST - LEAD + i] = EXT
    for tile in range(BLOCKS // 8):
        p = [halves(places[k, 8 * tile : 8 * tile + 8, :]) for k in range(3)]
        burg = [halves(burgers[a, 8 * tile : 8 * tile + 8, :]) for a in range(3)]
        for half in range(2):
            here = [x[half] for x in p]
            sources = [x[half] for x in burg]
            moments = [x * y for x in here for y in sources]
            values = []
            for group in (sources, moments):
                high = [round_bf16(x) for x in group]
                values += high + [x - h for x, h in zip(group, high)]
            rows[2 * tile + half] = pair_rows(values)
            one = jnp.ones((8, LANES), f32)
            square = sum(x * x for x in here) + far_sq
            values = [part for x in (here[0], here[1], square) for part in split3(x)]
            cols[2 * tile + half] = pair_rows(values + [one, one, one]).T.astype(bf16)
    acc[...] = jnp.zeros_like(acc)
    w_odd[...] = jnp.zeros_like(w_odd)
    slab, cell = centre_of()
    target = lax.broadcasted_iota(jnp.int32, (1, EXT), 1)
    apart = [(target // 32).astype(f32) - slab, (target % 32).astype(f32) - cell]
    square = apart[0] * apart[0] + apart[1] * apart[1]
    square_high = round_bf16(square)
    place = lax.broadcasted_iota(jnp.int32, (LANES, EXT), 0)
    values = jnp.where(place < 36, 1.0, 0.0)
    for first, last, x in (
        (0, 12, -2.0 * apart[0]),
        (12, 24, -2.0 * apart[1]),
        (36, 40, square_high),
        (40, 44, square - square_high),
    ):
        values = jnp.where((place >= first) & (place < last), x, values)
    for g in range(4):
        apart_by[g] = jnp.where(place % 4 == g, values, 0.0).astype(bf16)

    def sums(group, g, w):
        mine = rows[group, pl.ds(g, 32, stride=4), :].astype(bf16)
        acc[...] += jnp.dot(
            jnp.concatenate([mine, mine], axis=1), w[g], preferred_element_type=f32
        )

    def half(group, w_now, w_before):
        for i in range(4):
            for slot in range(NEAR):
                word = scalars[slot, 4 * group + i]
                at = lax.shift_right_logical(word, 15)
                control[AT_PAIRS + at] = word & (2**15 - 1)
        for d in range(4):
            for i in range(3):
                n = 3 * group + i
                control[AT_SENDS + GHOST * d + n] = scalars[8 + d, n]
        for g in range(4):
            sums(jnp.maximum(group - 1, 0), g, w_before)
            r = lax.rsqrt(jnp.dot(cols[group], apart_by[g], preferred_element_type=f32))
            r2 = r * r
            w3 = r2 * r
            for k, w in enumerate((w3, w3 * r2)):
                high, low = split2(w)
                w_now[g, :LANES, EXT * k : EXT * k + EXT] = high
                w_now[g, LANES:, EXT * k : EXT * k + EXT] = low

    copy.wait()

    def body(step, carry):
        half(2 * step, w_even, w_odd)
        half(2 * step + 1, w_odd, w_even)
        return carry

    lax.fori_loop(0, BLOCKS // 8, body, 0)
    amounts = [scalars[NEAR, 0], scalars[NEAR + 1, 0]]
    for k in range(2):
        for i in range(TAIL):
            control[AT_PAIRS + LIST * k + amounts[k] + i] = EXT
        control[k] = amounts[k]
    copy = pltpu.make_async_copy(control, control_out, sems.at[1])
    copy.start()
    for g in range(4):
        sums(BLOCKS // 4 - 1, g, w_odd)

    apart = apart + [jnp.zeros((1, EXT), f32)]

    def row(k, i):
        return acc[i : i + 1, EXT * k : EXT * k + EXT]

    direct = [row(0, a) + row(0, 3 + a) for a in range(3)]
    total = [row(1, a) + row(1, 3 + a) for a in range(3)]
    gradient = []
    for a in range(3):
        for k in range(3):
            moment = row(1, 6 + 3 * k + a) + row(1, 15 + 3 * k + a)
            gradient.append(-3.0 * (apart[k] * total[a] - moment))
    zero = jnp.zeros((LANES - 12, 2 * LANES), f32)
    values = jnp.concatenate(direct + gradient + [zero], axis=0)
    out[...] = jnp.concatenate([values[:, :LANES].T, values[:, LANES:].T], axis=0)
    copy.wait()


def tile_of(own, ghosts, index, tile):
    if tile < BLOCKS // 8:
        return own[index, 8 * tile : 8 * tile + 8, :]
    d, n = divmod(tile - BLOCKS // 8, GHOST // 8)
    return ghosts[d][index, 8 * n : 8 * n + 8, :]


def tiles_of(slots):
    n = GHOST // 8
    return [BLOCKS // 8 + n * d + i for d in slots for i in range(n)]


def prepare_sources(own, ghosts, tiles, left):
    shift = slot_shifts()
    one = jnp.ones((8, LANES), f32)
    low = lax.broadcasted_iota(jnp.int32, (8, LANES), 0) < 4

    for tile in tiles:
        p = [tile_of(own, ghosts, k, tile) for k in range(3)]
        if tile >= BLOCKS // 8:
            k, by = shift[(tile - BLOCKS // 8) // (GHOST // 8)]
            p[k] = p[k] + by
        parts_of = [split3(x) for x in p]
        parts_of.append(split3(p[0] * p[0] + p[1] * p[1] + p[2] * p[2]))
        turned = [[pltpu.roll(x, 4, 0) for x in group] for group in parts_of]
        for half in range(2):
            first, second = (parts_of, turned) if half == 0 else (turned, parts_of)
            values = []
            for (h, m, _), (h2, m2, l2) in zip(first[:3], second[:3]):
                values += [
                    jnp.where(low, h, h2),
                    jnp.where(low, m, m2),
                    jnp.where(low, h, l2),
                ]
            h, _, l = first[3]
            values += [jnp.where(low, h, second[3][1]), jnp.where(low, l, one), one]
            values += [jnp.zeros((8, LANES), f32)] * (LANES // 8 - len(values))
            left[2 * tile + half] = jnp.concatenate(values, axis=0).T.astype(bf16)
    left[EXT // 4] = jnp.zeros((LANES, LANES), bf16)


def prepare_targets(own, parts, right):
    one = jnp.ones((8, LANES), f32)
    low = lax.broadcasted_iota(jnp.int32, (8, LANES), 0) < 4

    x = [own[k] for k in range(3)]
    for k in range(3):
        for i, part in enumerate(split3(-2.0 * x[k])):
            parts[3 * k + i] = part
    for i, part in enumerate(split3(x[0] * x[0] + x[1] * x[1] + x[2] * x[2] + core_sq)):
        parts[9 + i] = part
    for b in range(BLOCKS):
        def row(i):
            return jnp.broadcast_to(parts[i, b : b + 1, :], (8, LANES))

        rows = []
        for k in range(3):
            h, m, l = row(3 * k), row(3 * k + 1), row(3 * k + 2)
            high_mid = jnp.where(low, h, m)
            rows += [high_mid, high_mid, jnp.where(low, l, h)]
        rows += [one, jnp.where(low, one, row(9)), jnp.where(low, row(10), row(11))]
        for i in range(6):
            right[b, i] = jnp.concatenate(rows[2 * i : 2 * i + 2], axis=0).astype(bf16)
        right[b, 6:] = jnp.zeros((2, 16, LANES), bf16)


def add_pairs(control, which, burg, left, right, mask, acc, k_even, k_odd):
    place = lax.broadcasted_iota(jnp.int32, (16, LANES), 0) % 4
    for g in range(4):
        mask[g] = jnp.where(place == g, 1.0, 0.0).astype(bf16)

    k_odd[...] = jnp.zeros_like(k_odd)

    def pair(i):
        word = control[AT_PAIRS + LIST * which + i]
        return lax.shift_right_logical(word, SHARE), word & (2**SHARE - 1)

    def sums(step, g, k_before):
        i = step * GROUP + g
        (b0, t0), (b1, t1) = pair(i), pair(i + 1)
        rows = jnp.concatenate(
            [burg[pl.ds(pl.multiple_of(8 * t, 8), 8), :] for t in (t0, t1)], axis=0
        ).astype(bf16)
        both = jnp.dot(
            jnp.concatenate([rows, rows], axis=1),
            jnp.concatenate([k_before[g], k_before[g + 1]], axis=1),
            preferred_element_type=f32,
        )
        at = pl.ds(pl.multiple_of(8 * b0, 8), 8)
        acc[at, :] = acc[at, :] + both[:8, :LANES]
        at = pl.ds(pl.multiple_of(8 * b1, 8), 8)
        acc[at, :] = acc[at, :] + both[8:, LANES:]

    def half(step, k_now, k_before):
        for g in range(GROUP):
            if g % 2 == 0:
                sums(step - 1, g, k_before)
            b, t = pair(step * GROUP + g)
            features = (right[b] * mask[t & 3][None]).reshape(LANES, LANES)
            near_sq = jnp.dot(
                left[lax.shift_right_logical(t, 2)], features, preferred_element_type=f32
            )
            near_sq = jnp.maximum(near_sq, core_sq)
            r = lax.rsqrt(near_sq)
            q = lax.rsqrt(near_sq + (far_sq - core_sq))
            high, low = split2(r * r * r - q * q * q)
            k_now[g, :LANES, :] = high
            k_now[g, LANES:, :] = low

    def body(step, carry):
        half(2 * step, k_even, k_odd)
        half(2 * step + 1, k_odd, k_even)
        return carry

    steps = (control[which] + 2 * GROUP - 1) // (2 * GROUP)
    lax.fori_loop(0, steps, body, 0)
    for g in range(0, GROUP, 2):
        sums(2 * steps - 1, g, k_odd)


def component(acc, a):
    return acc[pl.ds(a, BLOCKS, stride=8), :] + acc[pl.ds(3 + a, BLOCKS, stride=8), :]


parts_scratch = pltpu.VMEM((12, BLOCKS, LANES), f32)
right_shape = (BLOCKS, 8, 16, LANES)
acc_shape = (BLOCKS * 8, LANES)
control_scratch = [pltpu.SMEM((CONTROL,), jnp.int32), pltpu.SemaphoreType.DMA]
near_scratch = control_scratch + [
    pltpu.VMEM((EXT // 4 + 1, LANES, LANES), bf16),
    pltpu.VMEM((4, 16, LANES), bf16),
    pltpu.VMEM((GROUP, 2 * LANES, LANES), bf16),
    pltpu.VMEM((GROUP, 2 * LANES, LANES), bf16),
]


def total_force(expansion, near, places):
    out = []
    for a in range(3):
        far = expansion[0:1, a : a + 1]
        for k in range(3):
            far = far + expansion[0:1, 3 + 3 * a + k : 4 + 3 * a + k] * places[k]
        out.append(near[a] + far)
    return out


def first_kernel(
    control_in, own, burgers, g3, g0, g2, g1, near, burg, control, sem, left, mask, k_even, k_odd, parts, right, acc
):
    copy = pltpu.make_async_copy(control_in, control, sem)
    copy.start()
    ghosts = (g0, g1, g2, g3)
    exists = slot_exists()
    burg[...] = jnp.zeros_like(burg)
    for tile in range(EXT // 8):
        for a in range(3):
            if tile < BLOCKS // 8:
                value = burgers[a, 8 * tile : 8 * tile + 8, :]
            else:
                d = (tile - BLOCKS // 8) // (GHOST // 8)
                value = tile_of(None, ghosts, 3 + a, tile)
                if exists[d] is not None:
                    value = jnp.where(exists[d], value, 0.0)
            high = round_bf16(value)
            burg[pl.ds(tile * 64 + a, 8, stride=8), :] = high
            burg[pl.ds(tile * 64 + 3 + a, 8, stride=8), :] = value - high
    prepare_sources(own, ghosts, range(EXT // 8), left)
    prepare_targets(own, parts, right)
    acc[...] = jnp.zeros_like(acc)
    copy.wait()
    for which in range(2):
        add_pairs(control, which, burg, left, right, mask, acc, k_even, k_odd)
    for a in range(3):
        near[a] = component(acc, a)


def start_kernel(
    control_in, shares, near, places, mobility, expansion, moved, now, s0, s1, s2, s3, control, sem
):
    copy = pltpu.make_async_copy(control_in, control, sem)
    copy.start()
    expansion[...] = jnp.broadcast_to(jnp.sum(shares[...], axis=0, keepdims=True), (8, LANES))
    p = [places[k] for k in range(3)]
    force = total_force(expansion[...], [near[a] for a in range(3)], p)
    for a in range(3):
        step = (time_step * mobility[...]) * force[a]
        moved[a] = step
        now[a] = p[a] + step
    copy.wait()
    send_now(control, now, (s0, s1, s2, s3))


def early_kernel(
    control_in, own, g3, burg, right, acc, control, sem, left, mask, k_even, k_odd, parts
):
    copy = pltpu.make_async_copy(control_in, control, sem)
    copy.start()
    ghosts = (None, None, None, g3)
    prepare_sources(own, ghosts, list(range(BLOCKS // 8)) + tiles_of(EARLY), left)
    prepare_targets(own, parts, right)
    acc[...] = jnp.zeros_like(acc)
    copy.wait()
    add_pairs(control, 0, burg, left, right, mask, acc, k_even, k_odd)


def late_force(
    control_in, expansion, own, g0, g2, g1, burg, right, acc_in, control, sem, left, mask, k_even, k_odd, acc
):
    copy = pltpu.make_async_copy(control_in, control, sem)
    copy.start()
    prepare_sources(own, (g0, g1, g2, None), tiles_of(LATE), left)
    acc[...] = acc_in[...]
    copy.wait()
    add_pairs(control, 1, burg, left, right, mask, acc, k_even, k_odd)
    return total_force(
        expansion[...], [component(acc, a) for a in range(3)], [own[k] for k in range(3)]
    )


def step_kernel(
    final, control, expansion, own, g0, g2, g1, burg, right, acc_in, mobility, places, moved,
    new_moved, now, s0, s1, s2, s3, *scratch
):
    force = late_force(control, expansion, own, g0, g2, g1, burg, right, acc_in, *scratch)
    for a in range(3):
        total = moved[a] + (time_step * mobility[...]) * force[a]
        if final:
            put_rows(new_moved, a, total)
        else:
            new_moved[a] = total
        now[a] = places[a] + total
    send_now(scratch[0], now, (s0, s1, s2, s3))


def last_kernel(
    control, expansion, own, g0, g2, g1, burg, right, acc_in, mobility, velocity, *scratch
):
    force = late_force(control, expansion, own, g0, g2, g1, burg, right, acc_in, *scratch)
    for a in range(3):
        put_rows(velocity, a, mobility[...] * force[a])


def cost(flops):
    return pl.CostEstimate(flops=int(flops), bytes_accessed=2**20, transcendentals=0)


def shape(*dims, dtype=f32):
    return jax.ShapeDtypeStruct(dims, dtype)


def swap(x, slot):
    n_slabs, n_cells = lax.axis_size("slab"), lax.axis_size("cell")
    pairs = []
    for s in range(n_slabs):
        for c in range(n_cells):
            if slot == 0:
                to = (s ^ 1, c)
            elif slot == 3:
                to = (s, c ^ 1)
            elif slot == 1:
                t = s - 1 + 2 * (s % 2)
                to = (t, c) if 0 <= t < n_slabs else (s, c ^ 1)
            else:
                t = c - 1 + 2 * (c % 2)
                to = (s, t) if 0 <= t < n_cells else (s ^ 1, c)
            pairs.append((s * n_cells + c, to[0] * n_cells + to[1]))
    return lax.ppermute(x, ("slab", "cell"), pairs)


def exchange(sends):
    return [swap(sends[slot], slot) for slot in EARLY + LATE]


def local(positions, burgers, mobility, near_list, near_count, send_list):
    mobility = mobility.reshape(BLOCKS, LANES)
    flat = shape(*positions.shape)
    block = shape(3, BLOCKS, LANES)
    send = shape(3, GHOST, LANES)

    positions = positions.reshape(block.shape)
    burgers = burgers.reshape(block.shape)
    numbers = (
        jnp.pad(near_list.T, ((0, 16 - NEAR), (0, LANES - BLOCKS)))
        + jnp.pad(near_count[None], ((NEAR, 15 - NEAR), (0, LANES - BLOCKS)))
        + jnp.pad(send_list, ((8, 4), (0, LANES - GHOST)))
    )

    places, scalars, *sends = pl.pallas_call(
        pack_kernel,
        out_shape=[block, shape(16, LANES, dtype=jnp.int32)] + [shape(6, GHOST, LANES)] * 4,
        in_specs=[vmem] * 3,
        out_specs=[vmem] * 6,
        scratch_shapes=[pltpu.SMEM((16, LANES), jnp.int32), pltpu.SemaphoreType.DMA],
        compiler_params=params,
        name="pack",
    )(numbers, positions, burgers)
    ghosts = [swap(x, slot) for x, slot in zip(sends, (3, 0, 2, 1))]

    shares, control = pl.pallas_call(
        far_kernel,
        out_shape=[shape(EXT, LANES), shape(CONTROL, dtype=jnp.int32)],
        in_specs=[vmem] * 3,
        out_specs=[vmem] * 2,
        scratch_shapes=[
            pltpu.VMEM((32, 2 * EXT), f32),
            pltpu.VMEM((BLOCKS // 4, LANES, LANES), f32),
            pltpu.VMEM((BLOCKS // 4, LANES, LANES), bf16),
            pltpu.VMEM((4, LANES, EXT), bf16),
            pltpu.VMEM((4, 2 * LANES, 2 * EXT), bf16),
            pltpu.VMEM((4, 2 * LANES, 2 * EXT), bf16),
            pltpu.SMEM((16, LANES), jnp.int32),
            pltpu.SMEM((CONTROL,), jnp.int32),
            pltpu.SemaphoreType.DMA((2,)),
        ],
        compiler_params=params,
        cost_estimate=cost(20e9),
        name="far",
    )(scalars, places, burgers)
    shares = lax.all_to_all(shares, ("slab", "cell"), 0, 0, tiled=True)

    near, burg = pl.pallas_call(
        first_kernel,
        out_shape=[block, shape((EXT + 1) * 8, LANES)],
        in_specs=[vmem] * 7,
        out_specs=[vmem] * 2,
        scratch_shapes=near_scratch
        + [parts_scratch, pltpu.VMEM(right_shape, bf16), pltpu.VMEM(acc_shape, f32)],
        compiler_params=params,
        cost_estimate=cost(20e9),
        name="near_first",
    )(control, places, burgers, *ghosts)

    expansion, moved, now, *sends = pl.pallas_call(
        start_kernel,
        out_shape=[shape(8, LANES), block, block] + [send] * 4,
        in_specs=[vmem] * 5,
        out_specs=[vmem] * 7,
        scratch_shapes=control_scratch,
        compiler_params=params,
        name="start",
    )(control, shares, near, places, mobility)

    def evaluate(kernel, out_shape, name, *more):
        ghosts = exchange(sends)
        right, acc = pl.pallas_call(
            early_kernel,
            out_shape=[shape(*right_shape, dtype=bf16), shape(*acc_shape)],
            in_specs=[vmem] * 4,
            out_specs=[vmem] * 2,
            scratch_shapes=near_scratch + [parts_scratch],
            compiler_params=params,
            cost_estimate=cost(20e9),
            name="near_early",
        )(control, now, *ghosts[: len(EARLY)], burg)
        return pl.pallas_call(
            kernel,
            out_shape=out_shape,
            in_specs=[vmem] * (7 + len(LATE) + len(more)),
            out_specs=jax.tree.map(lambda _: vmem, out_shape),
            scratch_shapes=near_scratch + [pltpu.VMEM(acc_shape, f32)],
            compiler_params=params,
            cost_estimate=cost(10e9),
            name=name,
        )(control, expansion, now, *ghosts[len(EARLY) :], burg, right, acc, mobility, *more)

    for substep in range(1, SUBSTEPS):
        final = substep == SUBSTEPS - 1
        moved, now, *sends = evaluate(
            functools.partial(step_kernel, final),
            [flat if final else block, block] + [send] * 4,
            "near_step",
            places,
            moved,
        )
    velocity = evaluate(last_kernel, flat, "near_last")
    return moved, velocity


def solution(mesh):
    return jax.shard_map(
        local,
        mesh=mesh,
        in_specs=(
            P(None, ("slab", "cell")),
            P(None, ("slab", "cell")),
            P(("slab", "cell")),
            P(("slab", "cell"), None),
            P(("slab", "cell")),
            P(None, ("slab", "cell")),
        ),
        out_specs=(P(None, ("slab", "cell")), P(None, ("slab", "cell"))),
        check_vma=False,
    )
```

```python
import functools

import jax
import jax.numpy as jnp
from jax import lax
from jax.experimental import pallas as pl
from jax.experimental.pallas import tpu as pltpu
from jax.sharding import PartitionSpec as P

SUBSTEPS = 4
BLOCKS = 64
LANES = 128
NEAR = 6
GHOST = 48
EXT = 256
GROUP = 8
LEAD = GROUP
TAIL = 56
AT_SENDS = 8
AT_PAIRS = AT_SENDS + 4 * GHOST + LEAD
LIST = BLOCKS * NEAR + TAIL + LEAD
CONTROL = AT_PAIRS + 2 * LIST + 8
EARLY, LATE = (3,), (0, 2, 1)
SHARE = 9

core_sq = 0.04
far_sq = 1.0
time_step = 0.2

f32 = jnp.float32
bf16 = jnp.bfloat16

vmem = pl.BlockSpec(memory_space=pltpu.VMEM)
params = pltpu.CompilerParams(vmem_limit_bytes=40 * 2**20)


def round_bf16(x):
    return x.astype(bf16).astype(f32)


def split2(x):
    high = x.astype(bf16)
    return high, (x - high.astype(f32)).astype(bf16)


def split3(x):
    high = round_bf16(x)
    rest = x - high
    mid = round_bf16(rest)
    return high, mid, round_bf16(rest - mid)


def slab_index():
    return lax.axis_index("slab")


def cell_index():
    return 2 * lax.axis_index("chip") + lax.axis_index("core")


def n_slabs_cells():
    return lax.axis_size("slab"), 2 * lax.axis_size("chip")


def parity():
    return slab_index() % 2, cell_index() % 2


def send_rows():
    odd_slab, odd_cell = parity()
    return odd_slab, 1 - odd_slab, 3 - odd_cell, 2 + odd_cell


def slot_moves():
    odd_slab, odd_cell = parity()
    return (
        GHOST * (1 - odd_slab),
        GHOST * (odd_slab - 1),
        GHOST * odd_cell,
        -GHOST * odd_cell,
    )


def slot_shifts():
    odd_slab, odd_cell = parity()
    along_slab = (1 - 2 * odd_slab).astype(f32)
    along_cell = (1 - 2 * odd_cell).astype(f32)
    return (0, along_slab), (0, -along_slab), (1, -along_cell), (1, along_cell)


def slot_exists():
    out = []
    for i, n in zip((slab_index(), cell_index()), n_slabs_cells()):
        partner = i - 1 + 2 * (i % 2)
        out.append((partner >= 0) & (partner < n))
    return None, out[0], out[1], None


def fill_sends(block_of, sources, sends):
    def body(n, carry):
        for d in sends:
            block = block_of(d, n)
            for a, (ref, index) in enumerate(sources):
                sends[d][a, pl.ds(n, 1), :] = ref[index, pl.ds(block, 1), :]
        return carry

    lax.fori_loop(0, GHOST, body, 0, unroll=4)


def send_now(control, now, sends):
    fill_sends(
        lambda d, n: control[AT_SENDS + GHOST * d + n],
        [(now, k) for k in range(3)],
        dict(enumerate(sends)),
    )


def centre_of():
    return slab_index().astype(f32), cell_index().astype(f32)


def list_pairs(near_list, near_count):
    segment = (near_list + (GHOST - BLOCKS)) // GHOST
    exists = {0: None, 3: None}
    exists[1], exists[2] = slot_exists()[1:3]
    odd_slab, odd_cell = parity()
    sides = (
        (odd_slab == 1) | exists[1],
        (odd_slab == 0) | exists[1],
        (odd_cell == 1) | exists[2],
        (odd_cell == 0) | exists[2],
    )
    slot = lax.broadcasted_iota(jnp.int32, near_list.shape, 0)
    block = lax.broadcasted_iota(jnp.int32, near_list.shape, 1)
    live = jnp.where(slot < near_count, 1, 0)
    moved = near_list
    for i, (move, there) in enumerate(zip(slot_moves(), sides)):
        mine = segment == 1 + i
        moved = moved + jnp.where(mine, move, 0)
        live = jnp.where(mine, live * there.astype(jnp.int32), live)
    late = jnp.where(moved >= BLOCKS, live, 0)
    for d in EARLY:
        first = BLOCKS + GHOST * d
        late = jnp.where((moved >= first) & (moved < first + GHOST), 0, late)
    earlier = lax.broadcasted_iota(jnp.int32, (BLOCKS, BLOCKS), 0) < lax.broadcasted_iota(
        jnp.int32, (BLOCKS, BLOCKS), 1
    )
    place = jnp.full(near_list.shape, 2 * LIST, jnp.int32)
    amounts = []
    for i, mine in enumerate((live - late, late)):
        rows = [mine[n : n + 1] for n in range(NEAR)]
        before = [jnp.zeros_like(rows[0])]
        for row in rows:
            before.append(before[-1] + row)
        amount = before.pop().astype(f32)
        offset = jnp.dot(
            jnp.broadcast_to(amount, (8, BLOCKS)),
            jnp.where(earlier, 1.0, 0.0),
            preferred_element_type=f32,
        )[:1]
        at = jnp.concatenate([offset.astype(jnp.int32) + x for x in before], axis=0)
        place = jnp.where(mine > 0, at + LIST * i, place)
        amounts.append(jnp.sum(amount, axis=1, keepdims=True).astype(jnp.int32))
    words = 2**15 * place + 2**SHARE * block + moved
    return words, amounts


def pack_kernel(
    numbers, positions, burgers, places, scalars, s3, s0, s2, s1, numbers_smem, sem
):
    copy = pltpu.make_async_copy(numbers, numbers_smem, sem)
    copy.start()
    slab, cell = centre_of()
    for k, by in enumerate((slab + 0.5, cell + 0.5, 0.5)):
        places[k] = positions[k] - by
    scalars[...] = jnp.zeros_like(scalars)
    words, amounts = list_pairs(numbers[:NEAR, :BLOCKS], numbers[NEAR : NEAR + 1, :BLOCKS])
    scalars[:NEAR, :BLOCKS] = words
    for i in range(2):
        scalars[NEAR + i : NEAR + i + 1, :] = jnp.broadcast_to(amounts[i], (1, LANES))
    rows = send_rows()
    for d in range(4):
        first = 2 * (d // 2)
        scalars[8 + d : 9 + d, :] = jnp.where(
            rows[d] == first, numbers[8 + first : 9 + first, :], numbers[9 + first : 10 + first, :]
        )
    sources = [(places, k) for k in range(3)] + [(burgers, a) for a in range(3)]
    copy.wait()
    fill_sends(lambda d, n: numbers_smem[8 + rows[d], n], sources, {0: s0, 1: s1, 2: s2, 3: s3})


def put_rows(out, k, value):
    for b in range(BLOCKS):
        out[k : k + 1, LANES * b : LANES * b + LANES] = value[b : b + 1]


def halves(tile):
    low = lax.broadcasted_iota(jnp.int32, (8, LANES), 0) < 4
    turned = pltpu.roll(tile, 4, 0)
    return jnp.where(low, tile, turned), jnp.where(low, turned, tile)


def pair_rows(values):
    low = lax.broadcasted_iota(jnp.int32, (8, LANES), 0) < 4
    rows = [
        x if x is y else jnp.where(low, x, y) for x, y in zip(values[0::2], values[1::2])
    ]
    rows += [jnp.zeros((8, LANES), f32)] * (LANES // 8 - len(rows))
    return jnp.concatenate(rows, axis=0)


def far_kernel(
    scalars_in, places, burgers, mine_out, other_out, control_out, acc, rows, cols, apart_by, w_even, w_odd,
    scalars, control, sems, by_target
):
    copy = pltpu.make_async_copy(scalars_in, scalars, sems.at[0])
    copy.start()
    for i in range(LEAD):
        control[AT_PAIRS - LEAD + i] = EXT
        control[AT_PAIRS + LIST - LEAD + i] = EXT
    for tile in range(BLOCKS // 8):
        p = [halves(places[k, 8 * tile : 8 * tile + 8, :]) for k in range(3)]
        burg = [halves(burgers[a, 8 * tile : 8 * tile + 8, :]) for a in range(3)]
        for half in range(2):
            here = [x[half] for x in p]
            sources = [x[half] for x in burg]
            moments = [x * y for x in here for y in sources]
            values = []
            for group in (sources, moments):
                high = [round_bf16(x) for x in group]
                values += high + [x - h for x, h in zip(group, high)]
            rows[2 * tile + half] = pair_rows(values)
            one = jnp.ones((8, LANES), f32)
            square = sum(x * x for x in here) + far_sq
            values = [part for x in (here[0], here[1], square) for part in split3(x)]
            cols[2 * tile + half] = pair_rows(values + [one, one, one]).T.astype(bf16)
    acc[...] = jnp.zeros_like(acc)
    w_odd[...] = jnp.zeros_like(w_odd)
    slab, cell = centre_of()
    target = lax.broadcasted_iota(jnp.int32, (1, EXT), 1)
    apart = [(target // 32).astype(f32) - slab, (target % 32).astype(f32) - cell]
    square = apart[0] * apart[0] + apart[1] * apart[1]
    square_high = round_bf16(square)
    place = lax.broadcasted_iota(jnp.int32, (LANES, EXT), 0)
    values = jnp.where(place < 36, 1.0, 0.0)
    for first, last, x in (
        (0, 12, -2.0 * apart[0]),
        (12, 24, -2.0 * apart[1]),
        (36, 40, square_high),
        (40, 44, square - square_high),
    ):
        values = jnp.where((place >= first) & (place < last), x, values)
    for g in range(4):
        apart_by[g] = jnp.where(place % 4 == g, values, 0.0).astype(bf16)

    def sums(group, g, w):
        mine = rows[group, pl.ds(g, 32, stride=4), :].astype(bf16)
        acc[...] += jnp.dot(
            jnp.concatenate([mine, mine], axis=1), w[g], preferred_element_type=f32
        )

    def half(group, w_now, w_before):
        for i in range(4):
            for slot in range(NEAR):
                word = scalars[slot, 4 * group + i]
                at = lax.shift_right_logical(word, 15)
                control[AT_PAIRS + at] = word & (2**15 - 1)
        for d in range(4):
            for i in range(3):
                n = 3 * group + i
                control[AT_SENDS + GHOST * d + n] = scalars[8 + d, n]
        for g in range(4):
            sums(jnp.maximum(group - 1, 0), g, w_before)
            r = lax.rsqrt(jnp.dot(cols[group], apart_by[g], preferred_element_type=f32))
            r2 = r * r
            w3 = r2 * r
            for k, w in enumerate((w3, w3 * r2)):
                high, low = split2(w)
                w_now[g, :LANES, EXT * k : EXT * k + EXT] = high
                w_now[g, LANES:, EXT * k : EXT * k + EXT] = low

    copy.wait()

    def body(step, carry):
        half(2 * step, w_even, w_odd)
        half(2 * step + 1, w_odd, w_even)
        return carry

    lax.fori_loop(0, BLOCKS // 8, body, 0)
    amounts = [scalars[NEAR, 0], scalars[NEAR + 1, 0]]
    for k in range(2):
        for i in range(TAIL):
            control[AT_PAIRS + LIST * k + amounts[k] + i] = EXT
        control[k] = amounts[k]
    copy = pltpu.make_async_copy(control, control_out, sems.at[1])
    copy.start()
    for g in range(4):
        sums(BLOCKS // 4 - 1, g, w_odd)

    apart = apart + [jnp.zeros((1, EXT), f32)]

    def row(k, i):
        return acc[i : i + 1, EXT * k : EXT * k + EXT]

    direct = [row(0, a) + row(0, 3 + a) for a in range(3)]
    total = [row(1, a) + row(1, 3 + a) for a in range(3)]
    gradient = []
    for a in range(3):
        for k in range(3):
            moment = row(1, 6 + 3 * k + a) + row(1, 15 + 3 * k + a)
            gradient.append(-3.0 * (apart[k] * total[a] - moment))
    zero = jnp.zeros((LANES - 12, 2 * LANES), f32)
    values = jnp.concatenate(direct + gradient + [zero], axis=0)
    by_target[...] = jnp.concatenate([values[:, :LANES].T, values[:, LANES:].T], axis=0)
    first, second = (by_target[pl.ds(i, LANES, stride=2), :] for i in range(2))
    here = lax.axis_index("core") == 0
    mine_out[...] = jnp.where(here, first, second)
    other_out[...] = jnp.where(here, second, first)
    copy.wait()


def tile_of(own, ghosts, index, tile):
    if tile < BLOCKS // 8:
        return own[index, 8 * tile : 8 * tile + 8, :]
    d, n = divmod(tile - BLOCKS // 8, GHOST // 8)
    return ghosts[d][index, 8 * n : 8 * n + 8, :]


def tiles_of(slots):
    n = GHOST // 8
    return [BLOCKS // 8 + n * d + i for d in slots for i in range(n)]


def prepare_sources(own, ghosts, tiles, left):
    shift = slot_shifts()
    one = jnp.ones((8, LANES), f32)
    low = lax.broadcasted_iota(jnp.int32, (8, LANES), 0) < 4

    for tile in tiles:
        p = [tile_of(own, ghosts, k, tile) for k in range(3)]
        if tile >= BLOCKS // 8:
            k, by = shift[(tile - BLOCKS // 8) // (GHOST // 8)]
            p[k] = p[k] + by
        parts_of = [split3(x) for x in p]
        parts_of.append(split3(p[0] * p[0] + p[1] * p[1] + p[2] * p[2]))
        turned = [[pltpu.roll(x, 4, 0) for x in group] for group in parts_of]
        for half in range(2):
            first, second = (parts_of, turned) if half == 0 else (turned, parts_of)
            values = []
            for (h, m, _), (h2, m2, l2) in zip(first[:3], second[:3]):
                values += [
                    jnp.where(low, h, h2),
                    jnp.where(low, m, m2),
                    jnp.where(low, h, l2),
                ]
            h, _, l = first[3]
            values += [jnp.where(low, h, second[3][1]), jnp.where(low, l, one), one]
            values += [jnp.zeros((8, LANES), f32)] * (LANES // 8 - len(values))
            left[2 * tile + half] = jnp.concatenate(values, axis=0).T.astype(bf16)
    left[EXT // 4] = jnp.zeros((LANES, LANES), bf16)


def prepare_targets(own, parts, right):
    one = jnp.ones((8, LANES), f32)
    low = lax.broadcasted_iota(jnp.int32, (8, LANES), 0) < 4

    x = [own[k] for k in range(3)]
    for k in range(3):
        for i, part in enumerate(split3(-2.0 * x[k])):
            parts[3 * k + i] = part
    for i, part in enumerate(split3(x[0] * x[0] + x[1] * x[1] + x[2] * x[2] + core_sq)):
        parts[9 + i] = part
    for b in range(BLOCKS):
        def row(i):
            return jnp.broadcast_to(parts[i, b : b + 1, :], (8, LANES))

        rows = []
        for k in range(3):
            h, m, l = row(3 * k), row(3 * k + 1), row(3 * k + 2)
            high_mid = jnp.where(low, h, m)
            rows += [high_mid, high_mid, jnp.where(low, l, h)]
        rows += [one, jnp.where(low, one, row(9)), jnp.where(low, row(10), row(11))]
        for i in range(6):
            right[b, i] = jnp.concatenate(rows[2 * i : 2 * i + 2], axis=0).astype(bf16)
        right[b, 6:] = jnp.zeros((2, 16, LANES), bf16)


def add_pairs(control, which, burg, left, right, mask, acc, k_even, k_odd):
    place = lax.broadcasted_iota(jnp.int32, (16, LANES), 0) % 4
    for g in range(4):
        mask[g] = jnp.where(place == g, 1.0, 0.0).astype(bf16)

    k_odd[...] = jnp.zeros_like(k_odd)

    def pair(i):
        word = control[AT_PAIRS + LIST * which + i]
        return lax.shift_right_logical(word, SHARE), word & (2**SHARE - 1)

    def sums(step, g, k_before):
        i = step * GROUP + g
        (b0, t0), (b1, t1) = pair(i), pair(i + 1)
        rows = jnp.concatenate(
            [burg[pl.ds(pl.multiple_of(8 * t, 8), 8), :] for t in (t0, t1)], axis=0
        ).astype(bf16)
        both = jnp.dot(
            jnp.concatenate([rows, rows], axis=1),
            jnp.concatenate([k_before[g], k_before[g + 1]], axis=1),
            preferred_element_type=f32,
        )
        at = pl.ds(pl.multiple_of(8 * b0, 8), 8)
        acc[at, :] = acc[at, :] + both[:8, :LANES]
        at = pl.ds(pl.multiple_of(8 * b1, 8), 8)
        acc[at, :] = acc[at, :] + both[8:, LANES:]

    def half(step, k_now, k_before):
        for g in range(GROUP):
            if g % 2 == 0:
                sums(step - 1, g, k_before)
            b, t = pair(step * GROUP + g)
            features = (right[b] * mask[t & 3][None]).reshape(LANES, LANES)
            near_sq = jnp.dot(
                left[lax.shift_right_logical(t, 2)], features, preferred_element_type=f32
            )
            near_sq = jnp.maximum(near_sq, core_sq)
            r = lax.rsqrt(near_sq)
            q = lax.rsqrt(near_sq + (far_sq - core_sq))
            high, low = split2(r * r * r - q * q * q)
            k_now[g, :LANES, :] = high
            k_now[g, LANES:, :] = low

    def body(step, carry):
        half(2 * step, k_even, k_odd)
        half(2 * step + 1, k_odd, k_even)
        return carry

    steps = (control[which] + 2 * GROUP - 1) // (2 * GROUP)
    lax.fori_loop(0, steps, body, 0)
    for g in range(0, GROUP, 2):
        sums(2 * steps - 1, g, k_odd)


def component(acc, a):
    return acc[pl.ds(a, BLOCKS, stride=8), :] + acc[pl.ds(3 + a, BLOCKS, stride=8), :]


parts_scratch = pltpu.VMEM((12, BLOCKS, LANES), f32)
right_shape = (BLOCKS, 8, 16, LANES)
acc_shape = (BLOCKS * 8, LANES)
control_scratch = [pltpu.SMEM((CONTROL,), jnp.int32), pltpu.SemaphoreType.DMA]
near_scratch = control_scratch + [
    pltpu.VMEM((EXT // 4 + 1, LANES, LANES), bf16),
    pltpu.VMEM((4, 16, LANES), bf16),
    pltpu.VMEM((GROUP, 2 * LANES, LANES), bf16),
    pltpu.VMEM((GROUP, 2 * LANES, LANES), bf16),
]


def total_force(expansion, near, places):
    out = []
    for a in range(3):
        far = expansion[0:1, a : a + 1]
        for k in range(3):
            far = far + expansion[0:1, 3 + 3 * a + k : 4 + 3 * a + k] * places[k]
        out.append(near[a] + far)
    return out


def first_kernel(
    control_in, own, burgers, g3, g0, g2, g1, near, burg, control, sem, left, mask, k_even, k_odd, parts, right, acc
):
    copy = pltpu.make_async_copy(control_in, control, sem)
    copy.start()
    ghosts = (g0, g1, g2, g3)
    exists = slot_exists()
    burg[...] = jnp.zeros_like(burg)
    for tile in range(EXT // 8):
        for a in range(3):
            if tile < BLOCKS // 8:
                value = burgers[a, 8 * tile : 8 * tile + 8, :]
            else:
                d = (tile - BLOCKS // 8) // (GHOST // 8)
                value = tile_of(None, ghosts, 3 + a, tile)
                if exists[d] is not None:
                    value = jnp.where(exists[d], value, 0.0)
            high = round_bf16(value)
            burg[pl.ds(tile * 64 + a, 8, stride=8), :] = high
            burg[pl.ds(tile * 64 + 3 + a, 8, stride=8), :] = value - high
    prepare_sources(own, ghosts, range(EXT // 8), left)
    prepare_targets(own, parts, right)
    acc[...] = jnp.zeros_like(acc)
    copy.wait()
    for which in range(2):
        add_pairs(control, which, burg, left, right, mask, acc, k_even, k_odd)
    for a in range(3):
        near[a] = component(acc, a)


def start_kernel(
    control_in, shares, near, places, mobility, expansion, moved, now, s0, s1, s2, s3, control, sem
):
    copy = pltpu.make_async_copy(control_in, control, sem)
    copy.start()
    expansion[...] = jnp.broadcast_to(jnp.sum(shares[...], axis=0, keepdims=True), (8, LANES))
    p = [places[k] for k in range(3)]
    force = total_force(expansion[...], [near[a] for a in range(3)], p)
    for a in range(3):
        step = (time_step * mobility[...]) * force[a]
        moved[a] = step
        now[a] = p[a] + step
    copy.wait()
    send_now(control, now, (s0, s1, s2, s3))


def early_kernel(
    control_in, own, g3, burg, right, acc, control, sem, left, mask, k_even, k_odd, parts
):
    copy = pltpu.make_async_copy(control_in, control, sem)
    copy.start()
    ghosts = (None, None, None, g3)
    prepare_sources(own, ghosts, list(range(BLOCKS // 8)) + tiles_of(EARLY), left)
    prepare_targets(own, parts, right)
    acc[...] = jnp.zeros_like(acc)
    copy.wait()
    add_pairs(control, 0, burg, left, right, mask, acc, k_even, k_odd)


def late_force(
    control_in, expansion, own, g0, g2, g1, burg, right, acc_in, control, sem, left, mask, k_even, k_odd, acc
):
    copy = pltpu.make_async_copy(control_in, control, sem)
    copy.start()
    prepare_sources(own, (g0, g1, g2, None), tiles_of(LATE), left)
    acc[...] = acc_in[...]
    copy.wait()
    add_pairs(control, 1, burg, left, right, mask, acc, k_even, k_odd)
    return total_force(
        expansion[...], [component(acc, a) for a in range(3)], [own[k] for k in range(3)]
    )


def step_kernel(
    final, control, expansion, own, g0, g2, g1, burg, right, acc_in, mobility, places, moved,
    new_moved, now, s0, s1, s2, s3, *scratch
):
    force = late_force(control, expansion, own, g0, g2, g1, burg, right, acc_in, *scratch)
    for a in range(3):
        total = moved[a] + (time_step * mobility[...]) * force[a]
        if final:
            put_rows(new_moved, a, total)
        else:
            new_moved[a] = total
        now[a] = places[a] + total
    send_now(scratch[0], now, (s0, s1, s2, s3))


def last_kernel(
    control, expansion, own, g0, g2, g1, burg, right, acc_in, mobility, velocity, *scratch
):
    force = late_force(control, expansion, own, g0, g2, g1, burg, right, acc_in, *scratch)
    for a in range(3):
        put_rows(velocity, a, mobility[...] * force[a])


def cost(flops):
    return pl.CostEstimate(flops=int(flops), bytes_accessed=2**20, transcendentals=0)


def shape(*dims, dtype=f32):
    return jax.ShapeDtypeStruct(dims, dtype)


def swap(x, slot):
    n_slabs, n_cells = n_slabs_cells()
    pairs = []
    for s in range(n_slabs):
        for c in range(n_cells):
            if slot == 0:
                to = (s ^ 1, c)
            elif slot == 3:
                to = (s, c ^ 1)
            elif slot == 1:
                t = s - 1 + 2 * (s % 2)
                to = (t, c) if 0 <= t < n_slabs else (s, c ^ 1)
            else:
                t = c - 1 + 2 * (c % 2)
                to = (s, t) if 0 <= t < n_cells else (s ^ 1, c)
            pairs.append((s * n_cells + c, to[0] * n_cells + to[1]))
    return lax.ppermute(x, ("slab", "chip", "core"), pairs)


def exchange(sends):
    return [swap(sends[slot], slot) for slot in EARLY + LATE]


def local(positions, burgers, mobility, near_list, near_count, send_list):
    mobility = mobility.reshape(BLOCKS, LANES)
    flat = shape(*positions.shape)
    block = shape(3, BLOCKS, LANES)
    send = shape(3, GHOST, LANES)

    positions = positions.reshape(block.shape)
    burgers = burgers.reshape(block.shape)
    numbers = (
        jnp.pad(near_list.T, ((0, 16 - NEAR), (0, LANES - BLOCKS)))
        + jnp.pad(near_count[None], ((NEAR, 15 - NEAR), (0, LANES - BLOCKS)))
        + jnp.pad(send_list, ((8, 4), (0, LANES - GHOST)))
    )

    places, scalars, *sends = pl.pallas_call(
        pack_kernel,
        out_shape=[block, shape(16, LANES, dtype=jnp.int32)] + [shape(6, GHOST, LANES)] * 4,
        in_specs=[vmem] * 3,
        out_specs=[vmem] * 6,
        scratch_shapes=[pltpu.SMEM((16, LANES), jnp.int32), pltpu.SemaphoreType.DMA],
        compiler_params=params,
        name="pack",
    )(numbers, positions, burgers)
    ghosts = [swap(x, slot) for x, slot in zip(sends, (3, 0, 2, 1))]

    mine, other, control = pl.pallas_call(
        far_kernel,
        out_shape=[shape(EXT // 2, LANES)] * 2 + [shape(CONTROL, dtype=jnp.int32)],
        in_specs=[vmem] * 3,
        out_specs=[vmem] * 3,
        scratch_shapes=[
            pltpu.VMEM((32, 2 * EXT), f32),
            pltpu.VMEM((BLOCKS // 4, LANES, LANES), f32),
            pltpu.VMEM((BLOCKS // 4, LANES, LANES), bf16),
            pltpu.VMEM((4, LANES, EXT), bf16),
            pltpu.VMEM((4, 2 * LANES, 2 * EXT), bf16),
            pltpu.VMEM((4, 2 * LANES, 2 * EXT), bf16),
            pltpu.SMEM((16, LANES), jnp.int32),
            pltpu.SMEM((CONTROL,), jnp.int32),
            pltpu.SemaphoreType.DMA((2,)),
            pltpu.VMEM((EXT, LANES), f32),
        ],
        compiler_params=params,
        cost_estimate=cost(20e9),
        name="far",
    )(scalars, places, burgers)
    shares = lax.all_to_all(mine + swap(other, 3), ("slab", "chip"), 0, 0, tiled=True)

    near, burg = pl.pallas_call(
        first_kernel,
        out_shape=[block, shape((EXT + 1) * 8, LANES)],
        in_specs=[vmem] * 7,
        out_specs=[vmem] * 2,
        scratch_shapes=near_scratch
        + [parts_scratch, pltpu.VMEM(right_shape, bf16), pltpu.VMEM(acc_shape, f32)],
        compiler_params=params,
        cost_estimate=cost(20e9),
        name="near_first",
    )(control, places, burgers, *ghosts)

    expansion, moved, now, *sends = pl.pallas_call(
        start_kernel,
        out_shape=[shape(8, LANES), block, block] + [send] * 4,
        in_specs=[vmem] * 5,
        out_specs=[vmem] * 7,
        scratch_shapes=control_scratch,
        compiler_params=params,
        name="start",
    )(control, shares, near, places, mobility)

    def evaluate(kernel, out_shape, name, *more):
        ghosts = exchange(sends)
        right, acc = pl.pallas_call(
            early_kernel,
            out_shape=[shape(*right_shape, dtype=bf16), shape(*acc_shape)],
            in_specs=[vmem] * 4,
            out_specs=[vmem] * 2,
            scratch_shapes=near_scratch + [parts_scratch],
            compiler_params=params,
            cost_estimate=cost(20e9),
            name="near_early",
        )(control, now, *ghosts[: len(EARLY)], burg)
        return pl.pallas_call(
            kernel,
            out_shape=out_shape,
            in_specs=[vmem] * (7 + len(LATE) + len(more)),
            out_specs=jax.tree.map(lambda _: vmem, out_shape),
            scratch_shapes=near_scratch + [pltpu.VMEM(acc_shape, f32)],
            compiler_params=params,
            cost_estimate=cost(10e9),
            name=name,
        )(control, expansion, now, *ghosts[len(EARLY) :], burg, right, acc, mobility, *more)

    for substep in range(1, SUBSTEPS):
        final = substep == SUBSTEPS - 1
        moved, now, *sends = evaluate(
            functools.partial(step_kernel, final),
            [flat if final else block, block] + [send] * 4,
            "near_step",
            places,
            moved,
        )
    velocity = evaluate(last_kernel, flat, "near_last")
    return moved, velocity


AXES = ("slab", "chip", "core")


def solution(mesh):
    n_slabs, n_cells = mesh.devices.shape
    return jax.shard_map(
        local,
        mesh=jax.sharding.Mesh(mesh.devices.reshape(n_slabs, n_cells // 2, 2), AXES),
        in_specs=(
            P(None, AXES),
            P(None, AXES),
            P(AXES),
            P(AXES, None),
            P(AXES),
            P(None, AXES),
        ),
        out_specs=(P(None, AXES), P(None, AXES)),
        check_vma=False,
    )
```

```python
import functools

import jax
import jax.numpy as jnp
from jax import lax
from jax.experimental import pallas as pl
from jax.experimental.pallas import tpu as pltpu
from jax.sharding import PartitionSpec as P

SUBSTEPS = 4
BLOCKS = 64
LANES = 128
NEAR = 6
GHOST = 48
EXT = 256
GROUP = 8
LEAD = GROUP
TAIL = 56
AT_SENDS = 8
AT_PAIRS = AT_SENDS + 4 * GHOST + LEAD
LIST = BLOCKS * NEAR + TAIL + LEAD
CONTROL = AT_PAIRS + 2 * LIST + 8
EARLY, LATE = (3,), (1, 0, 2)
SHARE = 9

core_sq = 0.04
far_sq = 1.0
time_step = 0.2

f32 = jnp.float32
bf16 = jnp.bfloat16

vmem = pl.BlockSpec(memory_space=pltpu.VMEM)
params = pltpu.CompilerParams(vmem_limit_bytes=40 * 2**20)


def round_bf16(x):
    return x.astype(bf16).astype(f32)


def split2(x):
    high = x.astype(bf16)
    return high, (x - high.astype(f32)).astype(bf16)


def split3(x):
    high = round_bf16(x)
    rest = x - high
    mid = round_bf16(rest)
    return high, mid, round_bf16(rest - mid)


def parity():
    return lax.axis_index("slab") % 2, lax.axis_index("cell") % 2


def send_rows():
    odd_slab, odd_cell = parity()
    return odd_slab, 1 - odd_slab, 3 - odd_cell, 2 + odd_cell


def slot_moves():
    odd_slab, odd_cell = parity()
    return (
        GHOST * (1 - odd_slab),
        GHOST * (odd_slab - 1),
        GHOST * odd_cell,
        -GHOST * odd_cell,
    )


def slot_shifts():
    odd_slab, odd_cell = parity()
    along_slab = (1 - 2 * odd_slab).astype(f32)
    along_cell = (1 - 2 * odd_cell).astype(f32)
    return (0, along_slab), (0, -along_slab), (1, -along_cell), (1, along_cell)


def slot_exists():
    out = []
    for axis in ("slab", "cell"):
        i = lax.axis_index(axis)
        partner = i - 1 + 2 * (i % 2)
        out.append((partner >= 0) & (partner < lax.axis_size(axis)))
    return None, out[0], out[1], None


def fill_sends(block_of, sources, sends):
    def body(n, carry):
        for d in sends:
            block = block_of(d, n)
            for a, (ref, index) in enumerate(sources):
                sends[d][a, pl.ds(n, 1), :] = ref[index, pl.ds(block, 1), :]
        return carry

    lax.fori_loop(0, GHOST, body, 0, unroll=4)


def send_now(control, now, sends):
    fill_sends(
        lambda d, n: control[AT_SENDS + GHOST * d + n],
        [(now, k) for k in range(3)],
        dict(enumerate(sends)),
    )


def centre_of():
    slab = lax.axis_index("slab").astype(f32)
    cell = lax.axis_index("cell").astype(f32)
    return slab, cell


def list_pairs(near_list, near_count):
    segment = (near_list + (GHOST - BLOCKS)) // GHOST
    exists = {0: None, 3: None}
    exists[1], exists[2] = slot_exists()[1:3]
    odd_slab, odd_cell = parity()
    sides = (
        (odd_slab == 1) | exists[1],
        (odd_slab == 0) | exists[1],
        (odd_cell == 1) | exists[2],
        (odd_cell == 0) | exists[2],
    )
    slot = lax.broadcasted_iota(jnp.int32, near_list.shape, 0)
    block = lax.broadcasted_iota(jnp.int32, near_list.shape, 1)
    live = jnp.where(slot < near_count, 1, 0)
    moved = near_list
    for i, (move, there) in enumerate(zip(slot_moves(), sides)):
        mine = segment == 1 + i
        moved = moved + jnp.where(mine, move, 0)
        live = jnp.where(mine, live * there.astype(jnp.int32), live)
    late = jnp.where(moved >= BLOCKS, live, 0)
    for d in EARLY:
        first = BLOCKS + GHOST * d
        late = jnp.where((moved >= first) & (moved < first + GHOST), 0, late)
    earlier = lax.broadcasted_iota(jnp.int32, (BLOCKS, BLOCKS), 0) < lax.broadcasted_iota(
        jnp.int32, (BLOCKS, BLOCKS), 1
    )
    place = jnp.full(near_list.shape, 2 * LIST, jnp.int32)
    amounts = []
    for i, mine in enumerate((live - late, late)):
        rows = [mine[n : n + 1] for n in range(NEAR)]
        before = [jnp.zeros_like(rows[0])]
        for row in rows:
            before.append(before[-1] + row)
        amount = before.pop().astype(f32)
        offset = jnp.dot(
            jnp.broadcast_to(amount, (8, BLOCKS)),
            jnp.where(earlier, 1.0, 0.0),
            preferred_element_type=f32,
        )[:1]
        at = jnp.concatenate([offset.astype(jnp.int32) + x for x in before], axis=0)
        place = jnp.where(mine > 0, at + LIST * i, place)
        amounts.append(jnp.sum(amount, axis=1, keepdims=True).astype(jnp.int32))
    words = 2**15 * place + 2**SHARE * block + moved
    return words, amounts


def pack_kernel(
    numbers, positions, burgers, places, scalars, s3, s1, s0, s2, numbers_smem, sem
):
    copy = pltpu.make_async_copy(numbers, numbers_smem, sem)
    copy.start()
    slab, cell = centre_of()
    for k, by in enumerate((slab + 0.5, cell + 0.5, 0.5)):
        places[k] = positions[k] - by
    scalars[...] = jnp.zeros_like(scalars)
    words, amounts = list_pairs(numbers[:NEAR, :BLOCKS], numbers[NEAR : NEAR + 1, :BLOCKS])
    scalars[:NEAR, :BLOCKS] = words
    for i in range(2):
        scalars[NEAR + i : NEAR + i + 1, :] = jnp.broadcast_to(amounts[i], (1, LANES))
    rows = send_rows()
    for d in range(4):
        first = 2 * (d // 2)
        scalars[8 + d : 9 + d, :] = jnp.where(
            rows[d] == first, numbers[8 + first : 9 + first, :], numbers[9 + first : 10 + first, :]
        )
    sources = [(places, k) for k in range(3)] + [(burgers, a) for a in range(3)]
    copy.wait()
    fill_sends(lambda d, n: numbers_smem[8 + rows[d], n], sources, {0: s0, 1: s1, 2: s2, 3: s3})


def put_rows(out, k, value):
    for b in range(BLOCKS):
        out[k : k + 1, LANES * b : LANES * b + LANES] = value[b : b + 1]


def halves(tile):
    low = lax.broadcasted_iota(jnp.int32, (8, LANES), 0) < 4
    turned = pltpu.roll(tile, 4, 0)
    return jnp.where(low, tile, turned), jnp.where(low, turned, tile)


def pair_rows(values):
    low = lax.broadcasted_iota(jnp.int32, (8, LANES), 0) < 4
    rows = [
        x if x is y else jnp.where(low, x, y) for x, y in zip(values[0::2], values[1::2])
    ]
    rows += [jnp.zeros((8, LANES), f32)] * (LANES // 8 - len(rows))
    return jnp.concatenate(rows, axis=0)


def far_kernel(
    scalars_in, places, burgers, out, control_out, acc, rows, cols, apart_by, w_even, w_odd,
    scalars, control, sems
):
    copy = pltpu.make_async_copy(scalars_in, scalars, sems.at[0])
    copy.start()
    for i in range(LEAD):
        control[AT_PAIRS - LEAD + i] = EXT
        control[AT_PAIRS + LIST - LEAD + i] = EXT
    for tile in range(BLOCKS // 8):
        p = [halves(places[k, 8 * tile : 8 * tile + 8, :]) for k in range(3)]
        burg = [halves(burgers[a, 8 * tile : 8 * tile + 8, :]) for a in range(3)]
        for half in range(2):
            here = [x[half] for x in p]
            sources = [x[half] for x in burg]
            moments = [x * y for x in here for y in sources]
            values = []
            for group in (sources, moments):
                high = [round_bf16(x) for x in group]
                values += high + [x - h for x, h in zip(group, high)]
            rows[2 * tile + half] = pair_rows(values)
            one = jnp.ones((8, LANES), f32)
            square = sum(x * x for x in here) + far_sq
            values = [part for x in (here[0], here[1], square) for part in split3(x)]
            cols[2 * tile + half] = pair_rows(values + [one, one, one]).T.astype(bf16)
    acc[...] = jnp.zeros_like(acc)
    w_odd[...] = jnp.zeros_like(w_odd)
    slab, cell = centre_of()
    target = lax.broadcasted_iota(jnp.int32, (1, EXT), 1)
    apart = [(target // 32).astype(f32) - slab, (target % 32).astype(f32) - cell]
    square = apart[0] * apart[0] + apart[1] * apart[1]
    square_high = round_bf16(square)
    place = lax.broadcasted_iota(jnp.int32, (LANES, EXT), 0)
    values = jnp.where(place < 36, 1.0, 0.0)
    for first, last, x in (
        (0, 12, -2.0 * apart[0]),
        (12, 24, -2.0 * apart[1]),
        (36, 40, square_high),
        (40, 44, square - square_high),
    ):
        values = jnp.where((place >= first) & (place < last), x, values)
    for g in range(4):
        apart_by[g] = jnp.where(place % 4 == g, values, 0.0).astype(bf16)

    def sums(group, g, w):
        mine = rows[group, pl.ds(g, 32, stride=4), :].astype(bf16)
        acc[...] += jnp.dot(
            jnp.concatenate([mine, mine], axis=1), w[g], preferred_element_type=f32
        )

    def half(group, w_now, w_before):
        for i in range(4):
            for slot in range(NEAR):
                word = scalars[slot, 4 * group + i]
                at = lax.shift_right_logical(word, 15)
                control[AT_PAIRS + at] = word & (2**15 - 1)
        for d in range(4):
            for i in range(3):
                n = 3 * group + i
                control[AT_SENDS + GHOST * d + n] = scalars[8 + d, n]
        for g in range(4):
            sums(jnp.maximum(group - 1, 0), g, w_before)
            r = lax.rsqrt(jnp.dot(cols[group], apart_by[g], preferred_element_type=f32))
            r2 = r * r
            w3 = r2 * r
            for k, w in enumerate((w3, w3 * r2)):
                high, low = split2(w)
                w_now[g, :LANES, EXT * k : EXT * k + EXT] = high
                w_now[g, LANES:, EXT * k : EXT * k + EXT] = low

    copy.wait()

    def body(step, carry):
        half(2 * step, w_even, w_odd)
        half(2 * step + 1, w_odd, w_even)
        return carry

    lax.fori_loop(0, BLOCKS // 8, body, 0)
    amounts = [scalars[NEAR, 0], scalars[NEAR + 1, 0]]
    for k in range(2):
        for i in range(TAIL):
            control[AT_PAIRS + LIST * k + amounts[k] + i] = EXT
        control[k] = amounts[k]
    copy = pltpu.make_async_copy(control, control_out, sems.at[1])
    copy.start()
    for g in range(4):
        sums(BLOCKS // 4 - 1, g, w_odd)

    apart = apart + [jnp.zeros((1, EXT), f32)]

    def row(k, i):
        return acc[i : i + 1, EXT * k : EXT * k + EXT]

    direct = [row(0, a) + row(0, 3 + a) for a in range(3)]
    total = [row(1, a) + row(1, 3 + a) for a in range(3)]
    gradient = []
    for a in range(3):
        for k in range(3):
            moment = row(1, 6 + 3 * k + a) + row(1, 15 + 3 * k + a)
            gradient.append(-3.0 * (apart[k] * total[a] - moment))
    zero = jnp.zeros((LANES - 12, 2 * LANES), f32)
    values = jnp.concatenate(direct + gradient + [zero], axis=0)
    out[...] = jnp.concatenate([values[:, :LANES].T, values[:, LANES:].T], axis=0)
    copy.wait()


def tile_of(own, ghosts, index, tile):
    if tile < BLOCKS // 8:
        return own[index, 8 * tile : 8 * tile + 8, :]
    d, n = divmod(tile - BLOCKS // 8, GHOST // 8)
    return ghosts[d][index, 8 * n : 8 * n + 8, :]


def tiles_of(slots):
    n = GHOST // 8
    return [BLOCKS // 8 + n * d + i for d in slots for i in range(n)]


def prepare_sources(own, ghosts, tiles, left):
    shift = slot_shifts()
    one = jnp.ones((8, LANES), f32)
    low = lax.broadcasted_iota(jnp.int32, (8, LANES), 0) < 4

    for tile in tiles:
        p = [tile_of(own, ghosts, k, tile) for k in range(3)]
        if tile >= BLOCKS // 8:
            k, by = shift[(tile - BLOCKS // 8) // (GHOST // 8)]
            p[k] = p[k] + by
        parts_of = [split3(x) for x in p]
        parts_of.append(split3(p[0] * p[0] + p[1] * p[1] + p[2] * p[2]))
        turned = [[pltpu.roll(x, 4, 0) for x in group] for group in parts_of]
        for half in range(2):
            first, second = (parts_of, turned) if half == 0 else (turned, parts_of)
            values = []
            for (h, m, _), (h2, m2, l2) in zip(first[:3], second[:3]):
                values += [
                    jnp.where(low, h, h2),
                    jnp.where(low, m, m2),
                    jnp.where(low, h, l2),
                ]
            h, _, l = first[3]
            values += [jnp.where(low, h, second[3][1]), jnp.where(low, l, one), one]
            values += [jnp.zeros((8, LANES), f32)] * (LANES // 8 - len(values))
            left[2 * tile + half] = jnp.concatenate(values, axis=0).T.astype(bf16)
    left[EXT // 4] = jnp.zeros((LANES, LANES), bf16)


def prepare_targets(own, parts, right):
    one = jnp.ones((8, LANES), f32)
    low = lax.broadcasted_iota(jnp.int32, (8, LANES), 0) < 4

    x = [own[k] for k in range(3)]
    for k in range(3):
        for i, part in enumerate(split3(-2.0 * x[k])):
            parts[3 * k + i] = part
    for i, part in enumerate(split3(x[0] * x[0] + x[1] * x[1] + x[2] * x[2] + core_sq)):
        parts[9 + i] = part
    for b in range(BLOCKS):
        def row(i):
            return jnp.broadcast_to(parts[i, b : b + 1, :], (8, LANES))

        rows = []
        for k in range(3):
            h, m, l = row(3 * k), row(3 * k + 1), row(3 * k + 2)
            high_mid = jnp.where(low, h, m)
            rows += [high_mid, high_mid, jnp.where(low, l, h)]
        rows += [one, jnp.where(low, one, row(9)), jnp.where(low, row(10), row(11))]
        for i in range(6):
            right[b, i] = jnp.concatenate(rows[2 * i : 2 * i + 2], axis=0).astype(bf16)
        right[b, 6:] = jnp.zeros((2, 16, LANES), bf16)


def add_pairs(control, which, burg, left, right, mask, acc, k_even, k_odd):
    place = lax.broadcasted_iota(jnp.int32, (16, LANES), 0) % 4
    for g in range(4):
        mask[g] = jnp.where(place == g, 1.0, 0.0).astype(bf16)

    k_odd[...] = jnp.zeros_like(k_odd)

    def pair(i):
        word = control[AT_PAIRS + LIST * which + i]
        return lax.shift_right_logical(word, SHARE), word & (2**SHARE - 1)

    def sums(step, g, k_before):
        i = step * GROUP + g
        (b0, t0), (b1, t1) = pair(i), pair(i + 1)
        rows = jnp.concatenate(
            [burg[pl.ds(pl.multiple_of(8 * t, 8), 8), :] for t in (t0, t1)], axis=0
        ).astype(bf16)
        both = jnp.dot(
            jnp.concatenate([rows, rows], axis=1),
            jnp.concatenate([k_before[g], k_before[g + 1]], axis=1),
            preferred_element_type=f32,
        )
        at = pl.ds(pl.multiple_of(8 * b0, 8), 8)
        acc[at, :] = acc[at, :] + both[:8, :LANES]
        at = pl.ds(pl.multiple_of(8 * b1, 8), 8)
        acc[at, :] = acc[at, :] + both[8:, LANES:]

    def half(step, k_now, k_before):
        for g in range(GROUP):
            if g % 2 == 0:
                sums(step - 1, g, k_before)
            b, t = pair(step * GROUP + g)
            features = (right[b] * mask[t & 3][None]).reshape(LANES, LANES)
            near_sq = jnp.dot(
                left[lax.shift_right_logical(t, 2)], features, preferred_element_type=f32
            )
            near_sq = jnp.maximum(near_sq, core_sq)
            r = lax.rsqrt(near_sq)
            q = lax.rsqrt(near_sq + (far_sq - core_sq))
            high, low = split2(r * r * r - q * q * q)
            k_now[g, :LANES, :] = high
            k_now[g, LANES:, :] = low

    def body(step, carry):
        half(2 * step, k_even, k_odd)
        half(2 * step + 1, k_odd, k_even)
        return carry

    groups = lax.shift_right_logical(control[which] + GROUP - 1, 3)
    steps = lax.shift_right_logical(groups, 1)
    lax.fori_loop(0, steps, body, 0)

    @pl.when(groups == 2 * steps)
    def _():
        for g in range(0, GROUP, 2):
            sums(2 * steps - 1, g, k_odd)

    @pl.when(groups != 2 * steps)
    def _():
        half(2 * steps, k_even, k_odd)
        for g in range(0, GROUP, 2):
            sums(2 * steps, g, k_even)


def component(acc, a):
    return acc[pl.ds(a, BLOCKS, stride=8), :] + acc[pl.ds(3 + a, BLOCKS, stride=8), :]


parts_scratch = pltpu.VMEM((12, BLOCKS, LANES), f32)
right_shape = (BLOCKS, 8, 16, LANES)
acc_shape = (BLOCKS * 8, LANES)
control_scratch = [pltpu.SMEM((CONTROL,), jnp.int32), pltpu.SemaphoreType.DMA]
near_scratch = control_scratch + [
    pltpu.VMEM((EXT // 4 + 1, LANES, LANES), bf16),
    pltpu.VMEM((4, 16, LANES), bf16),
    pltpu.VMEM((GROUP, 2 * LANES, LANES), bf16),
    pltpu.VMEM((GROUP, 2 * LANES, LANES), bf16),
]


def total_force(expansion, near, places):
    out = []
    for a in range(3):
        far = expansion[0:1, a : a + 1]
        for k in range(3):
            far = far + expansion[0:1, 3 + 3 * a + k : 4 + 3 * a + k] * places[k]
        out.append(near[a] + far)
    return out


def first_kernel(
    control_in, own, burgers, g3, g1, g0, g2, near, burg, control, sem, left, mask, k_even, k_odd, parts, right, acc
):
    copy = pltpu.make_async_copy(control_in, control, sem)
    copy.start()
    ghosts = (g0, g1, g2, g3)
    exists = slot_exists()
    burg[...] = jnp.zeros_like(burg)
    for tile in range(EXT // 8):
        for a in range(3):
            if tile < BLOCKS // 8:
                value = burgers[a, 8 * tile : 8 * tile + 8, :]
            else:
                d = (tile - BLOCKS // 8) // (GHOST // 8)
                value = tile_of(None, ghosts, 3 + a, tile)
                if exists[d] is not None:
                    value = jnp.where(exists[d], value, 0.0)
            high = round_bf16(value)
            burg[pl.ds(tile * 64 + a, 8, stride=8), :] = high
            burg[pl.ds(tile * 64 + 3 + a, 8, stride=8), :] = value - high
    prepare_sources(own, ghosts, range(EXT // 8), left)
    prepare_targets(own, parts, right)
    acc[...] = jnp.zeros_like(acc)
    copy.wait()
    for which in range(2):
        add_pairs(control, which, burg, left, right, mask, acc, k_even, k_odd)
    for a in range(3):
        near[a] = component(acc, a)


def start_kernel(
    control_in, shares, near, places, mobility, expansion, moved, now, s0, s1, s2, s3, control, sem
):
    copy = pltpu.make_async_copy(control_in, control, sem)
    copy.start()
    expansion[...] = jnp.broadcast_to(jnp.sum(shares[...], axis=0, keepdims=True), (8, LANES))
    p = [places[k] for k in range(3)]
    force = total_force(expansion[...], [near[a] for a in range(3)], p)
    for a in range(3):
        step = (time_step * mobility[...]) * force[a]
        moved[a] = step
        now[a] = p[a] + step
    copy.wait()
    send_now(control, now, (s0, s1, s2, s3))


def early_kernel(
    control_in, own, g3, burg, right, acc, control, sem, left, mask, k_even, k_odd, parts
):
    copy = pltpu.make_async_copy(control_in, control, sem)
    copy.start()
    ghosts = (None, None, None, g3)
    prepare_sources(own, ghosts, list(range(BLOCKS // 8)) + tiles_of(EARLY), left)
    prepare_targets(own, parts, right)
    acc[...] = jnp.zeros_like(acc)
    copy.wait()
    add_pairs(control, 0, burg, left, right, mask, acc, k_even, k_odd)


def late_force(
    control_in, expansion, own, g1, g0, g2, burg, right, acc_in, control, sem, left, mask, k_even, k_odd, acc
):
    copy = pltpu.make_async_copy(control_in, control, sem)
    copy.start()
    prepare_sources(own, (g0, g1, g2, None), tiles_of(LATE), left)
    acc[...] = acc_in[...]
    copy.wait()
    add_pairs(control, 1, burg, left, right, mask, acc, k_even, k_odd)
    return total_force(
        expansion[...], [component(acc, a) for a in range(3)], [own[k] for k in range(3)]
    )


def step_kernel(
    final, control, expansion, own, g1, g0, g2, burg, right, acc_in, mobility, places, moved,
    new_moved, now, s0, s1, s2, s3, *scratch
):
    force = late_force(control, expansion, own, g1, g0, g2, burg, right, acc_in, *scratch)
    for a in range(3):
        total = moved[a] + (time_step * mobility[...]) * force[a]
        if final:
            put_rows(new_moved, a, total)
        else:
            new_moved[a] = total
        now[a] = places[a] + total
    send_now(scratch[0], now, (s0, s1, s2, s3))


def last_kernel(
    control, expansion, own, g1, g0, g2, burg, right, acc_in, mobility, velocity, *scratch
):
    force = late_force(control, expansion, own, g1, g0, g2, burg, right, acc_in, *scratch)
    for a in range(3):
        put_rows(velocity, a, mobility[...] * force[a])


def cost(flops):
    return pl.CostEstimate(flops=int(flops), bytes_accessed=2**20, transcendentals=0)


def shape(*dims, dtype=f32):
    return jax.ShapeDtypeStruct(dims, dtype)


def swap(x, slot):
    n_slabs, n_cells = lax.axis_size("slab"), lax.axis_size("cell")
    pairs = []
    for s in range(n_slabs):
        for c in range(n_cells):
            if slot == 0:
                to = (s ^ 1, c)
            elif slot == 3:
                to = (s, c ^ 1)
            elif slot == 1:
                t = s - 1 + 2 * (s % 2)
                to = (t, c) if 0 <= t < n_slabs else (s, c ^ 1)
            else:
                t = c - 1 + 2 * (c % 2)
                to = (s, t) if 0 <= t < n_cells else (s ^ 1, c)
            pairs.append((s * n_cells + c, to[0] * n_cells + to[1]))
    return lax.ppermute(x, ("slab", "cell"), pairs)


def exchange(sends):
    return [swap(sends[slot], slot) for slot in EARLY + LATE]


def local(positions, burgers, mobility, near_list, near_count, send_list):
    mobility = mobility.reshape(BLOCKS, LANES)
    flat = shape(*positions.shape)
    block = shape(3, BLOCKS, LANES)
    send = shape(3, GHOST, LANES)

    positions = positions.reshape(block.shape)
    burgers = burgers.reshape(block.shape)
    numbers = (
        jnp.pad(near_list.T, ((0, 16 - NEAR), (0, LANES - BLOCKS)))
        + jnp.pad(near_count[None], ((NEAR, 15 - NEAR), (0, LANES - BLOCKS)))
        + jnp.pad(send_list, ((8, 4), (0, LANES - GHOST)))
    )

    places, scalars, *sends = pl.pallas_call(
        pack_kernel,
        out_shape=[block, shape(16, LANES, dtype=jnp.int32)] + [shape(6, GHOST, LANES)] * 4,
        in_specs=[vmem] * 3,
        out_specs=[vmem] * 6,
        scratch_shapes=[pltpu.SMEM((16, LANES), jnp.int32), pltpu.SemaphoreType.DMA],
        compiler_params=params,
        name="pack",
    )(numbers, positions, burgers)
    ghosts = [swap(x, slot) for x, slot in zip(sends, EARLY + LATE)]

    shares, control = pl.pallas_call(
        far_kernel,
        out_shape=[shape(EXT, LANES), shape(CONTROL, dtype=jnp.int32)],
        in_specs=[vmem] * 3,
        out_specs=[vmem] * 2,
        scratch_shapes=[
            pltpu.VMEM((32, 2 * EXT), f32),
            pltpu.VMEM((BLOCKS // 4, LANES, LANES), f32),
            pltpu.VMEM((BLOCKS // 4, LANES, LANES), bf16),
            pltpu.VMEM((4, LANES, EXT), bf16),
            pltpu.VMEM((4, 2 * LANES, 2 * EXT), bf16),
            pltpu.VMEM((4, 2 * LANES, 2 * EXT), bf16),
            pltpu.SMEM((16, LANES), jnp.int32),
            pltpu.SMEM((CONTROL,), jnp.int32),
            pltpu.SemaphoreType.DMA((2,)),
        ],
        compiler_params=params,
        cost_estimate=cost(20e9),
        name="far",
    )(scalars, places, burgers)
    shares = lax.all_to_all(shares, ("slab", "cell"), 0, 0, tiled=True)

    near, burg = pl.pallas_call(
        first_kernel,
        out_shape=[block, shape((EXT + 1) * 8, LANES)],
        in_specs=[vmem] * 7,
        out_specs=[vmem] * 2,
        scratch_shapes=near_scratch
        + [parts_scratch, pltpu.VMEM(right_shape, bf16), pltpu.VMEM(acc_shape, f32)],
        compiler_params=params,
        cost_estimate=cost(20e9),
        name="near_first",
    )(control, places, burgers, *ghosts)

    expansion, moved, now, *sends = pl.pallas_call(
        start_kernel,
        out_shape=[shape(8, LANES), block, block] + [send] * 4,
        in_specs=[vmem] * 5,
        out_specs=[vmem] * 7,
        scratch_shapes=control_scratch,
        compiler_params=params,
        name="start",
    )(control, shares, near, places, mobility)

    def evaluate(kernel, out_shape, name, *more):
        ghosts = exchange(sends)
        right, acc = pl.pallas_call(
            early_kernel,
            out_shape=[shape(*right_shape, dtype=bf16), shape(*acc_shape)],
            in_specs=[vmem] * 4,
            out_specs=[vmem] * 2,
            scratch_shapes=near_scratch + [parts_scratch],
            compiler_params=params,
            cost_estimate=cost(20e9),
            name="near_early",
        )(control, now, *ghosts[: len(EARLY)], burg)
        return pl.pallas_call(
            kernel,
            out_shape=out_shape,
            in_specs=[vmem] * (7 + len(LATE) + len(more)),
            out_specs=jax.tree.map(lambda _: vmem, out_shape),
            scratch_shapes=near_scratch + [pltpu.VMEM(acc_shape, f32)],
            compiler_params=params,
            cost_estimate=cost(10e9),
            name=name,
        )(control, expansion, now, *ghosts[len(EARLY) :], burg, right, acc, mobility, *more)

    for substep in range(1, SUBSTEPS):
        final = substep == SUBSTEPS - 1
        moved, now, *sends = evaluate(
            functools.partial(step_kernel, final),
            [flat if final else block, block] + [send] * 4,
            "near_step",
            places,
            moved,
        )
    velocity = evaluate(last_kernel, flat, "near_last")
    return moved, velocity


def solution(mesh):
    return jax.shard_map(
        local,
        mesh=mesh,
        in_specs=(
            P(None, ("slab", "cell")),
            P(None, ("slab", "cell")),
            P(("slab", "cell")),
            P(("slab", "cell"), None),
            P(("slab", "cell")),
            P(None, ("slab", "cell")),
        ),
        out_specs=(P(None, ("slab", "cell")), P(None, ("slab", "cell"))),
        check_vma=False,
    )
```

```python
import functools

import jax
import jax.numpy as jnp
from jax import lax
from jax.experimental import pallas as pl
from jax.experimental.pallas import tpu as pltpu
from jax.sharding import PartitionSpec as P

SUBSTEPS = 4
BLOCKS = 64
LANES = 128
NEAR = 6
GHOST = 48
EXT = 256
GROUP = 8
LEAD = GROUP
TAIL = 56
AT_SENDS = 8
AT_PAIRS = AT_SENDS + 4 * GHOST + LEAD
LIST = BLOCKS * NEAR + TAIL + LEAD
CONTROL = AT_PAIRS + 2 * LIST + 8
EARLY, LATE = (3,), (0, 2, 1)
SHARE = 9

core_sq = 0.04
far_sq = 1.0
time_step = 0.2

f32 = jnp.float32
bf16 = jnp.bfloat16

vmem = pl.BlockSpec(memory_space=pltpu.VMEM)
params = pltpu.CompilerParams(vmem_limit_bytes=40 * 2**20)


def round_bf16(x):
    return x.astype(bf16).astype(f32)


def split2(x):
    high = x.astype(bf16)
    return high, (x - high.astype(f32)).astype(bf16)


def split3(x):
    high = round_bf16(x)
    rest = x - high
    mid = round_bf16(rest)
    return high, mid, round_bf16(rest - mid)


def parity():
    return lax.axis_index("slab") % 2, lax.axis_index("cell") % 2


def send_rows():
    odd_slab, odd_cell = parity()
    return odd_slab, 1 - odd_slab, 3 - odd_cell, 2 + odd_cell


def slot_moves():
    odd_slab, odd_cell = parity()
    return (
        GHOST * (1 - odd_slab),
        GHOST * (odd_slab - 1),
        GHOST * odd_cell,
        -GHOST * odd_cell,
    )


def slot_shifts():
    odd_slab, odd_cell = parity()
    along_slab = (1 - 2 * odd_slab).astype(f32)
    along_cell = (1 - 2 * odd_cell).astype(f32)
    return (0, along_slab), (0, -along_slab), (1, -along_cell), (1, along_cell)


def slot_exists():
    out = []
    for axis in ("slab", "cell"):
        i = lax.axis_index(axis)
        partner = i - 1 + 2 * (i % 2)
        out.append((partner >= 0) & (partner < lax.axis_size(axis)))
    return None, out[0], out[1], None


def fill_sends(block_of, sources, sends):
    def body(n, carry):
        for d in sends:
            block = block_of(d, n)
            for a, (ref, index) in enumerate(sources):
                sends[d][a, pl.ds(n, 1), :] = ref[index, pl.ds(block, 1), :]
        return carry

    lax.fori_loop(0, GHOST, body, 0, unroll=4)


def send_now(control, now, sends):
    fill_sends(
        lambda d, n: control[AT_SENDS + GHOST * d + n],
        [(now, k) for k in range(3)],
        dict(enumerate(sends)),
    )


def centre_of():
    slab = lax.axis_index("slab").astype(f32)
    cell = lax.axis_index("cell").astype(f32)
    return slab, cell


def list_pairs(near_list, near_count):
    segment = (near_list + (GHOST - BLOCKS)) // GHOST
    exists = {0: None, 3: None}
    exists[1], exists[2] = slot_exists()[1:3]
    odd_slab, odd_cell = parity()
    sides = (
        (odd_slab == 1) | exists[1],
        (odd_slab == 0) | exists[1],
        (odd_cell == 1) | exists[2],
        (odd_cell == 0) | exists[2],
    )
    slot = lax.broadcasted_iota(jnp.int32, near_list.shape, 0)
    block = lax.broadcasted_iota(jnp.int32, near_list.shape, 1)
    live = jnp.where(slot < near_count, 1, 0)
    moved = near_list
    for i, (move, there) in enumerate(zip(slot_moves(), sides)):
        mine = segment == 1 + i
        moved = moved + jnp.where(mine, move, 0)
        live = jnp.where(mine, live * there.astype(jnp.int32), live)
    late = jnp.where(moved >= BLOCKS, live, 0)
    for d in EARLY:
        first = BLOCKS + GHOST * d
        late = jnp.where((moved >= first) & (moved < first + GHOST), 0, late)
    earlier = lax.broadcasted_iota(jnp.int32, (BLOCKS, BLOCKS), 0) < lax.broadcasted_iota(
        jnp.int32, (BLOCKS, BLOCKS), 1
    )
    place = jnp.full(near_list.shape, 2 * LIST, jnp.int32)
    amounts = []
    for i, mine in enumerate((live - late, late)):
        rows = [mine[n : n + 1] for n in range(NEAR)]
        before = [jnp.zeros_like(rows[0])]
        for row in rows:
            before.append(before[-1] + row)
        amount = before.pop().astype(f32)
        offset = jnp.dot(
            jnp.broadcast_to(amount, (8, BLOCKS)),
            jnp.where(earlier, 1.0, 0.0),
            preferred_element_type=f32,
        )[:1]
        at = jnp.concatenate([offset.astype(jnp.int32) + x for x in before], axis=0)
        place = jnp.where(mine > 0, at + LIST * i, place)
        amounts.append(jnp.sum(amount, axis=1, keepdims=True).astype(jnp.int32))
    words = 2**15 * place + 2**SHARE * block + moved
    return words, amounts


def pack_kernel(
    numbers, positions, burgers, places, scalars, s3, s0, s2, s1, numbers_smem, sem
):
    copy = pltpu.make_async_copy(numbers, numbers_smem, sem)
    copy.start()
    slab, cell = centre_of()
    for k, by in enumerate((slab + 0.5, cell + 0.5, 0.5)):
        places[k] = positions[k] - by
    scalars[...] = jnp.zeros_like(scalars)
    words, amounts = list_pairs(numbers[:NEAR, :BLOCKS], numbers[NEAR : NEAR + 1, :BLOCKS])
    scalars[:NEAR, :BLOCKS] = words
    for i in range(2):
        scalars[NEAR + i : NEAR + i + 1, :] = jnp.broadcast_to(amounts[i], (1, LANES))
    rows = send_rows()
    for d in range(4):
        first = 2 * (d // 2)
        scalars[8 + d : 9 + d, :] = jnp.where(
            rows[d] == first, numbers[8 + first : 9 + first, :], numbers[9 + first : 10 + first, :]
        )
    sources = [(places, k) for k in range(3)] + [(burgers, a) for a in range(3)]
    copy.wait()
    fill_sends(lambda d, n: numbers_smem[8 + rows[d], n], sources, {0: s0, 1: s1, 2: s2, 3: s3})


def put_rows(out, k, value):
    for b in range(BLOCKS):
        out[k : k + 1, LANES * b : LANES * b + LANES] = value[b : b + 1]


def halves(tile):
    low = lax.broadcasted_iota(jnp.int32, (8, LANES), 0) < 4
    turned = pltpu.roll(tile, 4, 0)
    return jnp.where(low, tile, turned), jnp.where(low, turned, tile)


def pair_rows(values):
    low = lax.broadcasted_iota(jnp.int32, (8, LANES), 0) < 4
    rows = [
        x if x is y else jnp.where(low, x, y) for x, y in zip(values[0::2], values[1::2])
    ]
    rows += [jnp.zeros((8, LANES), f32)] * (LANES // 8 - len(rows))
    return jnp.concatenate(rows, axis=0)


def far_kernel(
    scalars_in, places, burgers, out, control_out, acc, rows, cols, apart_by, w_even, w_odd,
    scalars, control, sems
):
    copy = pltpu.make_async_copy(scalars_in, scalars, sems.at[0])
    copy.start()
    for i in range(LEAD):
        control[AT_PAIRS - LEAD + i] = EXT
        control[AT_PAIRS + LIST - LEAD + i] = EXT
    for tile in range(BLOCKS // 8):
        p = [halves(places[k, 8 * tile : 8 * tile + 8, :]) for k in range(3)]
        burg = [halves(burgers[a, 8 * tile : 8 * tile + 8, :]) for a in range(3)]
        for half in range(2):
            here = [x[half] for x in p]
            sources = [x[half] for x in burg]
            moments = [x * y for x in here for y in sources]
            values = []
            for group in (sources, moments):
                high = [round_bf16(x) for x in group]
                values += high + [x - h for x, h in zip(group, high)]
            rows[2 * tile + half] = pair_rows(values)
            one = jnp.ones((8, LANES), f32)
            square = sum(x * x for x in here) + far_sq
            values = [part for x in (here[0], here[1], square) for part in split3(x)]
            cols[2 * tile + half] = pair_rows(values + [one, one, one]).T.astype(bf16)
    acc[...] = jnp.zeros_like(acc)
    w_odd[...] = jnp.zeros_like(w_odd)
    slab, cell = centre_of()
    target = lax.broadcasted_iota(jnp.int32, (1, EXT), 1)
    apart = [(target // 32).astype(f32) - slab, (target % 32).astype(f32) - cell]
    square = apart[0] * apart[0] + apart[1] * apart[1]
    square_high = round_bf16(square)
    place = lax.broadcasted_iota(jnp.int32, (LANES, EXT), 0)
    values = jnp.where(place < 36, 1.0, 0.0)
    for first, last, x in (
        (0, 12, -2.0 * apart[0]),
        (12, 24, -2.0 * apart[1]),
        (36, 40, square_high),
        (40, 44, square - square_high),
    ):
        values = jnp.where((place >= first) & (place < last), x, values)
    for g in range(4):
        apart_by[g] = jnp.where(place % 4 == g, values, 0.0).astype(bf16)

    def sums(group, g, w):
        mine = rows[group, pl.ds(g, 32, stride=4), :].astype(bf16)
        acc[...] += jnp.dot(
            jnp.concatenate([mine, mine], axis=1), w[g], preferred_element_type=f32
        )

    def half(group, w_now, w_before):
        for i in range(4):
            for slot in range(NEAR):
                word = scalars[slot, 4 * group + i]
                at = lax.shift_right_logical(word, 15)
                control[AT_PAIRS + at] = word & (2**15 - 1)
        for d in range(4):
            for i in range(3):
                n = 3 * group + i
                control[AT_SENDS + GHOST * d + n] = scalars[8 + d, n]
        for g in range(4):
            sums(jnp.maximum(group - 1, 0), g, w_before)
            r = lax.rsqrt(jnp.dot(cols[group], apart_by[g], preferred_element_type=f32))
            r2 = r * r
            w3 = r2 * r
            for k, w in enumerate((w3, w3 * r2)):
                high, low = split2(w)
                w_now[g, :LANES, EXT * k : EXT * k + EXT] = high
                w_now[g, LANES:, EXT * k : EXT * k + EXT] = low

    copy.wait()

    def body(step, carry):
        half(2 * step, w_even, w_odd)
        half(2 * step + 1, w_odd, w_even)
        return carry

    lax.fori_loop(0, BLOCKS // 8, body, 0)
    amounts = [scalars[NEAR, 0], scalars[NEAR + 1, 0]]
    for k in range(2):
        for i in range(TAIL):
            control[AT_PAIRS + LIST * k + amounts[k] + i] = EXT
        control[k] = amounts[k]
    copy = pltpu.make_async_copy(control, control_out, sems.at[1])
    copy.start()
    for g in range(4):
        sums(BLOCKS // 4 - 1, g, w_odd)

    apart = apart + [jnp.zeros((1, EXT), f32)]

    def row(k, i):
        return acc[i : i + 1, EXT * k : EXT * k + EXT]

    direct = [row(0, a) + row(0, 3 + a) for a in range(3)]
    total = [row(1, a) + row(1, 3 + a) for a in range(3)]
    gradient = []
    for a in range(3):
        for k in range(3):
            moment = row(1, 6 + 3 * k + a) + row(1, 15 + 3 * k + a)
            gradient.append(-3.0 * (apart[k] * total[a] - moment))
    zero = jnp.zeros((LANES - 12, 2 * LANES), f32)
    values = jnp.concatenate(direct + gradient + [zero], axis=0)
    out[...] = jnp.concatenate([values[:, :LANES].T, values[:, LANES:].T], axis=0)
    copy.wait()


def tile_of(own, ghosts, index, tile):
    if tile < BLOCKS // 8:
        return own[index, 8 * tile : 8 * tile + 8, :]
    d, n = divmod(tile - BLOCKS // 8, GHOST // 8)
    return ghosts[d][index, 8 * n : 8 * n + 8, :]


def tiles_of(slots):
    n = GHOST // 8
    return [BLOCKS // 8 + n * d + i for d in slots for i in range(n)]


def prepare_sources(own, ghosts, tiles, left):
    shift = slot_shifts()
    one = jnp.ones((8, LANES), f32)
    low = lax.broadcasted_iota(jnp.int32, (8, LANES), 0) < 4

    for tile in tiles:
        p = [tile_of(own, ghosts, k, tile) for k in range(3)]
        if tile >= BLOCKS // 8:
            k, by = shift[(tile - BLOCKS // 8) // (GHOST // 8)]
            p[k] = p[k] + by
        parts_of = [split3(x) for x in p]
        parts_of.append(split3(p[0] * p[0] + p[1] * p[1] + p[2] * p[2]))
        turned = [[pltpu.roll(x, 4, 0) for x in group] for group in parts_of]
        for half in range(2):
            first, second = (parts_of, turned) if half == 0 else (turned, parts_of)
            values = []
            for (h, m, _), (h2, m2, l2) in zip(first[:3], second[:3]):
                values += [
                    jnp.where(low, h, h2),
                    jnp.where(low, m, m2),
                    jnp.where(low, h, l2),
                ]
            h, _, l = first[3]
            values += [jnp.where(low, h, second[3][1]), jnp.where(low, l, one), one]
            values += [jnp.zeros((8, LANES), f32)] * (LANES // 8 - len(values))
            left[2 * tile + half] = jnp.concatenate(values, axis=0).T.astype(bf16)
    left[EXT // 4] = jnp.zeros((LANES, LANES), bf16)


def prepare_targets(own, parts, right):
    one = jnp.ones((8, LANES), f32)
    low = lax.broadcasted_iota(jnp.int32, (8, LANES), 0) < 4

    x = [own[k] for k in range(3)]
    for k in range(3):
        for i, part in enumerate(split3(-2.0 * x[k])):
            parts[3 * k + i] = part
    for i, part in enumerate(split3(x[0] * x[0] + x[1] * x[1] + x[2] * x[2] + core_sq)):
        parts[9 + i] = part
    for b in range(BLOCKS):
        def row(i):
            return jnp.broadcast_to(parts[i, b : b + 1, :], (8, LANES))

        rows = []
        for k in range(3):
            h, m, l = row(3 * k), row(3 * k + 1), row(3 * k + 2)
            high_mid = jnp.where(low, h, m)
            rows += [high_mid, high_mid, jnp.where(low, l, h)]
        rows += [one, jnp.where(low, one, row(9)), jnp.where(low, row(10), row(11))]
        for i in range(6):
            right[b, i] = jnp.concatenate(rows[2 * i : 2 * i + 2], axis=0).astype(bf16)
        right[b, 6:] = jnp.zeros((2, 16, LANES), bf16)


def add_pairs(control, which, burg, left, right, mask, acc, k_even, k_odd):
    place = lax.broadcasted_iota(jnp.int32, (16, LANES), 0) % 4
    for g in range(4):
        mask[g] = jnp.where(place == g, 1.0, 0.0).astype(bf16)

    k_odd[...] = jnp.zeros_like(k_odd)

    def pair(i):
        word = control[AT_PAIRS + LIST * which + i]
        return lax.shift_right_logical(word, SHARE), word & (2**SHARE - 1)

    def sums(step, g, k_before):
        i = step * GROUP + g
        (b0, t0), (b1, t1) = pair(i), pair(i + 1)
        rows = jnp.concatenate(
            [burg[pl.ds(pl.multiple_of(8 * t, 8), 8), :] for t in (t0, t1)], axis=0
        ).astype(bf16)
        both = jnp.dot(
            jnp.concatenate([rows, rows], axis=1),
            jnp.concatenate([k_before[g], k_before[g + 1]], axis=1),
            preferred_element_type=f32,
        )
        at = pl.ds(pl.multiple_of(8 * b0, 8), 8)
        acc[at, :] = acc[at, :] + both[:8, :LANES]
        at = pl.ds(pl.multiple_of(8 * b1, 8), 8)
        acc[at, :] = acc[at, :] + both[8:, LANES:]

    def half(step, k_now, k_before):
        for g in range(GROUP):
            if g % 2 == 0:
                sums(step - 1, g, k_before)
            b, t = pair(step * GROUP + g)
            features = (right[b] * mask[t & 3][None]).reshape(LANES, LANES)
            near_sq = jnp.dot(
                left[lax.shift_right_logical(t, 2)], features, preferred_element_type=f32
            )
            near_sq = jnp.maximum(near_sq, core_sq)
            r = lax.rsqrt(near_sq)
            q = lax.rsqrt(near_sq + (far_sq - core_sq))
            high, low = split2(r * r * r - q * q * q)
            k_now[g, :LANES, :] = high
            k_now[g, LANES:, :] = low

    def body(step, carry):
        half(2 * step, k_even, k_odd)
        half(2 * step + 1, k_odd, k_even)
        return carry

    groups = lax.shift_right_logical(control[which] + GROUP - 1, 3)
    steps = lax.shift_right_logical(groups, 1)
    lax.fori_loop(0, steps, body, 0)

    @pl.when(groups == 2 * steps)
    def _():
        for g in range(0, GROUP, 2):
            sums(2 * steps - 1, g, k_odd)

    @pl.when(groups != 2 * steps)
    def _():
        half(2 * steps, k_even, k_odd)
        for g in range(0, GROUP, 2):
            sums(2 * steps, g, k_even)


def component(acc, a):
    return acc[pl.ds(a, BLOCKS, stride=8), :] + acc[pl.ds(3 + a, BLOCKS, stride=8), :]


parts_scratch = pltpu.VMEM((12, BLOCKS, LANES), f32)
right_shape = (BLOCKS, 8, 16, LANES)
acc_shape = (BLOCKS * 8, LANES)
control_scratch = [pltpu.SMEM((CONTROL,), jnp.int32), pltpu.SemaphoreType.DMA]
near_scratch = control_scratch + [
    pltpu.VMEM((EXT // 4 + 1, LANES, LANES), bf16),
    pltpu.VMEM((4, 16, LANES), bf16),
    pltpu.VMEM((GROUP, 2 * LANES, LANES), bf16),
    pltpu.VMEM((GROUP, 2 * LANES, LANES), bf16),
]


def total_force(expansion, near, places):
    out = []
    for a in range(3):
        far = expansion[0:1, a : a + 1]
        for k in range(3):
            far = far + expansion[0:1, 3 + 3 * a + k : 4 + 3 * a + k] * places[k]
        out.append(near[a] + far)
    return out


def first_kernel(
    control_in, own, burgers, g3, g0, g2, g1, near, burg, control, sem, left, mask, k_even, k_odd, parts, right, acc
):
    copy = pltpu.make_async_copy(control_in, control, sem)
    copy.start()
    ghosts = (g0, g1, g2, g3)
    exists = slot_exists()
    burg[...] = jnp.zeros_like(burg)
    for tile in range(EXT // 8):
        for a in range(3):
            if tile < BLOCKS // 8:
                value = burgers[a, 8 * tile : 8 * tile + 8, :]
            else:
                d = (tile - BLOCKS // 8) // (GHOST // 8)
                value = tile_of(None, ghosts, 3 + a, tile)
                if exists[d] is not None:
                    value = jnp.where(exists[d], value, 0.0)
            high = round_bf16(value)
            burg[pl.ds(tile * 64 + a, 8, stride=8), :] = high
            burg[pl.ds(tile * 64 + 3 + a, 8, stride=8), :] = value - high
    prepare_sources(own, ghosts, range(EXT // 8), left)
    prepare_targets(own, parts, right)
    acc[...] = jnp.zeros_like(acc)
    copy.wait()
    for which in range(2):
        add_pairs(control, which, burg, left, right, mask, acc, k_even, k_odd)
    for a in range(3):
        near[a] = component(acc, a)


def start_kernel(
    control_in, shares, near, places, mobility, expansion, moved, now, s0, s1, s2, s3, control, sem
):
    copy = pltpu.make_async_copy(control_in, control, sem)
    copy.start()
    expansion[...] = jnp.broadcast_to(jnp.sum(shares[...], axis=0, keepdims=True), (8, LANES))
    p = [places[k] for k in range(3)]
    force = total_force(expansion[...], [near[a] for a in range(3)], p)
    for a in range(3):
        step = (time_step * mobility[...]) * force[a]
        moved[a] = step
        now[a] = p[a] + step
    copy.wait()
    send_now(control, now, (s0, s1, s2, s3))


def early_kernel(
    control_in, own, g3, burg, right, acc, control, sem, left, mask, k_even, k_odd, parts
):
    copy = pltpu.make_async_copy(control_in, control, sem)
    copy.start()
    ghosts = (None, None, None, g3)
    prepare_sources(own, ghosts, list(range(BLOCKS // 8)) + tiles_of(EARLY), left)
    prepare_targets(own, parts, right)
    acc[...] = jnp.zeros_like(acc)
    copy.wait()
    add_pairs(control, 0, burg, left, right, mask, acc, k_even, k_odd)


def late_force(
    control_in, expansion, own, g0, g2, g1, burg, right, acc_in, control, sem, left, mask, k_even, k_odd, acc
):
    copy = pltpu.make_async_copy(control_in, control, sem)
    copy.start()
    prepare_sources(own, (g0, g1, g2, None), tiles_of(LATE), left)
    acc[...] = acc_in[...]
    copy.wait()
    add_pairs(control, 1, burg, left, right, mask, acc, k_even, k_odd)
    return total_force(
        expansion[...], [component(acc, a) for a in range(3)], [own[k] for k in range(3)]
    )


def step_kernel(
    final, control, expansion, own, g0, g2, g1, burg, right, acc_in, mobility, places, moved,
    new_moved, now, s0, s1, s2, s3, *scratch
):
    force = late_force(control, expansion, own, g0, g2, g1, burg, right, acc_in, *scratch)
    for a in range(3):
        total = moved[a] + (time_step * mobility[...]) * force[a]
        if final:
            put_rows(new_moved, a, total)
        else:
            new_moved[a] = total
        now[a] = places[a] + total
    send_now(scratch[0], now, (s0, s1, s2, s3))


def last_kernel(
    control, expansion, own, g0, g2, g1, burg, right, acc_in, mobility, velocity, *scratch
):
    force = late_force(control, expansion, own, g0, g2, g1, burg, right, acc_in, *scratch)
    for a in range(3):
        put_rows(velocity, a, mobility[...] * force[a])


def cost(flops):
    return pl.CostEstimate(flops=int(flops), bytes_accessed=2**20, transcendentals=0)


def shape(*dims, dtype=f32):
    return jax.ShapeDtypeStruct(dims, dtype)


def swap(x, slot):
    n_slabs, n_cells = lax.axis_size("slab"), lax.axis_size("cell")
    pairs = []
    for s in range(n_slabs):
        for c in range(n_cells):
            if slot == 0:
                to = (s ^ 1, c)
            elif slot == 3:
                to = (s, c ^ 1)
            elif slot == 1:
                t = s - 1 + 2 * (s % 2)
                to = (t, c) if 0 <= t < n_slabs else (s, c ^ 1)
            else:
                t = c - 1 + 2 * (c % 2)
                to = (s, t) if 0 <= t < n_cells else (s ^ 1, c)
            pairs.append((s * n_cells + c, to[0] * n_cells + to[1]))
    return lax.ppermute(x, ("slab", "cell"), pairs)


def exchange(sends):
    return [swap(sends[slot], slot) for slot in EARLY + LATE]


def local(positions, burgers, mobility, near_list, near_count, send_list):
    mobility = mobility.reshape(BLOCKS, LANES)
    flat = shape(*positions.shape)
    block = shape(3, BLOCKS, LANES)
    send = shape(3, GHOST, LANES)

    positions = positions.reshape(block.shape)
    burgers = burgers.reshape(block.shape)
    numbers = (
        jnp.pad(near_list.T, ((0, 16 - NEAR), (0, LANES - BLOCKS)))
        + jnp.pad(near_count[None], ((NEAR, 15 - NEAR), (0, LANES - BLOCKS)))
        + jnp.pad(send_list, ((8, 4), (0, LANES - GHOST)))
    )

    places, scalars, *sends = pl.pallas_call(
        pack_kernel,
        out_shape=[block, shape(16, LANES, dtype=jnp.int32)] + [shape(6, GHOST, LANES)] * 4,
        in_specs=[vmem] * 3,
        out_specs=[vmem] * 6,
        scratch_shapes=[pltpu.SMEM((16, LANES), jnp.int32), pltpu.SemaphoreType.DMA],
        compiler_params=params,
        name="pack",
    )(numbers, positions, burgers)
    ghosts = [swap(x, slot) for x, slot in zip(sends, (3, 0, 2, 1))]

    shares, control = pl.pallas_call(
        far_kernel,
        out_shape=[shape(EXT, LANES), shape(CONTROL, dtype=jnp.int32)],
        in_specs=[vmem] * 3,
        out_specs=[vmem] * 2,
        scratch_shapes=[
            pltpu.VMEM((32, 2 * EXT), f32),
            pltpu.VMEM((BLOCKS // 4, LANES, LANES), f32),
            pltpu.VMEM((BLOCKS // 4, LANES, LANES), bf16),
            pltpu.VMEM((4, LANES, EXT), bf16),
            pltpu.VMEM((4, 2 * LANES, 2 * EXT), bf16),
            pltpu.VMEM((4, 2 * LANES, 2 * EXT), bf16),
            pltpu.SMEM((16, LANES), jnp.int32),
            pltpu.SMEM((CONTROL,), jnp.int32),
            pltpu.SemaphoreType.DMA((2,)),
        ],
        compiler_params=params,
        cost_estimate=cost(20e9),
        name="far",
    )(scalars, places, burgers)
    shares = lax.all_to_all(shares, ("slab", "cell"), 0, 0, tiled=True)

    near, burg = pl.pallas_call(
        first_kernel,
        out_shape=[block, shape((EXT + 1) * 8, LANES)],
        in_specs=[vmem] * 7,
        out_specs=[vmem] * 2,
        scratch_shapes=near_scratch
        + [parts_scratch, pltpu.VMEM(right_shape, bf16), pltpu.VMEM(acc_shape, f32)],
        compiler_params=params,
        cost_estimate=cost(20e9),
        name="near_first",
    )(control, places, burgers, *ghosts)

    expansion, moved, now, *sends = pl.pallas_call(
        start_kernel,
        out_shape=[shape(8, LANES), block, block] + [send] * 4,
        in_specs=[vmem] * 5,
        out_specs=[vmem] * 7,
        scratch_shapes=control_scratch,
        compiler_params=params,
        name="start",
    )(control, shares, near, places, mobility)

    def evaluate(kernel, out_shape, name, *more):
        ghosts = exchange(sends)
        right, acc = pl.pallas_call(
            early_kernel,
            out_shape=[shape(*right_shape, dtype=bf16), shape(*acc_shape)],
            in_specs=[vmem] * 4,
            out_specs=[vmem] * 2,
            scratch_shapes=near_scratch + [parts_scratch],
            compiler_params=params,
            cost_estimate=cost(20e9),
            name="near_early",
        )(control, now, *ghosts[: len(EARLY)], burg)
        return pl.pallas_call(
            kernel,
            out_shape=out_shape,
            in_specs=[vmem] * (7 + len(LATE) + len(more)),
            out_specs=jax.tree.map(lambda _: vmem, out_shape),
            scratch_shapes=near_scratch + [pltpu.VMEM(acc_shape, f32)],
            compiler_params=params,
            cost_estimate=cost(10e9),
            name=name,
        )(control, expansion, now, *ghosts[len(EARLY) :], burg, right, acc, mobility, *more)

    for substep in range(1, SUBSTEPS):
        final = substep == SUBSTEPS - 1
        moved, now, *sends = evaluate(
            functools.partial(step_kernel, final),
            [flat if final else block, block] + [send] * 4,
            "near_step",
            places,
            moved,
        )
    velocity = evaluate(last_kernel, flat, "near_last")
    return moved, velocity


def solution(mesh):
    return jax.shard_map(
        local,
        mesh=mesh,
        in_specs=(
            P(None, ("slab", "cell")),
            P(None, ("slab", "cell")),
            P(("slab", "cell")),
            P(("slab", "cell"), None),
            P(("slab", "cell")),
            P(None, ("slab", "cell")),
        ),
        out_specs=(P(None, ("slab", "cell")), P(None, ("slab", "cell"))),
        check_vma=False,
    )
```
